128 devices in a mesh: rows: 8 (over y, core), cols: 16 (over z, x).
Axes of the slice: x: 4, y: 4, z: 4, core: 2. Of those that a mesh axis runs over, the one named last changes fastest.
Arguments:
- points: bfloat16 [4, 9, 32, 16384], P(None, None, None, ('rows', 'cols')), may hold values from -6 to 6
- counts: int32 [4, 16384], P(None, ('rows', 'cols')), may hold values from 1 to 32
- tiles: int32 [4, 16384, 1], P(None, ('rows', 'cols')), may hold values from 0 to 127; in each aligned block of 128 rows (0 to 127, 128 to 255, ..., all dimensions but the last counted through in order) at most 3 rows name the same one
- cells: int32 [4, 16384], P(None, ('rows', 'cols')), may hold values from 0 to 2047
- pfn_weight: bfloat16 [9, 64], P(None, 'rows'), may hold values from -2 to 2
- conv_weight: bfloat16 [2, 576, 64], P(None, 'rows'), may hold values from -0.25 to 0.25
- norm_gain: bfloat16 [3, 64], P(None, 'rows'), may hold values from 0.5 to 1.5
- norm_bias: bfloat16 [3, 64], P(None, 'rows'), may hold values from -3 to 3
- cotangent: bfloat16 [4, 256, 16384], P(None, 'rows', 'cols'), may hold values from -6 to 6
Outputs:
- features: bfloat16 [4, 256, 16384], P(None, 'rows', 'cols')
- point_grads: float32 [4, 9, 32, 16384], P(None, None, None, ('rows', 'cols'))
- pfn_weight_grad: float32 [9, 64], P(None, 'rows')
- conv_weight_grad: float32 [2, 576, 64], P(None, 'rows')
- norm_gain_grad: float32 [3, 64], P(None, 'rows')
- norm_bias_grad: float32 [3, 64], P(None, 'rows')
The draws below stay inside these ranges and needn't reach their ends.
Inputs may be any that keep to these rules, and one draw needn't show every extreme that they name: `tiles`: at most 3 of one device's pillars in one scene share a tile.
All inputs are finite; a program needn't handle non-finite values.
Results may differ from the reference program's by a relative error of at most 0.023.
Values may be sent and summed in bfloat16 or wider, within the bound.
A program may use at most 128 MiB of HBM per device.

```python
import math
import jax
import jax.numpy as jnp
import numpy as np
from jax import lax

MB = 4
P_DEV = 128
NPT = 32
FEAT = 9
CH = 64
TH = 64
TW = 32
CAP = 3
PILLARS = 16384
H = 512
W = 512
N_COLS = 16
DEVICES = 128


def draw_counts(key, part):
    key = jax.random.fold_in(key, 11)
    raw_draw = jax.random.randint(key, (MB, PILLARS), 0, NPT ** 3, dtype=jnp.int32)
    cubes = jnp.arange(1, NPT, dtype=jnp.int32) ** 3
    passed = jnp.sum((raw_draw[:, :, None] >= cubes[None, None, :]).astype(jnp.int32), axis=2)
    counts_out = NPT - passed
    position = jnp.arange(PILLARS, dtype=jnp.int32) % P_DEV
    counts_out = jnp.where(position[None, :] == 0, NPT, counts_out)
    counts_out = jnp.where(position[None, :] == 1, 1, counts_out)
    return counts_out.astype(jnp.int32)


def touch_ends(values, rng, least, high):
    index_at = [jax.random.randint(jax.random.fold_in(rng, axis), (), 0, length) for axis, length in enumerate(values.shape)]
    widest = values.shape.index(max(values.shape))
    beside = index_at[:widest] + [(index_at[widest] + 1) % values.shape[widest]] + index_at[widest + 1:]
    return values.at[tuple(index_at)].set(least).at[tuple(beside)].set(high)


def block_levels(key, extent, pieces, least, top_value):
    def one(dim, blocks):
        steps = jax.random.uniform(jax.random.fold_in(jax.random.fold_in(key, 6), dim), (blocks,), jnp.float32, least / len(pieces), top_value / len(pieces))
        return jnp.repeat(jnp.exp(steps), extent[dim] // blocks).reshape((-1,) + (1,) * (len(extent) - dim - 1))

    level = one(*pieces[0])
    for cut in pieces[1:]:
        level = level * one(*cut)
    return level


def deal_out(own_key, own, number, rows, number_of, top, most, lean):
    ranking = jax.random.permutation(own_key, number_of)
    packed, ordinary = portions_of(number_of, rows * top, most, lean, True), portions_of(number_of, rows * top, most, lean, False)
    places = jnp.arange(number_of)

    def named(tallies, turn):
        used = int((tallies > 0).sum())
        fixed = max(1, used // 4)
        moved = fixed + (places - fixed + turn * (used - fixed)) % max(1, number_of - fixed)
        return jnp.zeros((number_of,), jnp.int32).at[ranking[jnp.where(places < fixed, places, moved)]].set(jnp.asarray(tallies, jnp.int32))

    tallies = jnp.where(number % 4 == 0, named(packed, number // 4), named(ordinary, number - number // 4 - 1))
    mixed = jax.random.permutation(jax.random.fold_in(own, 3), number_of)
    donor, sink = mixed[0:number_of // 2 * 2:2], mixed[1:number_of // 2 * 2:2]
    margin = jnp.minimum(tallies[donor] - 1, most - tallies[sink]) // 2
    margin = jnp.where((donor == ranking[0]) | (sink == ranking[0]) | (tallies[sink] == 0), 0, jnp.maximum(margin, 0))
    moved = jax.random.randint(jax.random.fold_in(own, 4), (number_of // 2,), 0, 1 << 20) % (margin + 1)
    tallies = tallies.at[donor].add(-moved).at[sink].add(moved)
    members = jnp.searchsorted(jnp.cumsum(tallies), jnp.arange(rows * top), side="right").astype(jnp.int32)
    grid = members.reshape(top, rows).T
    grid = grid[jax.random.permutation(jax.random.fold_in(own, 1), rows)]
    turn = jax.random.randint(jax.random.fold_in(own, 2), (rows, 1), 0, top)
    return jnp.take_along_axis(grid, (jnp.arange(top)[None, :] + turn) % top, axis=1)


def portions_of(amount, total, bound, skew, full):
    loads = [(1 << 20) // math.isqrt(grade ** skew) + 1 for grade in range(1, amount + 1)]
    largest = bound if full else min(bound, max(-(-total // amount), total * loads[0] // sum(loads)))
    least = 1 if total - largest >= amount - 1 else 0
    given, surplus = [largest] + [least] * (amount - 1), total - largest - least * (amount - 1)
    while surplus > 0:
        movable = [i for i in range(1, amount) if given[i] < largest] or [i for i in range(1, amount) if given[i] < bound]
        whole, left = sum([loads[i] for i in movable]), surplus
        for i in movable:
            addition = min(bound - given[i], max(1, left * loads[i] // whole), surplus)
            given[i] = given[i] + addition
            surplus = surplus - addition
    return np.array(given)


def centred(key, dims, width, bound, shards=(), kind=jnp.bfloat16):
    values = jax.random.normal(key, dims, jnp.float32) * width
    if len(shards) > 0:
        values = block_levels(key, dims, shards, -0.22, 0.18) * values
    return jnp.clip(values, min=-bound, max=bound).astype(kind)


def setup_inputs(seed: int = 0) -> dict:
    key_of = jax.random.split(jax.random.key(seed), 10)
    points = centred(key_of[0], (MB, FEAT, NPT, PILLARS), 1.0, 6.0, ((3, 128),))
    counts = draw_counts(jax.random.fold_in(key_of[9], 71), 0)
    tiles_keys = jax.random.split(jax.random.fold_in(key_of[2], 1), MB * PILLARS // P_DEV)
    tiles_turns = jax.random.permutation(jax.random.fold_in(key_of[2], 3), MB * PILLARS // P_DEV)
    tiles = jax.vmap(lambda own, number: deal_out(jax.random.fold_in(key_of[2], 2), own, number, P_DEV, DEVICES, 1, CAP, 2))(tiles_keys, tiles_turns).reshape((MB, PILLARS, 1))
    cells = touch_ends(jax.random.randint(key_of[3], (MB, PILLARS), 0, TH * TW), jax.random.fold_in(key_of[3], 1), 0, (TH * TW) - 1).astype(jnp.int32)
    pfn_weight = centred(key_of[4], (FEAT, CH), FEAT ** -0.5, 2.0, ((1, 8),))
    conv_weight = centred(key_of[5], (2, 9 * CH, CH), (9 * CH) ** -0.5, 0.25, ((1, 8),))
    norm_gain = jnp.clip(0.5 + 1.0 * jax.random.uniform(key_of[6], (3, CH), jnp.float32) ** block_levels(key_of[6], (3, CH), ((1, 8),), -0.2, 0.2), 0.5, 1.5).astype(jnp.bfloat16)
    norm_bias = centred(key_of[7], (3, CH), 0.5, 3.0, ((1, 8),))
    cotangent = centred(key_of[8], (MB, H // 2, (W // 2) * CH), 1.0, 6.0, ((1, 8), (2, 16)))
    return {"points": points, "counts": counts, "tiles": tiles, "cells": cells, "pfn_weight": pfn_weight, "conv_weight": conv_weight, "norm_gain": norm_gain, "norm_bias": norm_bias, "cotangent": cotangent}


@jax.custom_vjp
def low(v):
    return lax.optimization_barrier(v.astype(jnp.bfloat16)).astype(jnp.float32)

@jax.custom_vjp
def low_back(v):
    return v

def low_keep(v):
    return (low(v), None)

def low_pass(kept, grad):
    return (grad,)

def back_keep(v):
    return (v, None)

def back_low(kept, grad):
    return (low(grad),)
low.defvjp(low_keep, low_pass)
low_back.defvjp(back_keep, back_low)
epsilon = 1e-05
highest = lax.Precision.HIGHEST

def canvas_conv(picture, kernel, stride):
    rows_all, cols_all, channels = picture.shape
    out_rows = rows_all // stride
    out_cols = cols_all // stride
    padded = jnp.pad(picture, ((1, 1), (1, 1), (0, 0)))
    result = jnp.zeros((out_rows, out_cols, kernel.shape[1]), jnp.float32)
    for row_off in range(3):
        for col_off in range(3):
            tap_start = (3 * row_off + col_off) * channels
            window = padded[row_off:row_off + stride * (out_rows - 1) + 1:stride, col_off:col_off + stride * (out_cols - 1) + 1:stride]
            result = result + jnp.einsum('hwc,co->hwo', window, kernel[tap_start:tap_start + channels], precision=highest)
    return result

def canvas_norm(values, gain_row, bias_row):
    center = lax.optimization_barrier(jnp.mean(values, axis=(0, 1)))
    spread = lax.optimization_barrier(jnp.mean(values * values, axis=(0, 1))) - center * center
    return (values - center) * lax.rsqrt(spread + epsilon) * gain_row + bias_row

def forward(point_data, pfn_matrix, conv_stack, gain_rows, bias_rows, count_row, tile_row, cell_row):
    linear = jnp.einsum('cnp,co->npo', point_data, pfn_matrix, precision=highest)
    valid_pts = (jnp.arange(NPT)[:, None] < count_row[None, :]).astype(jnp.float32)[:, :, None]
    total_pts = jnp.sum(valid_pts)
    center = lax.optimization_barrier(jnp.sum(linear * valid_pts, axis=(0, 1))) / total_pts
    spread = lax.optimization_barrier(jnp.sum(linear * linear * valid_pts, axis=(0, 1))) / total_pts - center * center
    pre_pfn = (linear - center) * lax.rsqrt(spread + epsilon) * gain_rows[0] + bias_rows[0]
    active = jax.nn.silu(pre_pfn)
    masked = jnp.where(valid_pts > 0, active, -1e+30)
    peak_value = lax.optimization_barrier(jnp.max(masked, axis=0))
    pillar = peak_value + jnp.log(lax.optimization_barrier(jnp.sum(jnp.exp(masked - peak_value[None]), axis=0)))
    pillar = low(low_back(pillar))
    row_pos = tile_row // N_COLS * TH + cell_row // TW
    col_pos = tile_row % N_COLS * TW + cell_row % TW
    canvas = jnp.zeros((H, W, CH), jnp.float32).at[row_pos, col_pos].add(pillar)
    canvas = low(canvas)
    conv_first = low_back(canvas_conv(canvas, conv_stack[0], 2))
    hidden = low(jax.nn.silu(canvas_norm(conv_first, gain_rows[1], bias_rows[1])))
    conv_second = low_back(canvas_conv(hidden, conv_stack[1], 1))
    return jax.nn.silu(canvas_norm(conv_second, gain_rows[2], bias_rows[2])).reshape(H // 2, W // 2 * CH)

def reference(points, counts, tiles, cells, pfn_weight, conv_weight, norm_gain, norm_bias, cotangent):
    pfn_matrix = pfn_weight.astype(jnp.float32)
    conv_stack = conv_weight.astype(jnp.float32)
    gain_rows = norm_gain.astype(jnp.float32)
    bias_rows = norm_bias.astype(jnp.float32)
    outputs = []
    point_list = []
    pfn_total = jnp.zeros(pfn_matrix.shape, jnp.float32)
    conv_total = jnp.zeros(conv_stack.shape, jnp.float32)
    gain_total = jnp.zeros(gain_rows.shape, jnp.float32)
    bias_total = jnp.zeros(bias_rows.shape, jnp.float32)
    for scene_index in range(MB):

        def scene(point_data, pfn_arg, conv_arg, gain_arg, bias_arg, scene_index=scene_index):
            return forward(point_data, pfn_arg, conv_arg, gain_arg, bias_arg, counts[scene_index], tiles[scene_index, :, 0], cells[scene_index])
        result, pullback = jax.vjp(scene, points[scene_index].astype(jnp.float32), pfn_matrix, conv_stack, gain_rows, bias_rows)
        gradients = pullback(cotangent[scene_index].astype(jnp.float32))
        outputs.append(result)
        point_list.append(gradients[0])
        pfn_total = pfn_total + gradients[1]
        conv_total = conv_total + gradients[2]
        gain_total = gain_total + gradients[3]
        bias_total = bias_total + gradients[4]
    return (jnp.stack(outputs).astype(jnp.bfloat16), jnp.stack(point_list), pfn_total, conv_total, gain_total, bias_total)
```

```python
import functools
import types

import jax
import jax.numpy as jnp
from jax import lax
from jax.experimental import pallas as pl
from jax.experimental.pallas import tpu as pltpu
from jax.sharding import PartitionSpec as P

EPSILON = 1e-05
HIGH = lax.Precision.HIGHEST
MESH = pl.DeviceIdType.MESH
F32, BF16, I32 = jnp.float32, jnp.bfloat16, jnp.int32

SCENES = 4
PAIRS = 2
FEATS = 9
DEPTH = 32
PILLARS = 128
CH = 64
LANES = 128
HALF_ROWS = 32
HALF_COLS = 16
PIXELS = HALF_ROWS * HALF_COLS
SLOTS = 3
EDGE = 8
EXT_COLS = 32
EXT_ROWS = HALF_ROWS + 2
TAPS = 9
OWN_ROWS = 72
PAD_ROWS = 80


def dot_nn(a, b, precision=None):
    return lax.dot_general(
        a, b, (((1,), (0,)), ((), ())), precision=precision, preferred_element_type=F32
    )


def dot_nt(a, b, precision=None):
    return lax.dot_general(
        a, b, (((1,), (1,)), ((), ())), precision=precision, preferred_element_type=F32
    )


def dot_tn(a, b):
    return lax.dot_general(a, b, (((0,), (0,)), ((), ())), preferred_element_type=F32)


def iota(shape, dim):
    return lax.broadcasted_iota(I32, shape, dim)


def sigmoid(v):
    return 1.0 / (1.0 + jnp.exp(-v))


def low(v):
    return v.astype(BF16).astype(F32)


def one_hot(mask):
    return jnp.where(mask, 1.0, 0.0).astype(BF16)


def roll64(v):
    return pltpu.roll(v, CH, axis=1)


SCRATCH = dict(
    w_tmp=((16, LANES), F32),
    w_send=((16, LANES), F32),
    w_land=((8, 16, LANES), F32),
    c_send=((PAD_ROWS, LANES), BF16),
    c_land=((8, PAD_ROWS, LANES), BF16),
    taps=((TAPS * CH, LANES), F32),
    wide1=((TAPS * LANES, LANES), BF16),
    wide2=((TAPS * LANES, LANES), BF16),
    back2=((TAPS * LANES, LANES), BF16),
    back1=((4 * LANES, 4 * LANES), BF16),
    pts32=((SCENES, 16 * DEPTH, LANES), F32),
    aug=((SCENES, 16, DEPTH * LANES), BF16),
    hot=((SCENES * SLOTS, LANES, LANES), BF16),
    b_send=((128, 8, LANES), F32),
    b_land=((128, 8, LANES), F32),
    gram=((SCENES, 16, LANES), F32),
    place=((PAIRS, 4 * PIXELS, 6 * LANES), BF16),
    fetch=((PAIRS, 6 * LANES, 4 * PIXELS), BF16),
    pre=((SCENES, DEPTH, CH, LANES), F32),
    act=((SCENES, DEPTH, CH, LANES), F32),
    slope=((SCENES, DEPTH, CH, LANES), F32),
    pil=((SCENES, CH, LANES), F32),
    t_sum=((SCENES, FEATS, CH, LANES), F32),
    q_sum=((SCENES, 2, CH, LANES), F32),
    x_send=((128, 8, LANES), F32),
    x_land=((128, 8, LANES), F32),
    y_send=((128, 8, LANES), F32),
    y_land=((128, 8, LANES), F32),
    canvas=((PAIRS, 4, 33 * 24, LANES), F32),
    drow_land=((PAIRS, 2, HALF_COLS, LANES), F32),
    drow_send=((PAIRS, 2, HALF_COLS, LANES), F32),
    dcol_send=((PAIRS, 2, HALF_ROWS, LANES), F32),
    dcol_land=((PAIRS, 2, HALF_ROWS, LANES), F32),
    dcor_land=((PAIRS, 8, LANES), F32),
    im1=((PAIRS, PIXELS, TAPS * LANES), BF16),
    im2=((PAIRS, PIXELS, TAPS * LANES), BF16),
    y1=((PAIRS, PIXELS, LANES), F32),
    y2=((PAIRS, PIXELS, LANES), F32),
    x1=((PAIRS, PIXELS, LANES), F32),
    x2=((PAIRS, PIXELS, LANES), F32),
    s1=((PAIRS, PIXELS, LANES), F32),
    g1=((PAIRS, PIXELS, LANES), F32),
    g2=((PAIRS, PIXELS, LANES), F32),
    feat=((PAIRS, PIXELS, LANES), F32),
    cot=((PAIRS, PIXELS, LANES), F32),
    d1=((PAIRS, PIXELS, LANES), BF16),
    d2=((PAIRS, PIXELS, LANES), BF16),
    cols=((4, 2, PAIRS, HALF_ROWS, LANES), F32),
    halo=((4, PAIRS, LANES, LANES), F32),
    ext=((3, PAIRS, EXT_ROWS * EXT_COLS, LANES), F32),
    back=((PAIRS, 4 * PIXELS, LANES), BF16),
    st_send=((4, 4, LANES), F32),
    st_land=((4, 128, 4, LANES), F32),
    k_send=((4, LANES), F32),
    k_land=((128, 4, LANES), F32),
    p_col=((CH, LANES), F32),
    p_send=((8, 8, LANES), F32),
    p_land=((8, 8, LANES), F32),
    p2_send=((8, LANES), F32),
    p2_land=((16, 8, LANES), F32),
    dk=((TAPS * CH, LANES), F32),
    g_send=((8, PAD_ROWS, LANES), BF16),
    g_land=((8, PAD_ROWS, LANES), BF16),
    g2_send=((PAD_ROWS, LANES), BF16),
    g2_land=((16, PAD_ROWS, LANES), BF16),
    upd=((SCENES, 16, DEPTH * LANES), F32),
    small=((8, LANES), F32),
)
SEMS = 64


class Wire:
    def __init__(self, n_rows, n_cols, send_sems, recv_sems):
        self.n_rows, self.n_cols = n_rows, n_cols
        self.total = n_rows * n_cols
        self.row, self.col = lax.axis_index("rows"), lax.axis_index("cols")
        self.me = self.row * n_cols + self.col
        self.send_sems, self.recv_sems = send_sems, recv_sems
        self.used = 0
        self.sent = []

    def any_peer(self, step):
        other = lax.rem(self.me + step + self.total, self.total)
        return (other // self.n_cols, lax.rem(other, self.n_cols))

    def row_peer(self, step):
        return (lax.rem(self.row + step + self.n_rows, self.n_rows), self.col)

    def col_peer(self, step):
        return (self.row, lax.rem(self.col + step + self.n_cols, self.n_cols))

    def near(self, down, right):
        return (
            lax.rem(self.row + down + self.n_rows, self.n_rows),
            lax.rem(self.col + right + self.n_cols, self.n_cols),
        )

    def copy(self, src, dst, sem, peer):
        return pltpu.make_async_remote_copy(
            src_ref=src,
            dst_ref=dst,
            send_sem=self.send_sems.at[sem],
            recv_sem=self.recv_sems.at[sem],
            device_id=peer,
            device_id_type=MESH,
        )

    def one(self, src, dst, peer):
        sem = self.used
        self.used += 1
        copy = self.copy(src, dst, sem, peer)
        copy.start()
        self.sent.append(copy)
        return copy

    def spread(self, count, peer_of, src_of, dst_of, whole):
        sem = self.used
        self.used += 1

        def step(i, carry):
            self.copy(src_of(i), dst_of(i), sem, peer_of(i)).start()
            return carry

        lax.fori_loop(1, count, step, 0)
        copy = self.copy(whole, whole, sem, peer_of(1))
        self.sent.append(copy)
        return copy

    def settle(self):
        for copy in self.sent:
            copy.wait_send()


def step_kernel(n_rows, n_cols, *refs):
    ref = types.SimpleNamespace(**dict(zip(SCRATCH, refs[15:], strict=False)))
    ref.points, ref.counts, ref.tiles, ref.cells, ref.pfn, ref.conv = refs[:6]
    ref.gain, ref.bias, ref.cotangent, ref.features, ref.point_grads = refs[6:11]
    ref.pfn_grad, ref.conv_grad, ref.gain_grad, ref.bias_grad = refs[11:15]
    ref.send_sems, ref.recv_sems = refs[-2:]
    wire = Wire(n_rows, n_cols, ref.send_sems, ref.recv_sems)
    total, row, col, me = wire.total, wire.row, wire.col, wire.me
    lane = iota((1, LANES), 1)
    first_half = lane < CH

    barrier = pltpu.get_barrier_semaphore()

    def greet(i, carry):
        pl.semaphore_signal(barrier, inc=1, device_id=wire.any_peer(i), device_id_type=MESH)
        return carry

    lax.fori_loop(1, total, greet, 0)

    w_tmp = ref.w_tmp
    w_tmp[...] = jnp.zeros((16, LANES), F32)
    w_tmp[0:9, 0:8] = ref.pfn[...].astype(F32)
    w_tmp[9:12, 0:8] = ref.gain[...].astype(F32)
    w_tmp[12:15, 0:8] = ref.bias[...].astype(F32)
    ref.w_send[...] = pltpu.roll(w_tmp[...], row * 8, axis=1)
    ref.w_land[0] = ref.w_send[...]
    own_taps = jnp.concatenate(
        [ref.conv[0].astype(F32), ref.conv[1].astype(F32)], axis=1
    )
    own_taps = jnp.concatenate([own_taps, jnp.zeros((PAD_ROWS - OWN_ROWS, LANES), F32)], axis=0)
    ref.c_send[...] = own_taps.astype(BF16)
    ref.c_land[0] = ref.c_send[...]

    pts32, aug = ref.pts32, ref.aug
    slot_number = iota((DEPTH, LANES), 0)
    for s in range(SCENES):
        valid = slot_number < ref.counts[s : s + 1, :]
        for c in range(FEATS):
            block = ref.points[s, c * DEPTH : (c + 1) * DEPTH, :].astype(F32)
            pts32[s, c * DEPTH : (c + 1) * DEPTH, :] = jnp.where(valid, block, 0.0)
        pts32[s, FEATS * DEPTH : (FEATS + 1) * DEPTH, :] = jnp.where(valid, 1.0, 0.0)
        pts32[s, (FEATS + 1) * DEPTH :, :] = jnp.zeros((6 * DEPTH, LANES), F32)
        scene_pts = pts32.at[s]
        for n in range(DEPTH):
            aug[s, :, n * LANES : (n + 1) * LANES] = scene_pts[pl.ds(n, 16, stride=DEPTH), :].astype(
                BF16
            )
    stacked = jnp.concatenate([aug[s] for s in range(SCENES)], axis=0)
    gram_all = dot_nt(stacked, jnp.concatenate([stacked, stacked], axis=0))
    moments = jnp.zeros((4, LANES), F32)
    for s in range(SCENES):
        for b in range(3):
            piece = gram_all[16 * s + 4 * b : 16 * s + 4 * b + 4, :]
            at = 40 * b + 10 * s
            piece = pltpu.roll(piece, (at - 16 * s) % LANES, axis=1)
            moments = moments + jnp.where((lane >= at) & (lane < at + 10), piece, 0.0)

    hot = ref.hot
    above = iota((LANES, LANES), 0) < iota((LANES, LANES), 1)
    slot_row = iota((LANES, LANES), 0).astype(F32) * 4.0
    for s in range(SCENES):
        tile = lax.rem(ref.tiles[s : s + 1, :] - me + total, total).astype(F32)
        wide = jnp.broadcast_to(tile, (LANES, LANES))
        same = (jnp.transpose(wide) == wide) & above
        rank = jnp.sum(jnp.where(same, 1.0, 0.0), axis=0, keepdims=True)
        code = tile * 4.0 + rank
        for k in range(SLOTS):
            hot[s * SLOTS + k] = one_hot(slot_row + float(k) == code)

    b_send = ref.b_send.reshape(128 * 8, LANES)
    lane_row = iota((LANES, LANES), 0)
    for q in range(4):
        extra = jnp.zeros((LANES, LANES), F32)
        for pair in range(PAIRS):
            s = 2 * pair + q // 2
            cell = ref.cells[s : s + 1, :]
            place = (jnp.bitwise_and(cell, 31) if q % 2 else jnp.right_shift(cell, 5)) + 1
            for k in range(SLOTS):
                spot = jnp.where(lane_row == 120 + 3 * pair + k, place.astype(F32), 0.0)
                extra = extra + dot_nt(hot[s * SLOTS + k], spot.astype(BF16))
        b_send[pl.ds(q, 128, stride=8), :] = extra + moments[q : q + 1, :]
    ref.b_land[0, 0:4, :] = ref.b_send[0, 0:4, :]

    pl.semaphore_wait(barrier, total - 1)

    w_wait = wire.spread(
        n_rows,
        wire.row_peer,
        lambda i: ref.w_send,
        lambda i: ref.w_land.at[i],
        ref.w_land.at[pl.ds(1, n_rows - 1)],
    )
    b_wait = wire.spread(
        total,
        wire.any_peer,
        lambda i: ref.b_send.at[i, pl.ds(0, 4)],
        lambda i: ref.b_land.at[i, pl.ds(0, 4)],
        ref.b_land.at[pl.ds(1, total - 1), pl.ds(0, 4)],
    )
    c_wait = wire.spread(
        n_rows,
        wire.row_peer,
        lambda i: ref.c_send,
        lambda i: ref.c_land.at[i],
        ref.c_land.at[pl.ds(1, n_rows - 1)],
    )

    def halo_send(values, index, full):
        cols, halo = ref.cols.at[index], ref.halo.at[index]
        for pair in range(PAIRS):
            for side in range(2):
                start = side * (HALF_COLS - 1)
                cols[side, pair] = values.at[pair][pl.ds(start, HALF_ROWS, stride=HALF_COLS), :]
        waits = [
            wire.one(values.at[:, pl.ds(0, 16)], halo.at[:, pl.ds(16, 16)], wire.near(-1, 0)),
            wire.one(cols.at[0], halo.at[:, pl.ds(64, 32)], wire.near(0, -1)),
            wire.one(values.at[:, pl.ds(0, 8)], halo.at[:, pl.ds(120, 8)], wire.near(-1, -1)),
        ]
        if full:
            waits += [
                wire.one(values.at[:, pl.ds(496, 16)], halo.at[:, pl.ds(0, 16)], wire.near(1, 0)),
                wire.one(cols.at[1], halo.at[:, pl.ds(32, 32)], wire.near(0, 1)),
                wire.one(values.at[:, pl.ds(8, 8)], halo.at[:, pl.ds(112, 8)], wire.near(-1, 1)),
                wire.one(values.at[:, pl.ds(496, 8)], halo.at[:, pl.ds(104, 8)], wire.near(1, -1)),
                wire.one(values.at[:, pl.ds(504, 8)], halo.at[:, pl.ds(96, 8)], wire.near(1, 1)),
            ]
        return waits

    def there(cond):
        return jnp.where(cond, 1.0, 0.0)

    up, down = there(row > 0), there(row < n_rows - 1)
    left, right = there(col > 0), there(col < n_cols - 1)
    spot = iota((LANES, LANES), 0)
    halo_mask = jnp.where(spot < 16, up, jnp.where(spot < 32, down, jnp.where(spot < 64, left, right)))
    halo_mask = jnp.where(spot < 96, halo_mask, jnp.where(spot < 112, up, down))
    halo_mask = jnp.where(
        spot < 96,
        halo_mask,
        halo_mask * jnp.where((spot < 104) | ((spot >= 112) & (spot < 120)), left, right),
    )

    def fill_ext(index, pair, inner, edge):
        grid = ref.ext.at[index, pair]
        for i in range(HALF_ROWS):
            at = (i + 1) * EXT_COLS + EDGE
            grid[at : at + HALF_COLS, :] = inner[i * HALF_COLS : (i + 1) * HALF_COLS, :]
        grid[EDGE : EDGE + HALF_COLS, :] = edge[0:16, :]
        last = (EXT_ROWS - 1) * EXT_COLS
        grid[last + EDGE : last + EDGE + HALF_COLS, :] = edge[16:32, :]
        grid[pl.ds(EXT_COLS + EDGE - 1, HALF_ROWS, stride=EXT_COLS), :] = edge[32:64, :]
        grid[pl.ds(EXT_COLS + EDGE + HALF_COLS, HALF_ROWS, stride=EXT_COLS), :] = edge[64:96, :]
        grid[EDGE - 1 : EDGE, :] = edge[103:104, :]
        grid[EDGE + HALF_COLS : EDGE + HALF_COLS + 1, :] = edge[104:105, :]
        grid[last + EDGE - 1 : last + EDGE, :] = edge[119:120, :]
        grid[last + EDGE + HALF_COLS : last + EDGE + HALF_COLS + 1, :] = edge[120:121, :]

    def shifted(index, pair, shift, rows):
        grid = ref.ext.at[index, pair]
        start = EDGE - 1 + shift
        return [
            grid[i * EXT_COLS + start : i * EXT_COLS + start + HALF_COLS, :].astype(BF16)
            for i in rows
        ]

    def global_sums(index, rows_of):
        send, land = ref.st_send.at[index], ref.st_land.at[index]
        for i, value in enumerate(rows_of):
            send[i : i + 1, :] = value
        land[0] = send[...]
        return wire.spread(
            total,
            wire.any_peer,
            lambda i: send,
            lambda i: land.at[i],
            land.at[pl.ds(1, total - 1)],
        )

    def summed(index):
        return jnp.sum(ref.st_land[index], axis=0)

    def column_sum(v):
        return jnp.sum(v, axis=0, keepdims=True)

    cot = ref.cot
    for pair in range(PAIRS):
        spread_to = cot.at[pair]
        for m in range(HALF_COLS // 2):
            a = ref.cotangent[2 * pair, :, m * LANES : (m + 1) * LANES].astype(F32)
            b = ref.cotangent[2 * pair + 1, :, m * LANES : (m + 1) * LANES].astype(F32)
            spread_to[pl.ds(2 * m, HALF_ROWS, stride=HALF_COLS), :] = jnp.where(
                first_half, a, roll64(b)
            )
            spread_to[pl.ds(2 * m + 1, HALF_ROWS, stride=HALF_COLS), :] = jnp.where(
                first_half, roll64(a), b
            )
    cot_waits = halo_send(cot, 0, True)

    w_wait.wait_recv()
    b_wait.wait_recv()
    w_full = jnp.sum(ref.w_land[...], axis=0)
    feature_row = iota((16, LANES), 0)
    w_row = jnp.where(feature_row < FEATS, w_full, 0.0)
    gain0, bias0 = w_full[9:10, :], w_full[12:13, :]
    gain1, bias1 = w_full[10:11, :] + roll64(w_full[10:11, :]), w_full[13:14, :] + roll64(w_full[13:14, :])
    gain2, bias2 = w_full[11:12, :] + roll64(w_full[11:12, :]), w_full[14:15, :] + roll64(w_full[14:15, :])
    moments = jnp.sum(ref.b_land[:, 0:4, :], axis=0)
    gram = ref.gram
    norm0 = []
    for s in range(SCENES):
        gram[s] = jnp.zeros((16, LANES), F32)
        for b in range(3):
            piece = pltpu.roll(moments, (LANES - 40 * b - 10 * s) % LANES, axis=1)
            gram[s, 4 * b : 4 * b + 4, :] = jnp.where(lane < 10, piece, 0.0)
        products = gram[s]
        cross = dot_nn(products[:, 0:16], w_row, HIGH)
        count = products[9:10, 9:10]
        center = cross[9:10, :] / count
        spread = column_sum(w_row * cross) / count - center * center
        factor = lax.rsqrt(spread + EPSILON)
        norm0.append((center, factor, factor * gain0, count, cross, products))

    for s in range(SCENES):
        center, factor, scale, count, _, _ = norm0[s]
        folded = w_row * scale + jnp.where(feature_row == FEATS, bias0 - center * scale, 0.0)
        coarse = low(folded)
        both = jnp.concatenate(
            [coarse, low(folded - coarse), jnp.zeros((LANES - 32, LANES), F32)], axis=0
        )
        matrix = jnp.transpose(both)[0:CH, 0:32].astype(BF16)
        bound = ref.counts[s : s + 1, :]

        def forward(j, peak, s=s, matrix=matrix, bound=bound):
            points = aug[s, :, pl.ds(pl.multiple_of(j * 4 * LANES, 4 * LANES), 4 * LANES)]
            value = dot_nn(matrix, jnp.concatenate([points, points], axis=0))
            for t in range(4):
                pre = value[:, t * LANES : (t + 1) * LANES]
                sigma = sigmoid(pre)
                active = jnp.where(4 * j + t < bound, pre * sigma, -1e30)
                ref.pre[s, 4 * j + t] = pre
                ref.slope[s, 4 * j + t] = sigma
                ref.act[s, 4 * j + t] = active
                peak = jnp.maximum(peak, active)
            return peak

        peak = lax.fori_loop(0, DEPTH // 4, forward, jnp.full((CH, LANES), -1e30, F32))

        def gather_exp(j, whole, s=s, peak=peak):
            for t in range(4):
                whole = whole + jnp.exp(ref.act[s, 4 * j + t] - peak)
            return whole

        whole = lax.fori_loop(0, DEPTH // 4, gather_exp, jnp.zeros((CH, LANES), F32))
        ref.pil[s] = peak + jnp.log(whole)

    x_send = ref.x_send.reshape(128 * 8, LANES)
    for pair in range(PAIRS):
        a, b = ref.pil[2 * pair].astype(BF16), ref.pil[2 * pair + 1].astype(BF16)
        none = jnp.zeros((CH, LANES), BF16)
        both = jnp.concatenate(
            [jnp.concatenate([a, none], axis=1), jnp.concatenate([none, b], axis=1)], axis=0
        )
        for k in range(SLOTS):
            pick = jnp.concatenate(
                [hot[2 * pair * SLOTS + k], hot[(2 * pair + 1) * SLOTS + k]], axis=1
            )
            x_send[pl.ds(3 * pair + k, 128, stride=8), :] = dot_nt(pick, both)
    ref.x_land[0, 0:6, :] = ref.x_send[0, 0:6, :]
    x_wait = wire.spread(
        total,
        wire.any_peer,
        lambda i: ref.x_send.at[i, pl.ds(0, 6)],
        lambda i: ref.x_land.at[i, pl.ds(0, 6)],
        ref.x_land.at[pl.ds(1, total - 1), pl.ds(0, 6)],
    )

    b_land = ref.b_land.reshape(128 * 8, LANES)
    pieces = [b_land[pl.ds(q, 128, stride=8), :] for q in range(4)]
    turned = [jnp.transpose(piece) for piece in pieces]
    place, fetch = ref.place, ref.fetch

    def pixel_of(tall, wide):
        i, j = tall.astype(I32) - 1, wide.astype(I32) - 1
        odd = jnp.bitwise_and(i, 1) * 1024 + jnp.bitwise_and(j, 1) * 512
        return jnp.where(
            i < 0, -1, odd + jnp.right_shift(i, 1) * HALF_COLS + jnp.right_shift(j, 1)
        )

    for pair in range(PAIRS):
        for half in range(2):
            for k in range(SLOTS):
                at = 120 + 3 * pair + k
                block = (half * SLOTS + k) * LANES
                across = pixel_of(
                    turned[2 * half][at : at + 1, :], turned[2 * half + 1][at : at + 1, :]
                )
                along = pixel_of(
                    pieces[2 * half][:, at : at + 1], pieces[2 * half + 1][:, at : at + 1]
                )
                along = jnp.broadcast_to(along, (LANES, LANES))
                for m in range(4 * PIXELS // LANES):
                    place[pair, m * LANES : (m + 1) * LANES, block : block + LANES] = one_hot(
                        iota((LANES, LANES), 0) + m * LANES == across
                    )
                    fetch[pair, block : block + LANES, m * LANES : (m + 1) * LANES] = one_hot(
                        iota((LANES, LANES), 1) + m * LANES == along
                    )

    c_wait.wait_recv()
    taps = ref.taps
    for i in range(n_rows):
        owner = lax.rem(row - i + n_rows, n_rows)
        taps[pl.ds(pl.multiple_of(owner * OWN_ROWS, 8), OWN_ROWS), :] = ref.c_land[i].astype(F32)[
            0:OWN_ROWS, :
        ]
    ref.back1[...] = jnp.zeros((4 * LANES, 4 * LANES), BF16)
    for t in range(TAPS):
        both = taps[t * CH : (t + 1) * CH, :]
        swapped = roll64(both)
        at = t * LANES
        k1 = jnp.concatenate(
            [jnp.where(first_half, both, 0.0), jnp.where(first_half, 0.0, swapped)], axis=0
        )
        k2 = jnp.concatenate(
            [jnp.where(first_half, swapped, 0.0), jnp.where(first_half, 0.0, both)], axis=0
        )
        ref.wide1[at : at + LANES, :] = k1.astype(BF16)
        ref.wide2[at : at + LANES, :] = k2.astype(BF16)
        ref.back2[at : at + LANES, :] = jnp.transpose(k2).astype(BF16)
        a, b = t // 3, t % 3
        window = 2 * (a == 0) + (b == 0)
        parity = 2 * (a != 1) + (b != 1)
        ref.back1[
            window * LANES : (window + 1) * LANES, parity * LANES : (parity + 1) * LANES
        ] = jnp.transpose(k1).astype(BF16)

    def slopes(step, carry):
        s, block = step // 4, lax.rem(step, 4)
        rows = pl.ds(pl.multiple_of(block * 16, 16), 16)
        top = ref.pil[s, rows, :]

        def inner(j, sums):
            sums = list(sums)
            for t in range(2):
                n = 2 * j + t
                active, sigma = ref.act[s, n, rows, :], ref.slope[s, n, rows, :]
                share = jnp.exp(active - top) * (sigma + active * (1.0 - sigma))
                ref.slope[s, n, rows, :] = share
                sums[0] = sums[0] + share
                sums[1] = sums[1] + share * ref.pre[s, n, rows, :]
                for c in range(FEATS):
                    sums[2 + c] = sums[2 + c] + share * pts32[s, pl.ds(c * DEPTH + n, 1), :]
            return tuple(sums)

        zero = jnp.zeros((16, LANES), F32)
        sums = lax.fori_loop(0, DEPTH // 2, inner, (zero,) * (2 + FEATS))
        ref.q_sum[s, 0, rows, :] = sums[0]
        ref.q_sum[s, 1, rows, :] = sums[1]
        for c in range(FEATS):
            ref.t_sum[s, c, rows, :] = sums[2 + c]
        return carry

    lax.fori_loop(0, 4 * SCENES, slopes, 0)

    x_wait.wait_recv()
    x_land = ref.x_land.reshape(128 * 8, LANES)
    canvas = ref.canvas
    for pair in range(PAIRS):
        landed = [x_land[pl.ds(3 * pair + k, 128, stride=8), :] for k in range(SLOTS)]
        values = [jnp.where(first_half, v, 0.0) for v in landed]
        values += [jnp.where(first_half, 0.0, v) for v in landed]
        values = jnp.concatenate(values, axis=0).astype(BF16)
        for plane in range(4):
            grid = low(dot_nn(place[pair, plane * PIXELS : (plane + 1) * PIXELS, :], values))
            for i in range(HALF_ROWS):
                at = (i + 1) * 24 + EDGE
                canvas[pair, plane, at : at + HALF_COLS, :] = grid[
                    i * HALF_COLS : (i + 1) * HALF_COLS, :
                ]
        for p in range(2):
            at = 32 * 24 + EDGE
            ref.drow_send[pair, p] = canvas[pair, 2 + p, at : at + HALF_COLS, :]
            ref.dcol_send[pair, p] = canvas.at[pair, 1 + 2 * p][
                pl.ds(24 + EDGE + HALF_COLS - 1, HALF_ROWS, stride=24), :
            ]
    d_waits = [
        wire.one(ref.drow_send, ref.drow_land, wire.near(1, 0)),
        wire.one(ref.dcol_send, ref.dcol_land, wire.near(0, 1)),
        wire.one(ref.dcol_send.at[:, 1, pl.ds(24, 8)], ref.dcor_land, wire.near(1, 1)),
    ]
    for wait in d_waits:
        wait.wait_recv()
    for pair in range(PAIRS):
        for p in range(2):
            canvas[pair, 2 + p, EDGE : EDGE + HALF_COLS, :] = ref.drow_land[pair, p] * up
            canvas.at[pair, 1 + 2 * p][pl.ds(24 + EDGE - 1, HALF_ROWS, stride=24), :] = (
                ref.dcol_land[pair, p] * left
            )
        canvas[pair, 3, EDGE - 1 : EDGE, :] = ref.dcor_land[pair, 7:8, :] * (up * left)

    sums = []
    y1 = ref.y1
    for pair in range(PAIRS):
        for t in range(TAPS):
            a, b = t // 3, t % 3
            plane = 2 * (a != 1) + (b != 1)
            first, start = (0 if a == 0 else 1), (EDGE - 1 if b == 0 else EDGE)
            for i in range(HALF_ROWS):
                at = (i + first) * 24 + start
                ref.im1[
                    pair, i * HALF_COLS : (i + 1) * HALF_COLS, t * LANES : (t + 1) * LANES
                ] = canvas[pair, plane, at : at + HALF_COLS, :].astype(BF16)
        value = dot_nn(ref.im1[pair], ref.wide1[...])
        y1[pair] = value
        sums += [column_sum(value), column_sum(value * value)]
    e_wait = global_sums(0, sums)
    e_waits = halo_send(y1, 1, True)

    pixel_total = float(PIXELS * total)

    def norm_of(index, pair):
        sums = summed(index)
        center = sums[2 * pair : 2 * pair + 1, :] / pixel_total
        spread = sums[2 * pair + 1 : 2 * pair + 2, :] / pixel_total - center * center
        return center, lax.rsqrt(spread + EPSILON)

    for wait in cot_waits:
        wait.wait_recv()

    e_wait.wait_recv()
    for wait in e_waits:
        wait.wait_recv()

    norm1, sums = [], []
    y2 = ref.y2
    for pair in range(PAIRS):
        center, factor = norm_of(0, pair)
        norm1.append((center, factor))
        scaled = (y1[pair] - center) * factor
        pre = scaled * gain1 + bias1
        sigma = sigmoid(pre)
        active = low(pre * sigma)
        edge = (ref.halo[1, pair] - center) * factor * gain1 + bias1
        edge = low(edge * sigmoid(edge)) * halo_mask
        fill_ext(0, pair, active, edge)
        for b in range(3):
            window = shifted(0, pair, b, range(EXT_ROWS))
            for a in range(3):
                t = 3 * a + b
                ref.im2[pair, :, t * LANES : (t + 1) * LANES] = jnp.concatenate(
                    window[a : a + HALF_ROWS], axis=0
                )
        value = dot_nn(ref.im2[pair], ref.wide2[...])
        y2[pair] = value
        sums += [column_sum(value), column_sum(value * value)]
        ref.x1[pair] = scaled
        ref.s1[pair] = sigma * (1.0 + pre * (1.0 - sigma))
    f_wait = global_sums(1, sums)
    f_waits = halo_send(y2, 2, True)
    f_wait.wait_recv()
    for wait in f_waits:
        wait.wait_recv()

    norm2, sums = [], []
    for pair in range(PAIRS):
        center, factor = norm_of(1, pair)
        norm2.append((center, factor))
        scaled = (y2[pair] - center) * factor
        pre = scaled * gain2 + bias2
        sigma = sigmoid(pre)
        grad = cot[pair] * (sigma * (1.0 + pre * (1.0 - sigma)))
        sums += [column_sum(grad), column_sum(grad * scaled)]
        ref.x2[pair] = scaled
        ref.g2[pair] = grad
        ref.feat[pair] = pre * sigma
    g_wait = global_sums(2, sums)
    for pair in range(PAIRS):
        grid = ref.feat.at[pair]
        for m in range(HALF_COLS // 2):
            a = grid[pl.ds(2 * m, HALF_ROWS, stride=HALF_COLS), :]
            b = grid[pl.ds(2 * m + 1, HALF_ROWS, stride=HALF_COLS), :]
            at = m * LANES
            ref.features[2 * pair, :, at : at + LANES] = jnp.where(
                first_half, a, roll64(b)
            ).astype(BF16)
            ref.features[2 * pair + 1, :, at : at + LANES] = jnp.where(
                first_half, roll64(a), b
            ).astype(BF16)
    edges2 = []
    for pair in range(PAIRS):
        center, factor = norm2[pair]
        scaled = (ref.halo[2, pair] - center) * factor
        pre = scaled * gain2 + bias2
        sigma = sigmoid(pre)
        edges2.append((scaled, ref.halo[0, pair] * (sigma * (1.0 + pre * (1.0 - sigma)))))
    g_wait.wait_recv()

    total2 = summed(2)
    sums = []
    for pair in range(PAIRS):
        scale = norm2[pair][1] * gain2
        mean_grad = total2[2 * pair : 2 * pair + 1, :] / pixel_total
        mean_scaled = total2[2 * pair + 1 : 2 * pair + 2, :] / pixel_total
        inner = low(scale * (ref.g2[pair] - mean_grad - ref.x2[pair] * mean_scaled))
        edge_scaled, edge_grad = edges2[pair]
        edge = low(scale * (edge_grad - mean_grad - edge_scaled * mean_scaled)) * halo_mask
        ref.d2[pair] = inner.astype(BF16)
        fill_ext(1, pair, inner, edge)
        blocks = [None] * TAPS
        for b in range(3):
            window = shifted(1, pair, 2 - b, range(EXT_ROWS))
            for a in range(3):
                blocks[3 * a + b] = jnp.concatenate(window[2 - a : 2 - a + HALF_ROWS], axis=0)
        grad = dot_nn(jnp.concatenate(blocks, axis=1), ref.back2[...]) * ref.s1[pair]
        ref.g1[pair] = grad
        sums += [column_sum(grad), column_sum(grad * ref.x1[pair])]
    h_wait = global_sums(3, sums)
    h_waits = halo_send(ref.g1, 3, False)

    def kernel_grad(windows, grads, t):
        at = t * LANES
        product = dot_tn(windows[0, :, at : at + LANES], grads[0])
        product = product + dot_tn(windows[1, :, at : at + LANES], grads[1])
        return product[0:CH, :] + roll64(product[CH:LANES, :])

    dk = ref.dk
    for t in range(TAPS):
        dk[t * CH : (t + 1) * CH, :] = roll64(kernel_grad(ref.im2, ref.d2, t))

    h_wait.wait_recv()
    for wait in h_waits:
        wait.wait_recv()

    total1 = summed(3)
    y_send = ref.y_send.reshape(128 * 8, LANES)
    for pair in range(PAIRS):
        center, factor = norm1[pair]
        scale = factor * gain1
        mean_grad = total1[2 * pair : 2 * pair + 1, :] / pixel_total
        mean_scaled = total1[2 * pair + 1 : 2 * pair + 2, :] / pixel_total
        inner = low(scale * (ref.g1[pair] - mean_grad - ref.x1[pair] * mean_scaled))
        edge_scaled = (ref.halo[1, pair] - center) * factor
        edge = low(scale * (ref.halo[3, pair] - mean_grad - edge_scaled * mean_scaled))
        edge = jnp.where(halo_mask > 0.0, edge, 0.0)
        ref.d1[pair] = inner.astype(BF16)
        fill_ext(2, pair, inner, edge)
        here = shifted(2, pair, 1, range(1, EXT_ROWS))
        beside = shifted(2, pair, 2, range(1, EXT_ROWS))
        windows = [here[:HALF_ROWS], beside[:HALF_ROWS], here[1:], beside[1:]]
        windows = jnp.concatenate([jnp.concatenate(w, axis=0) for w in windows], axis=1)
        value = dot_nn(windows, ref.back1[...])
        for plane in range(4):
            ref.back[pair, plane * PIXELS : (plane + 1) * PIXELS, :] = value[
                :, plane * LANES : (plane + 1) * LANES
            ].astype(BF16)
        value = dot_nn(fetch[pair], ref.back[pair])
        for k in range(SLOTS):
            y_send[pl.ds(3 * pair + k, 128, stride=8), :] = jnp.where(
                first_half,
                value[k * LANES : (k + 1) * LANES, :],
                value[(SLOTS + k) * LANES : (SLOTS + k + 1) * LANES, :],
            )
    ref.y_land[0, 0:6, :] = ref.y_send[0, 0:6, :]
    y_wait = wire.spread(
        total,
        lambda i: wire.any_peer(-i),
        lambda i: ref.y_send.at[i, pl.ds(0, 6)],
        lambda i: ref.y_land.at[i, pl.ds(0, 6)],
        ref.y_land.at[pl.ds(1, total - 1), pl.ds(0, 6)],
    )

    for t in range(TAPS):
        at = t * CH
        own = kernel_grad(ref.im1, ref.d1, t)
        dk[at : at + CH, :] = jnp.where(first_half, own, dk[at : at + CH, :])
    padding = jnp.zeros((PAD_ROWS - OWN_ROWS, LANES), F32)
    for i in range(n_rows):
        owner = lax.rem(row + i, n_rows)
        block = dk[pl.ds(pl.multiple_of(owner * OWN_ROWS, 8), OWN_ROWS), :]
        block = jnp.concatenate([block, padding], axis=0).astype(BF16)
        ref.g_send[i] = block
        if i == 0:
            ref.g_land[0] = block
    g1_wait = wire.spread(
        n_rows,
        wire.row_peer,
        lambda i: ref.g_send.at[i],
        lambda i: ref.g_land.at[i],
        ref.g_land.at[pl.ds(1, n_rows - 1)],
    )
    g1_wait.wait_recv()
    block = jnp.sum(ref.g_land[...].astype(F32), axis=0).astype(BF16)
    ref.g2_send[...] = block
    ref.g2_land[0] = block
    g2_wait = wire.spread(
        n_cols,
        wire.col_peer,
        lambda i: ref.g2_send,
        lambda i: ref.g2_land.at[i],
        ref.g2_land.at[pl.ds(1, n_cols - 1)],
    )
    scales = jnp.concatenate(
        [norm0[s][2] for s in range(SCENES)] + [jnp.zeros((LANES - SCENES, LANES), F32)], axis=0
    )
    scales = jnp.transpose(scales)[0:CH, :]

    y_wait.wait_recv()
    y_land = ref.y_land.reshape(128 * 8, LANES)
    grads = []
    for pair in range(PAIRS):
        landed = [
            jnp.transpose(y_land[pl.ds(3 * pair + k, 128, stride=8), :]) for k in range(SLOTS)
        ]
        landed = jnp.concatenate(landed, axis=1).astype(BF16)
        for half in range(2):
            s = 2 * pair + half
            pick = jnp.concatenate([hot[s * SLOTS + k] for k in range(SLOTS)], axis=0)
            grads.append(dot_nn(landed[half * CH : (half + 1) * CH, :], pick))

    sums = jnp.zeros((8, CH), F32)
    sub_row = iota((8, LANES), 0)
    for s in range(SCENES):
        for kind in range(2):
            chosen = jnp.where(sub_row == kind * 4 + s, 1.0, 0.0)
            sums = sums + dot_nt(chosen, grads[s] * ref.q_sum[s, kind], HIGH)
    sums = jnp.concatenate([sums, jnp.zeros((8, CH), F32)], axis=1)
    ref.k_send[...] = sums[0:4, :] + roll64(sums[4:8, :])
    ref.k_land[0] = ref.k_send[...]
    k_wait = wire.spread(
        total,
        wire.any_peer,
        lambda i: ref.k_send,
        lambda i: ref.k_land.at[i],
        ref.k_land.at[pl.ds(1, total - 1)],
    )
    scaled_grads = [grads[s] * scales[:, s : s + 1] for s in range(SCENES)]
    weight_grad = jnp.zeros((CH, LANES), F32)
    for c in range(FEATS):
        product = scaled_grads[0] * ref.t_sum[0, c]
        for s in range(1, SCENES):
            product = product + scaled_grads[s] * ref.t_sum[s, c]
        weight_grad = jnp.where(lane == c, jnp.sum(product, axis=1, keepdims=True), weight_grad)
    ref.p_col[...] = weight_grad
    for i in range(n_rows):
        owner = lax.rem(row + i, n_rows)
        block = ref.p_col[pl.ds(pl.multiple_of(owner * 8, 8), 8), :]
        ref.p_send[i] = block
        if i == 0:
            ref.p_land[0] = block
    p_wait = wire.spread(
        n_rows,
        wire.row_peer,
        lambda i: ref.p_send.at[i],
        lambda i: ref.p_land.at[i],
        ref.p_land.at[pl.ds(1, n_rows - 1)],
    )

    for s in range(SCENES):
        scaled_w = w_row * norm0[s][2]
        coarse = low(scaled_w)
        matrix = jnp.where(first_half, coarse, roll64(scaled_w - coarse)).astype(BF16)
        for j in range(DEPTH // 4):
            block = [
                (ref.slope[s, 4 * j + t] * grads[s]).astype(BF16) for t in range(4)
            ]
            block = jnp.concatenate(block, axis=1)
            ref.upd[s, :, j * 4 * LANES : (j + 1) * 4 * LANES] = dot_nn(
                matrix, jnp.concatenate([block, block], axis=0)
            )

    p_wait.wait_recv()
    block = jnp.sum(ref.p_land[...], axis=0)
    ref.p2_send[...] = block
    ref.p2_land[0] = block
    p2_wait = wire.spread(
        n_cols,
        wire.col_peer,
        lambda i: ref.p2_send,
        lambda i: ref.p2_land.at[i],
        ref.p2_land.at[pl.ds(1, n_cols - 1)],
    )

    g2_wait.wait_recv()
    block = jnp.sum(ref.g2_land[...].astype(F32), axis=0)
    ref.conv_grad[0] = block[0:OWN_ROWS, 0:CH]
    ref.conv_grad[1] = roll64(block)[0:OWN_ROWS, 0:CH]

    k_wait.wait_recv()
    sums = jnp.sum(ref.k_land[...], axis=0)
    swapped = roll64(sums)
    bias_sum, gain_sum = jnp.zeros((1, LANES), F32), jnp.zeros((1, LANES), F32)
    correction = jnp.zeros((16, LANES), F32)
    for s in range(SCENES):
        center, factor, scale, count, cross, products = norm0[s]
        grad_sum = jnp.where(first_half, sums[s : s + 1, :], 0.0)
        scaled_sum = jnp.where(first_half, swapped[s : s + 1, :], 0.0)
        gain_safe = jnp.where(first_half, gain0, 1.0)
        scaled_sum = (scaled_sum - bias0 * grad_sum) / gain_safe
        bias_sum, gain_sum = bias_sum + grad_sum, gain_sum + scaled_sum
        grad_mean, scaled_mean = grad_sum / count, scaled_sum / count
        point_sums = products[:, 9:10]
        correction = correction + scale * (
            grad_mean * point_sums + scaled_mean * factor * (cross - center * point_sums)
        )
        unit = w_row * factor - jnp.where(feature_row == FEATS, center * factor, 0.0)
        unit = unit * scaled_mean + jnp.where(feature_row == FEATS, grad_mean, 0.0)
        mix = dot_nt(w_row * scale, unit, HIGH)
        coarse = low(mix)
        fine = mix - coarse
        mix = jnp.concatenate([coarse, fine], axis=1).astype(BF16)
        out = ref.point_grads.at[s]
        for j in range(DEPTH // 4):
            lanes = slice(j * 4 * LANES, (j + 1) * 4 * LANES)
            points = aug[s, :, lanes]
            value = ref.upd[s, :, lanes] - dot_nn(
                mix, jnp.concatenate([points, points], axis=0)
            )
            for t in range(4):
                n = 4 * j + t
                at = slice(t * LANES, (t + 1) * LANES)
                out[pl.ds(n, 8, stride=DEPTH), :] = value[0:8, at]
                out[8 * DEPTH + n : 8 * DEPTH + n + 1, :] = value[8:9, at]

    def own_lanes(values):
        return pltpu.roll(values, lax.rem(LANES - 8 * row, LANES), axis=1)

    def both_scenes(values, index):
        added = values[index : index + 1, :] + values[2 + index : 3 + index, :]
        return added + roll64(added)

    small = ref.small
    small[...] = jnp.zeros((8, LANES), F32)
    small[0:1, :] = bias_sum
    small[1:2, :] = both_scenes(total1, 0)
    small[2:3, :] = both_scenes(total2, 0)
    small[3:4, :] = gain_sum
    small[4:5, :] = both_scenes(total1, 1)
    small[5:6, :] = both_scenes(total2, 1)
    owned = own_lanes(small[...])
    ref.bias_grad[...] = owned[0:3, 0:8]
    ref.gain_grad[...] = owned[3:6, 0:8]
    correction = own_lanes(correction)

    p2_wait.wait_recv()
    block = jnp.sum(ref.p2_land[...], axis=0)
    block = jnp.concatenate([block, jnp.zeros((LANES - 8, LANES), F32)], axis=0)
    ref.pfn_grad[...] = (jnp.transpose(block)[0:16, :] - correction)[0:FEATS, 0:8]
    wire.settle()


def body(points, counts, tiles, cells, pfn_weight, conv_weight, norm_gain, norm_bias, cotangent):
    scenes, feats, depth, pillars = points.shape
    n_rows, n_cols = lax.axis_size("rows"), lax.axis_size("cols")
    vmem = pl.BlockSpec(memory_space=pltpu.VMEM)
    results = pl.pallas_call(
        functools.partial(step_kernel, n_rows, n_cols),
        out_shape=(
            jax.ShapeDtypeStruct(cotangent.shape, BF16),
            jax.ShapeDtypeStruct((scenes, feats * depth, pillars), F32),
            jax.ShapeDtypeStruct(pfn_weight.shape, F32),
            jax.ShapeDtypeStruct(conv_weight.shape, F32),
            jax.ShapeDtypeStruct(norm_gain.shape, F32),
            jax.ShapeDtypeStruct(norm_bias.shape, F32),
        ),
        in_specs=[vmem] * 9,
        out_specs=[vmem] * 6,
        scratch_shapes=[pltpu.VMEM(shape, dtype) for shape, dtype in SCRATCH.values()]
        + [pltpu.SemaphoreType.DMA((SEMS,)), pltpu.SemaphoreType.DMA((SEMS,))],
        compiler_params=pltpu.CompilerParams(
            collective_id=0, has_side_effects=True, vmem_limit_bytes=60 * 2**20
        ),
    )(
        points.reshape(scenes, feats * depth, pillars),
        counts,
        tiles.reshape(scenes, pillars),
        cells,
        pfn_weight,
        conv_weight,
        norm_gain,
        norm_bias,
        cotangent,
    )
    return (results[0], results[1].reshape(points.shape), *results[2:])


def solution(mesh):
    in_specs = (
        P(None, None, None, ("rows", "cols")),
        P(None, ("rows", "cols")),
        P(None, ("rows", "cols"), None),
        P(None, ("rows", "cols")),
        P(None, "rows"),
        P(None, "rows", None),
        P(None, "rows"),
        P(None, "rows"),
        P(None, "rows", "cols"),
    )
    out_specs = (
        P(None, "rows", "cols"),
        P(None, None, None, ("rows", "cols")),
        P(None, "rows"),
        P(None, "rows", None),
        P(None, "rows"),
        P(None, "rows"),
    )
    return jax.shard_map(body, mesh=mesh, in_specs=in_specs, out_specs=out_specs, check_vma=False)
```

```python
import functools
import types

import jax
import jax.numpy as jnp
from jax import lax
from jax.experimental import pallas as pl
from jax.experimental.pallas import tpu as pltpu
from jax.sharding import PartitionSpec as P

EPSILON = 1e-05
HIGH = lax.Precision.HIGHEST
MESH = pl.DeviceIdType.MESH
F32, BF16, I32 = jnp.float32, jnp.bfloat16, jnp.int32

SCENES = 4
PAIRS = 2
FEATS = 9
DEPTH = 32
PILLARS = 128
CH = 64
LANES = 128
HALF_ROWS = 32
HALF_COLS = 16
PIXELS = HALF_ROWS * HALF_COLS
SLOTS = 3
EDGE = 8
EXT_COLS = 32
EXT_ROWS = HALF_ROWS + 2
TAPS = 9
OWN_ROWS = 72
PAD_ROWS = 80


def dot_nn(a, b, precision=None):
    return lax.dot_general(
        a, b, (((1,), (0,)), ((), ())), precision=precision, preferred_element_type=F32
    )


def dot_nt(a, b, precision=None):
    return lax.dot_general(
        a, b, (((1,), (1,)), ((), ())), precision=precision, preferred_element_type=F32
    )


def dot_tn(a, b):
    return lax.dot_general(a, b, (((0,), (0,)), ((), ())), preferred_element_type=F32)


def iota(shape, dim):
    return lax.broadcasted_iota(I32, shape, dim)


def sigmoid(v):
    return 0.5 * jnp.tanh(0.5 * v) + 0.5


def low(v):
    return v.astype(BF16).astype(F32)


def one_hot(mask):
    return jnp.where(mask, 1.0, 0.0).astype(BF16)


def square_of(v):
    rows, cols = v.shape
    if cols < LANES:
        v = jnp.concatenate([v, jnp.zeros((rows, LANES - cols), v.dtype)], axis=1)
    return jnp.concatenate([v, jnp.zeros((LANES - rows, LANES), v.dtype)], axis=0)


def roll64(v):
    return pltpu.roll(v, CH, axis=1)


SCRATCH = dict(
    points=((SCENES, FEATS * DEPTH, LANES), BF16),
    counts=((SCENES, LANES), I32),
    tiles=((SCENES, LANES), I32),
    cells=((SCENES, LANES), I32),
    pfn=((8, FEATS), BF16),
    conv=((2, CH, OWN_ROWS), BF16),
    gain=((3, 8), BF16),
    bias=((3, 8), BF16),
    cotangent=((SCENES, HALF_ROWS, HALF_COLS * CH), BF16),
    features=((SCENES, HALF_ROWS, HALF_COLS * CH), BF16),
    point_grads=((SCENES, FEATS * DEPTH, LANES), F32),
    pfn_grad=((8, FEATS), F32),
    conv_grad=((2, CH, OWN_ROWS), F32),
    gain_grad=((3, 8), F32),
    bias_grad=((3, 8), F32),
    square=((LANES, LANES), F32),
    w_tmp=((16, LANES), F32),
    w_send=((16, LANES), F32),
    w_land=((8, 16, LANES), F32),
    c_send=((PAD_ROWS, LANES), BF16),
    c_land=((8, PAD_ROWS, LANES), BF16),
    taps=((TAPS * CH, LANES), F32),
    wide1=((TAPS * LANES, LANES), BF16),
    side1=((3 * LANES, LANES), BF16),
    wide2=((TAPS * LANES, LANES), BF16),
    back2=((TAPS * LANES, LANES), BF16),
    back1=((4 * LANES, 4 * LANES), BF16),
    pts32=((SCENES, 16 * DEPTH, LANES), F32),
    aug=((SCENES, 16, DEPTH * LANES), BF16),
    hot=((SCENES * SLOTS, LANES, LANES), BF16),
    b_send=((128, 8, LANES), F32),
    b_land=((128, 8, LANES), F32),
    gram=((SCENES, 16, LANES), F32),
    place=((PAIRS, PIXELS, 6 * LANES), BF16),
    rim=((PAIRS, 48, 6 * LANES), BF16),
    parity=((PAIRS, 6 * LANES, 4 * LANES), BF16),
    fetch=((PAIRS, 6 * LANES, PIXELS), BF16),
    pre=((SCENES, DEPTH, CH, LANES), F32),
    act=((SCENES, DEPTH, CH, LANES), F32),
    share=((SCENES, DEPTH, CH, LANES), F32),
    pil=((SCENES, CH, LANES), F32),
    t_sum=((SCENES, FEATS, CH, LANES), F32),
    q_sum=((SCENES, 2, CH, LANES), F32),
    x_send=((PAIRS, 128, 8, LANES), F32),
    x_land=((PAIRS, 128, 8, LANES), F32),
    y_send=((PAIRS, 128, 8, LANES), F32),
    y_land=((PAIRS, 128, 8, LANES), F32),
    rim_send=((PAIRS, 2, 48, LANES), F32),
    rim_land=((PAIRS, 2, 56, LANES), F32),
    im1=((PAIRS, PIXELS, TAPS * LANES), BF16),
    top1=((PAIRS, 16, 3 * LANES), BF16),
    left1=((PAIRS, 32, 3 * LANES), BF16),
    im2=((PAIRS, PIXELS, TAPS * LANES), BF16),
    y1=((PAIRS, PIXELS, LANES), F32),
    y2=((PAIRS, PIXELS, LANES), F32),
    x1=((PAIRS, PIXELS, LANES), F32),
    x2=((PAIRS, PIXELS, LANES), F32),
    s1=((PAIRS, PIXELS, LANES), F32),
    g1=((PAIRS, PIXELS, LANES), F32),
    g2=((PAIRS, PIXELS, LANES), F32),
    feat=((PAIRS, PIXELS, LANES), F32),
    cot=((PAIRS, PIXELS, LANES), F32),
    d1=((PAIRS, PIXELS, LANES), F32),
    d2=((PAIRS, PIXELS, LANES), BF16),
    cols=((4, PAIRS, 2, HALF_ROWS, LANES), F32),
    halo=((4, PAIRS, LANES, LANES), F32),
    ext=((3, PAIRS, EXT_ROWS * EXT_COLS, LANES), F32),
    st_send=((10, 2, LANES), F32),
    st_land=((10, 128, 2, LANES), F32),
    grads=((SCENES, CH, LANES), F32),
    p_col=((CH, LANES), F32),
    p_send=((8, 8, LANES), F32),
    p_land=((8, 8, LANES), F32),
    p2_send=((8, LANES), F32),
    p2_land=((16, 8, LANES), F32),
    dk=((TAPS * CH, LANES), F32),
    g_send=((8, PAD_ROWS, LANES), BF16),
    g_land=((8, PAD_ROWS, LANES), BF16),
    g2_send=((PAD_ROWS, LANES), BF16),
    g2_land=((16, PAD_ROWS, LANES), BF16),
    upd=((SCENES, 16, DEPTH * LANES), F32),
    small=((8, LANES), F32),
)
INPUTS = 9
RESULTS = 6
SEMS = 96


class Wire:
    def __init__(self, n_rows, n_cols, send_sems, recv_sems):
        self.n_rows, self.n_cols = n_rows, n_cols
        self.total = n_rows * n_cols
        self.row, self.col = lax.axis_index("rows"), lax.axis_index("cols")
        self.me = self.row * n_cols + self.col
        self.send_sems, self.recv_sems = send_sems, recv_sems
        self.used = 0
        self.sent = []

    def any_peer(self, step):
        other = jnp.bitwise_and(self.me + step, self.total - 1)
        return (
            jnp.right_shift(other, self.n_cols.bit_length() - 1),
            jnp.bitwise_and(other, self.n_cols - 1),
        )

    def row_peer(self, step):
        return (lax.rem(self.row + step + self.n_rows, self.n_rows), self.col)

    def col_peer(self, step):
        return (self.row, lax.rem(self.col + step + self.n_cols, self.n_cols))

    def near(self, down, right):
        return (
            lax.rem(self.row + down + self.n_rows, self.n_rows),
            lax.rem(self.col + right + self.n_cols, self.n_cols),
        )

    def copy(self, src, dst, sem, peer):
        return pltpu.make_async_remote_copy(
            src_ref=src,
            dst_ref=dst,
            send_sem=self.send_sems.at[sem],
            recv_sem=self.recv_sems.at[sem],
            device_id=peer,
            device_id_type=MESH,
        )

    def one(self, src, dst, peer):
        sem = self.used
        self.used += 1
        copy = self.copy(src, dst, sem, peer)
        copy.start()
        self.sent.append(copy)
        return copy

    def spread(self, count, peer_of, src_of, dst_of, whole):
        sem = self.used
        self.used += 1

        def step(i, carry):
            self.copy(src_of(i), dst_of(i), sem, peer_of(i)).start()
            return carry

        lax.fori_loop(1, count, step, 0, unroll=8)
        copy = self.copy(whole, whole, sem, peer_of(1))
        self.sent.append(copy)
        return copy

    def local(self, src, dst, sems, index):
        copy = pltpu.make_async_copy(src, dst, sems.at[index])
        copy.start()
        return copy

    def settle(self):
        for copy in self.sent:
            copy.wait_send()


def step_kernel(n_rows, n_cols, *refs):
    inputs, results = refs[:INPUTS], refs[INPUTS : INPUTS + RESULTS]
    ref = types.SimpleNamespace(**dict(zip(SCRATCH, refs[INPUTS + RESULTS :], strict=False)))
    send_sems, recv_sems, in_sems, out_sems = refs[-4:]
    wire = Wire(n_rows, n_cols, send_sems, recv_sems)
    total, row, col, me = wire.total, wire.row, wire.col, wire.me
    lane = iota((1, LANES), 1)
    first_half = lane < CH

    held = [
        ref.points, ref.counts, ref.tiles, ref.cells, ref.pfn, ref.conv, ref.gain, ref.bias,
        ref.cotangent,
    ]
    order = [1, 0, 2, 3, 4, 6, 7, 5, 8]
    loads = {i: wire.local(inputs[i], held[i], in_sems, i) for i in order}
    barrier = pltpu.get_barrier_semaphore()

    def greet(i, carry):
        pl.semaphore_signal(barrier, inc=1, device_id=wire.any_peer(i), device_id_type=MESH)
        return carry

    lax.fori_loop(1, total, greet, 0, unroll=8)

    for i in range(INPUTS):
        loads[i].wait()
    pts32, aug = ref.pts32, ref.aug
    slot_number = iota((DEPTH, LANES), 0)
    for s in range(SCENES):
        valid = slot_number < ref.counts[s : s + 1, :]
        for c in range(FEATS):
            block = ref.points[s, c * DEPTH : (c + 1) * DEPTH, :].astype(F32)
            pts32[s, c * DEPTH : (c + 1) * DEPTH, :] = jnp.where(valid, block, 0.0)
        pts32[s, FEATS * DEPTH : (FEATS + 1) * DEPTH, :] = jnp.where(valid, 1.0, 0.0)
        pts32[s, (FEATS + 1) * DEPTH :, :] = jnp.zeros((6 * DEPTH, LANES), F32)
        scene_pts = pts32.at[s]
        for n in range(DEPTH):
            aug[s, :, n * LANES : (n + 1) * LANES] = scene_pts[pl.ds(n, 16, stride=DEPTH), :].astype(
                BF16
            )
    stacked = jnp.concatenate([aug[s] for s in range(SCENES)], axis=0)
    gram_all = dot_nt(stacked, jnp.concatenate([stacked, stacked], axis=0))
    moments = jnp.zeros((4, LANES), F32)
    for s in range(SCENES):
        for b in range(3):
            piece = gram_all[16 * s + 4 * b : 16 * s + 4 * b + 4, :]
            at = 40 * b + 10 * s
            piece = pltpu.roll(piece, (at - 16 * s) % LANES, axis=1)
            moments = moments + jnp.where((lane >= at) & (lane < at + 10), piece, 0.0)

    hot = ref.hot
    above = iota((LANES, LANES), 0) < iota((LANES, LANES), 1)
    slot_row = iota((LANES, LANES), 0).astype(F32) * 4.0
    for s in range(SCENES):
        tile = lax.rem(ref.tiles[s : s + 1, :] - me + total, total).astype(F32)
        wide = jnp.broadcast_to(tile, (LANES, LANES))
        same = (jnp.transpose(wide) == wide) & above
        rank = jnp.sum(jnp.where(same, 1.0, 0.0), axis=0, keepdims=True)
        code = tile * 4.0 + rank
        for k in range(SLOTS):
            hot[s * SLOTS + k] = one_hot(slot_row + float(k) == code)

    b_send = ref.b_send.reshape(128 * 8, LANES)
    lane_row = iota((LANES, LANES), 0)
    for q in range(4):
        extra = jnp.zeros((LANES, LANES), F32)
        for pair in range(PAIRS):
            s = 2 * pair + q // 2
            cell = ref.cells[s : s + 1, :]
            spot = (jnp.bitwise_and(cell, 31) if q % 2 else jnp.right_shift(cell, 5)) + 1
            for k in range(SLOTS):
                at = jnp.where(lane_row == 120 + 3 * pair + k, spot.astype(F32), 0.0)
                extra = extra + dot_nt(hot[s * SLOTS + k], at.astype(BF16))
        b_send[pl.ds(q, 128, stride=8), :] = extra + moments[q : q + 1, :]
    ref.b_land[0, 0:4, :] = ref.b_send[0, 0:4, :]

    ref.square[...] = jnp.zeros((LANES, LANES), F32)
    ref.square[0:8, 0:FEATS] = ref.pfn[...].astype(F32)
    ref.w_tmp[...] = jnp.transpose(ref.square[...])[0:16, :]
    ref.w_tmp[9:12, 0:8] = ref.gain[...].astype(F32)
    ref.w_tmp[12:15, 0:8] = ref.bias[...].astype(F32)
    ref.w_send[...] = pltpu.roll(ref.w_tmp[...], row * 8, axis=1)
    ref.w_land[0] = ref.w_send[...]
    pl.semaphore_wait(barrier, total - 1)
    w_wait = wire.spread(
        n_rows,
        wire.row_peer,
        lambda i: ref.w_send,
        lambda i: ref.w_land.at[i],
        ref.w_land.at[pl.ds(1, n_rows - 1)],
    )
    b_wait = wire.spread(
        total,
        wire.any_peer,
        lambda i: ref.b_send.at[i, pl.ds(0, 4)],
        lambda i: ref.b_land.at[i, pl.ds(0, 4)],
        ref.b_land.at[pl.ds(1, total - 1), pl.ds(0, 4)],
    )

    def halo_send(values, index, pair, full):
        cols, halo = ref.cols.at[index, pair], ref.halo.at[index, pair]
        inner = values.at[pair]
        for side in range(2 if full else 1):
            cols[side] = inner[pl.ds(side * (HALF_COLS - 1), HALF_ROWS, stride=HALF_COLS), :]

        def send(src, start, count, at, down, right):
            return wire.one(
                src.at[pl.ds(start, count)], halo.at[pl.ds(at, count)], wire.near(down, right)
            )

        waits = [
            send(inner, 0, 8, 120, -1, -1),
            send(cols.at[0], 0, 32, 64, 0, -1),
            send(inner, 0, 16, 16, -1, 0),
        ]
        if full:
            waits += [
                send(inner, 504, 8, 96, 1, 1),
                send(inner, 8, 8, 112, -1, 1),
                send(inner, 496, 8, 104, 1, -1),
                send(cols.at[1], 0, 32, 32, 0, 1),
                send(inner, 496, 16, 0, 1, 0),
            ]
        return waits

    def there(cond):
        return jnp.where(cond, 1.0, 0.0)

    up, down = there(row > 0), there(row < n_rows - 1)
    left, right = there(col > 0), there(col < n_cols - 1)
    spot = iota((LANES, LANES), 0)
    halo_mask = jnp.where(spot < 16, up, jnp.where(spot < 32, down, jnp.where(spot < 64, left, right)))
    halo_mask = jnp.where(spot < 96, halo_mask, jnp.where(spot < 112, up, down))
    halo_mask = jnp.where(
        spot < 96,
        halo_mask,
        halo_mask * jnp.where((spot < 104) | ((spot >= 112) & (spot < 120)), left, right),
    )

    def fill_ext(index, pair, inner, edge):
        grid = ref.ext.at[index, pair]
        for i in range(HALF_ROWS):
            at = (i + 1) * EXT_COLS + EDGE
            grid[at : at + HALF_COLS, :] = inner[i * HALF_COLS : (i + 1) * HALF_COLS, :]
        grid[EDGE : EDGE + HALF_COLS, :] = edge[0:16, :]
        last = (EXT_ROWS - 1) * EXT_COLS
        grid[last + EDGE : last + EDGE + HALF_COLS, :] = edge[16:32, :]
        grid[pl.ds(EXT_COLS + EDGE - 1, HALF_ROWS, stride=EXT_COLS), :] = edge[32:64, :]
        grid[pl.ds(EXT_COLS + EDGE + HALF_COLS, HALF_ROWS, stride=EXT_COLS), :] = edge[64:96, :]
        grid[EDGE - 1 : EDGE, :] = edge[103:104, :]
        grid[EDGE + HALF_COLS : EDGE + HALF_COLS + 1, :] = edge[104:105, :]
        grid[last + EDGE - 1 : last + EDGE, :] = edge[119:120, :]
        grid[last + EDGE + HALF_COLS : last + EDGE + HALF_COLS + 1, :] = edge[120:121, :]

    def shifted(index, pair, shift, rows):
        grid = ref.ext.at[index, pair]
        start = EDGE - 1 + shift
        return [
            grid[i * EXT_COLS + start : i * EXT_COLS + start + HALF_COLS, :].astype(BF16)
            for i in rows
        ]

    def column_sum(v):
        return jnp.sum(v, axis=0, keepdims=True)

    def global_sums(index, first, second):
        send, land = ref.st_send.at[index], ref.st_land.at[index]
        send[0:1, :] = first
        send[1:2, :] = second
        land[0] = send[...]
        return wire.spread(
            total,
            wire.any_peer,
            lambda i: send,
            lambda i: land.at[i],
            land.at[pl.ds(1, total - 1)],
        )

    def summed(index):
        return jnp.sum(ref.st_land[index], axis=0)

    pixel_total = float(PIXELS * total)

    def norm_of(sums):
        center = sums[0:1, :] / pixel_total
        spread = sums[1:2, :] / pixel_total - center * center
        return center, lax.rsqrt(spread + EPSILON)

    cot = ref.cot
    for pair in range(PAIRS):
        spread_to = cot.at[pair]
        for m in range(HALF_COLS // 2):
            a = ref.cotangent[2 * pair, :, m * LANES : (m + 1) * LANES].astype(F32)
            b = ref.cotangent[2 * pair + 1, :, m * LANES : (m + 1) * LANES].astype(F32)
            spread_to[pl.ds(2 * m, HALF_ROWS, stride=HALF_COLS), :] = jnp.where(
                first_half, a, roll64(b)
            )
            spread_to[pl.ds(2 * m + 1, HALF_ROWS, stride=HALF_COLS), :] = jnp.where(
                first_half, roll64(a), b
            )
    ref.square[:, 0:OWN_ROWS] = jnp.concatenate(
        [ref.conv[0].astype(F32), ref.conv[1].astype(F32)], axis=0
    )
    ref.c_send[...] = jnp.transpose(ref.square[...])[0:PAD_ROWS, :].astype(BF16)
    ref.c_land[0] = ref.c_send[...]
    w_wait.wait_recv()
    b_wait.wait_recv()

    c_wait = wire.spread(
        n_rows,
        wire.row_peer,
        lambda i: ref.c_send,
        lambda i: ref.c_land.at[i],
        ref.c_land.at[pl.ds(1, n_rows - 1)],
    )
    cot_waits = [wait for pair in range(PAIRS) for wait in halo_send(cot, 0, pair, True)]
    w_full = jnp.sum(ref.w_land[...], axis=0)
    feature_row = iota((16, LANES), 0)
    w_row = jnp.where(feature_row < FEATS, w_full, 0.0)

    def twice(v):
        return v + roll64(v)

    gain0, bias0 = w_full[9:10, :], w_full[12:13, :]
    gain1, bias1 = twice(w_full[10:11, :]), twice(w_full[13:14, :])
    gain2, bias2 = twice(w_full[11:12, :]), twice(w_full[14:15, :])
    moments = jnp.sum(ref.b_land[:, 0:4, :], axis=0)
    gram = ref.gram
    norm0, matrices = [], []
    for s in range(SCENES):
        gram[s] = jnp.zeros((16, LANES), F32)
        for b in range(3):
            piece = pltpu.roll(moments, (LANES - 40 * b - 10 * s) % LANES, axis=1)
            gram[s, 4 * b : 4 * b + 4, :] = jnp.where(lane < 10, piece, 0.0)
    for s in range(SCENES):
        products = gram[s]
        cross = dot_nn(products[:, 0:16], w_row, HIGH)
        count = products[9:10, 9:10]
        center = cross[9:10, :] / count
        spread = column_sum(w_row * cross) / count - center * center
        factor = lax.rsqrt(spread + EPSILON)
        scale = factor * gain0
        norm0.append((center, factor, scale, count, cross, products))
        folded = w_row * scale + jnp.where(feature_row == FEATS, bias0 - center * scale, 0.0)
        coarse = low(folded)
        both = square_of(jnp.concatenate([coarse, low(folded - coarse)], axis=0))
        matrices.append(jnp.transpose(both)[0:CH, 0:32].astype(BF16))

    STEP = 8
    x_waits = []
    for pair in range(PAIRS):
        for s in (2 * pair, 2 * pair + 1):
            bound = ref.counts[s : s + 1, :]
            matrix = matrices[s]

            def forward(j, peak, s=s, matrix=matrix, bound=bound):
                width = STEP * LANES
                points = aug[s, :, pl.ds(pl.multiple_of(j * width, width), width)]
                value = dot_nn(matrix, jnp.concatenate([points, points], axis=0))
                for t in range(STEP):
                    n = STEP * j + t
                    pre = value[:, t * LANES : (t + 1) * LANES]
                    active = jnp.where(n < bound, pre * sigmoid(pre), -1e30)
                    ref.pre[s, n] = pre
                    ref.act[s, n] = active
                    peak = jnp.maximum(peak, active)
                return peak

            peak = lax.fori_loop(0, DEPTH // STEP, forward, jnp.full((CH, LANES), -1e30, F32))

            def gather_exp(j, whole, s=s, peak=peak):
                for t in range(STEP):
                    whole = whole + jnp.exp(ref.act[s, STEP * j + t] - peak)
                return whole

            whole = lax.fori_loop(0, DEPTH // STEP, gather_exp, jnp.zeros((CH, LANES), F32))
            ref.pil[s] = peak + jnp.log(whole)
        x_send = ref.x_send.at[pair].reshape(128 * 8, LANES)
        a, b = ref.pil[2 * pair].astype(BF16), ref.pil[2 * pair + 1].astype(BF16)
        none = jnp.zeros((CH, LANES), BF16)
        both = jnp.concatenate(
            [jnp.concatenate([a, none], axis=1), jnp.concatenate([none, b], axis=1)], axis=0
        )
        for k in range(SLOTS):
            pick = jnp.concatenate(
                [hot[2 * pair * SLOTS + k], hot[(2 * pair + 1) * SLOTS + k]], axis=1
            )
            x_send[pl.ds(k, 128, stride=8), :] = dot_nt(pick, both)
        ref.x_land[pair, 0, 0:SLOTS, :] = ref.x_send[pair, 0, 0:SLOTS, :]
        x_waits.append(
            wire.spread(
                total,
                wire.any_peer,
                lambda i, pair=pair: ref.x_send.at[pair, i, pl.ds(0, SLOTS)],
                lambda i, pair=pair: ref.x_land.at[pair, i, pl.ds(0, SLOTS)],
                ref.x_land.at[pair, pl.ds(1, total - 1), pl.ds(0, SLOTS)],
            )
        )

    b_land = ref.b_land.reshape(128 * 8, LANES)
    pieces = [b_land[pl.ds(q, 128, stride=8), :] for q in range(4)]
    turned = [jnp.transpose(piece) for piece in pieces]
    place, rim, parity, fetch = ref.place, ref.rim, ref.parity, ref.fetch

    def pixel_of(tall, wide):
        i, j = tall.astype(I32) - 1, wide.astype(I32) - 1
        pixel = jnp.right_shift(i, 1) * HALF_COLS + jnp.right_shift(j, 1)
        plane = 2 * jnp.bitwise_and(i, 1) + jnp.bitwise_and(j, 1)
        return jnp.where(i < 0, -1, pixel), jnp.where(i < 0, -1, plane)

    rim_pixel = iota((48, LANES), 0)
    rim_pixel = jnp.where(rim_pixel < 16, 496 + rim_pixel, rim_pixel * 16 - 241)
    for pair in range(PAIRS):
        for half in range(2):
            for k in range(SLOTS):
                at = 120 + 3 * pair + k
                block = (half * SLOTS + k) * LANES
                blocks = slice(block, block + LANES)
                across, _ = pixel_of(
                    turned[2 * half][at : at + 1, :], turned[2 * half + 1][at : at + 1, :]
                )
                _, along = pixel_of(
                    pieces[2 * half][:, at : at + 1], pieces[2 * half + 1][:, at : at + 1]
                )
                along = jnp.broadcast_to(along, (LANES, LANES))
                for m in range(4):
                    tile = slice(m * LANES, (m + 1) * LANES)
                    place[pair, tile, blocks] = one_hot(
                        iota((LANES, LANES), 0) + m * LANES == across
                    )
                    parity[pair, blocks, tile] = one_hot(along == m)
                rim[pair, :, blocks] = one_hot(rim_pixel == across)

    c_wait.wait_recv()
    taps = ref.taps
    for i in range(n_rows):
        owner = lax.rem(row - i + n_rows, n_rows)
        taps[pl.ds(pl.multiple_of(owner * OWN_ROWS, 8), OWN_ROWS), :] = ref.c_land[i].astype(F32)[
            0:OWN_ROWS, :
        ]
    ref.back1[...] = jnp.zeros((4 * LANES, 4 * LANES), BF16)
    for t in range(TAPS):
        both = taps[t * CH : (t + 1) * CH, :]
        swapped = roll64(both)
        at = t * LANES
        k1 = jnp.concatenate(
            [jnp.where(first_half, both, 0.0), jnp.where(first_half, 0.0, swapped)], axis=0
        )
        k2 = jnp.concatenate(
            [jnp.where(first_half, swapped, 0.0), jnp.where(first_half, 0.0, both)], axis=0
        )
        ref.wide1[at : at + LANES, :] = k1.astype(BF16)
        if t % 3 == 0:
            ref.side1[t // 3 * LANES : (t // 3 + 1) * LANES, :] = k1.astype(BF16)
        ref.wide2[at : at + LANES, :] = k2.astype(BF16)
        ref.back2[at : at + LANES, :] = jnp.transpose(k2).astype(BF16)
        a, b = t // 3, t % 3
        window = 2 * (a == 0) + (b == 0)
        plane = 2 * (a != 1) + (b != 1)
        ref.back1[
            window * LANES : (window + 1) * LANES, plane * LANES : (plane + 1) * LANES
        ] = jnp.transpose(k1).astype(BF16)

    planes_of, d_waits = [], []
    for pair in range(PAIRS):
        x_waits[pair].wait_recv()
        x_land = ref.x_land.at[pair].reshape(128 * 8, LANES)
        landed = [x_land[pl.ds(k, 128, stride=8), :] for k in range(SLOTS)]
        values = [jnp.where(first_half, v, 0.0) for v in landed]
        values += [jnp.where(first_half, 0.0, v) for v in landed]
        values = jnp.concatenate(values, axis=0).astype(BF16)
        values = jnp.concatenate([values] * 4, axis=1) * parity[pair]
        planes_of.append(values)
        edge = low(dot_nn(rim[pair], values))
        rim_send, rim_land = ref.rim_send.at[pair], ref.rim_land.at[pair]
        rim_send[0, 0:16, :] = edge[0:16, 2 * LANES : 3 * LANES]
        rim_send[1, 0:16, :] = edge[0:16, 3 * LANES :]
        rim_send[0, 16:48, :] = edge[16:48, LANES : 2 * LANES]
        rim_send[1, 16:48, :] = edge[16:48, 3 * LANES :]
        d_waits.append(
            [
                wire.one(rim_send.at[1, pl.ds(40, 8)], rim_land.at[0, pl.ds(48, 8)], wire.near(1, 1)),
                wire.one(
                    rim_send.at[:, pl.ds(16, 32)], rim_land.at[:, pl.ds(16, 32)], wire.near(0, 1)
                ),
                wire.one(rim_send.at[:, pl.ds(0, 16)], rim_land.at[:, pl.ds(0, 16)], wire.near(1, 0)),
            ]
        )

    y1 = ref.y1
    first_col = jnp.bitwise_and(iota((PIXELS, LANES), 0), HALF_COLS - 1) == 0
    no_row = jnp.zeros((HALF_COLS, LANES), BF16)
    for pair in range(PAIRS):
        grid = low(dot_nn(place[pair], planes_of[pair]))
        still = [grid[:, q * LANES : (q + 1) * LANES] for q in range(4)]
        moved = {q: jnp.where(first_col, 0.0, pltpu.roll(still[q], 1, axis=0)) for q in (1, 3)}
        for t in range(TAPS):
            a, b = t // 3, t % 3
            plane = 2 * (a != 1) + (b != 1)
            window = (moved[plane] if b == 0 else still[plane]).astype(BF16)
            if a == 0:
                window = jnp.concatenate([no_row, window[: PIXELS - HALF_COLS, :]], axis=0)
            ref.im1[pair, :, t * LANES : (t + 1) * LANES] = window
        y1[pair] = dot_nn(ref.im1[pair], ref.wide1[...])

    e_waits, e_edges = [], []
    for pair in range(PAIRS):
        for wait in d_waits[pair]:
            wait.wait_recv()
        rim_land = ref.rim_land.at[pair]
        rows_in = [rim_land[p, 0:16, :] * up for p in range(2)]
        cols_in = [rim_land[p, 16:48, :] * left for p in range(2)]
        corner = rim_land[0, 55:56, :] * (up * left)
        top = [
            jnp.where(iota((16, LANES), 0) == 0, corner, pltpu.roll(rows_in[1], 1, axis=0)),
            rows_in[0],
            rows_in[1],
        ]
        side = [
            jnp.where(iota((32, LANES), 0) == 0, 0.0, pltpu.roll(cols_in[1], 1, axis=0)),
            cols_in[0],
            cols_in[1],
        ]
        ref.top1[pair] = jnp.concatenate(top, axis=1).astype(BF16)
        ref.left1[pair] = jnp.concatenate(side, axis=1).astype(BF16)
        y1[pair, 0:16, :] += dot_nn(ref.top1[pair], ref.wide1[0 : 3 * LANES, :])
        beside = pl.ds(0, HALF_ROWS, stride=HALF_COLS)
        y1.at[pair][beside, :] += dot_nn(ref.left1[pair], ref.side1[...])
        value = y1[pair]
        e_waits.append(global_sums(pair, column_sum(value), column_sum(value * value)))
        e_edges.append(halo_send(y1, 1, pair, True))

    for pair in range(PAIRS):
        for half in range(2):
            for k in range(SLOTS):
                at = 120 + 3 * pair + k
                block = (half * SLOTS + k) * LANES
                along, _ = pixel_of(
                    pieces[2 * half][:, at : at + 1], pieces[2 * half + 1][:, at : at + 1]
                )
                along = jnp.broadcast_to(along, (LANES, LANES))
                for m in range(4):
                    fetch[pair, block : block + LANES, m * LANES : (m + 1) * LANES] = one_hot(
                        iota((LANES, LANES), 1) + m * LANES == along
                    )
    for wait in cot_waits:
        wait.wait_recv()

    norm1, f_waits, f_edges = [], [], []
    y2 = ref.y2
    for pair in range(PAIRS):
        e_waits[pair].wait_recv()
        for wait in e_edges[pair]:
            wait.wait_recv()
        center, factor = norm_of(summed(pair))
        norm1.append((center, factor))
        scaled = (y1[pair] - center) * factor
        pre = scaled * gain1 + bias1
        sigma = sigmoid(pre)
        edge = (ref.halo[1, pair] - center) * factor * gain1 + bias1
        fill_ext(0, pair, low(pre * sigma), low(edge * sigmoid(edge)) * halo_mask)
        for b in range(3):
            window = shifted(0, pair, b, range(EXT_ROWS))
            for a in range(3):
                t = 3 * a + b
                ref.im2[pair, :, t * LANES : (t + 1) * LANES] = jnp.concatenate(
                    window[a : a + HALF_ROWS], axis=0
                )
        value = dot_nn(ref.im2[pair], ref.wide2[...])
        y2[pair] = value
        f_waits.append(global_sums(2 + pair, column_sum(value), column_sum(value * value)))
        f_edges.append(halo_send(y2, 2, pair, True))
        ref.x1[pair] = scaled
        ref.s1[pair] = sigma * (1.0 + pre * (1.0 - sigma))

    def slopes(step, carry):
        s, block = step // 4, lax.rem(step, 4)
        rows = pl.ds(pl.multiple_of(block * 16, 16), 16)
        top = ref.pil[s, rows, :]

        def inner(j, sums):
            sums = list(sums)
            for t in range(2):
                n = 2 * j + t
                pre, active = ref.pre[s, n, rows, :], ref.act[s, n, rows, :]
                sigma = sigmoid(pre)
                share = jnp.exp(active - top) * (sigma + active * (1.0 - sigma))
                ref.share[s, n, rows, :] = share
                sums[0] = sums[0] + share
                sums[1] = sums[1] + share * pre
                for c in range(FEATS):
                    sums[2 + c] = sums[2 + c] + share * pts32[s, pl.ds(c * DEPTH + n, 1), :]
            return tuple(sums)

        zero = jnp.zeros((16, LANES), F32)
        sums = lax.fori_loop(0, DEPTH // 2, inner, (zero,) * (2 + FEATS))
        ref.q_sum[s, 0, rows, :] = sums[0]
        ref.q_sum[s, 1, rows, :] = sums[1]
        for c in range(FEATS):
            ref.t_sum[s, c, rows, :] = sums[2 + c]
        return carry

    lax.fori_loop(0, 2 * SCENES, slopes, 0)

    norm2, g_waits = [], []
    for pair in range(PAIRS):
        f_waits[pair].wait_recv()
        center, factor = norm_of(summed(2 + pair))
        norm2.append((center, factor))
        scaled = (y2[pair] - center) * factor
        pre = scaled * gain2 + bias2
        sigma = sigmoid(pre)
        grad = cot[pair] * (sigma * (1.0 + pre * (1.0 - sigma)))
        g_waits.append(global_sums(4 + pair, column_sum(grad), column_sum(grad * scaled)))
        ref.x2[pair] = scaled
        ref.g2[pair] = grad
        ref.feat[pair] = pre * sigma

    for pair in range(PAIRS):
        grid = ref.feat.at[pair]
        for m in range(HALF_COLS // 2):
            a = grid[pl.ds(2 * m, HALF_ROWS, stride=HALF_COLS), :]
            b = grid[pl.ds(2 * m + 1, HALF_ROWS, stride=HALF_COLS), :]
            at = slice(m * LANES, (m + 1) * LANES)
            ref.features[2 * pair, :, at] = jnp.where(first_half, a, roll64(b)).astype(BF16)
            ref.features[2 * pair + 1, :, at] = jnp.where(first_half, roll64(a), b).astype(BF16)
    outs = [wire.local(ref.features, results[0], out_sems, 0)]
    edges2 = []
    for pair in range(PAIRS):
        for wait in f_edges[pair]:
            wait.wait_recv()
        center, factor = norm2[pair]
        scaled = (ref.halo[2, pair] - center) * factor
        pre = scaled * gain2 + bias2
        sigma = sigmoid(pre)
        edges2.append((scaled, ref.halo[0, pair] * (sigma * (1.0 + pre * (1.0 - sigma)))))
    lax.fori_loop(2 * SCENES, 4 * SCENES, slopes, 0)

    total2, h_waits, h_edges = [], [], []
    for pair in range(PAIRS):
        g_waits[pair].wait_recv()
        sums = summed(4 + pair)
        total2.append(sums)
        scale = norm2[pair][1] * gain2
        mean_grad, mean_scaled = sums[0:1, :] / pixel_total, sums[1:2, :] / pixel_total
        inner = low(scale * (ref.g2[pair] - mean_grad - ref.x2[pair] * mean_scaled))
        edge_scaled, edge_grad = edges2[pair]
        edge = low(scale * (edge_grad - mean_grad - edge_scaled * mean_scaled)) * halo_mask
        ref.d2[pair] = inner.astype(BF16)
        fill_ext(1, pair, inner, edge)
        blocks = [None] * TAPS
        for b in range(3):
            window = shifted(1, pair, 2 - b, range(EXT_ROWS))
            for a in range(3):
                blocks[3 * a + b] = jnp.concatenate(window[2 - a : 2 - a + HALF_ROWS], axis=0)
        grad = dot_nn(jnp.concatenate(blocks, axis=1), ref.back2[...]) * ref.s1[pair]
        ref.g1[pair] = grad
        h_waits.append(global_sums(6 + pair, column_sum(grad), column_sum(grad * ref.x1[pair])))
        h_edges.append(halo_send(ref.g1, 3, pair, False))

    def both_halves(product):
        return product[0:CH, :] + roll64(product[CH:LANES, :])

    dk = ref.dk
    for t in range(TAPS):
        tap = slice(t * LANES, (t + 1) * LANES)
        product = dot_tn(ref.im2[0, :, tap], ref.d2[0]) + dot_tn(ref.im2[1, :, tap], ref.d2[1])
        dk[t * CH : (t + 1) * CH, :] = roll64(both_halves(product))

    total1, y_waits = [], []
    for pair in range(PAIRS):
        h_waits[pair].wait_recv()
        for wait in h_edges[pair]:
            wait.wait_recv()
        sums = summed(6 + pair)
        total1.append(sums)
        center, factor = norm1[pair]
        scale = factor * gain1
        mean_grad, mean_scaled = sums[0:1, :] / pixel_total, sums[1:2, :] / pixel_total
        inner = low(scale * (ref.g1[pair] - mean_grad - ref.x1[pair] * mean_scaled))
        edge_scaled = (ref.halo[1, pair] - center) * factor
        edge = low(scale * (ref.halo[3, pair] - mean_grad - edge_scaled * mean_scaled))
        edge = jnp.where(halo_mask > 0.0, edge, 0.0)
        ref.d1[pair] = inner
        fill_ext(2, pair, inner, edge)
        here = shifted(2, pair, 1, range(1, EXT_ROWS))
        beside = shifted(2, pair, 2, range(1, EXT_ROWS))
        windows = [here[:HALF_ROWS], beside[:HALF_ROWS], here[1:], beside[1:]]
        windows = jnp.concatenate([jnp.concatenate(w, axis=0) for w in windows], axis=1)
        value = dot_nn(windows, ref.back1[...]).astype(BF16)
        value = dot_nn(fetch[pair], value)
        y_send = ref.y_send.at[pair].reshape(128 * 8, LANES)
        chosen = []
        for block in range(2 * SLOTS):
            rows = slice(block * LANES, (block + 1) * LANES)
            picked = value[rows, 0:LANES] * parity[pair, rows, 0:LANES].astype(F32)
            for q in range(1, 4):
                tile = slice(q * LANES, (q + 1) * LANES)
                picked = picked + value[rows, tile] * parity[pair, rows, tile].astype(F32)
            chosen.append(picked)
        for k in range(SLOTS):
            y_send[pl.ds(k, 128, stride=8), :] = jnp.where(first_half, chosen[k], chosen[SLOTS + k])
        ref.y_land[pair, 0, 0:SLOTS, :] = ref.y_send[pair, 0, 0:SLOTS, :]
        y_waits.append(
            wire.spread(
                total,
                lambda i: wire.any_peer(-i),
                lambda i, pair=pair: ref.y_send.at[pair, i, pl.ds(0, SLOTS)],
                lambda i, pair=pair: ref.y_land.at[pair, i, pl.ds(0, SLOTS)],
                ref.y_land.at[pair, pl.ds(1, total - 1), pl.ds(0, SLOTS)],
            )
        )

    upper, lefts = jnp.zeros((3 * LANES, LANES), F32), jnp.zeros((3 * LANES, LANES), F32)
    own1 = [ref.d1[pair].astype(BF16) for pair in range(PAIRS)]
    for pair in range(PAIRS):
        beside = ref.d1.at[pair][pl.ds(0, HALF_ROWS, stride=HALF_COLS), :].astype(BF16)
        upper = upper + dot_tn(ref.top1[pair], own1[pair][0:HALF_COLS, :])
        lefts = lefts + dot_tn(ref.left1[pair], beside)
    for t in range(TAPS):
        tap = slice(t * LANES, (t + 1) * LANES)
        product = dot_tn(ref.im1[0, :, tap], own1[0]) + dot_tn(ref.im1[1, :, tap], own1[1])
        if t < 3:
            product = product + upper[tap, :]
        if t % 3 == 0:
            product = product + lefts[t // 3 * LANES : (t // 3 + 1) * LANES, :]
        at = slice(t * CH, (t + 1) * CH)
        dk[at, :] = jnp.where(first_half, both_halves(product), dk[at, :])
    padding = jnp.zeros((PAD_ROWS - OWN_ROWS, LANES), F32)
    for i in range(n_rows):
        owner = lax.rem(row + i, n_rows)
        block = dk[pl.ds(pl.multiple_of(owner * OWN_ROWS, 8), OWN_ROWS), :]
        block = jnp.concatenate([block, padding], axis=0).astype(BF16)
        ref.g_send[i] = block
        if i == 0:
            ref.g_land[0] = block
    g1_wait = wire.spread(
        n_rows,
        wire.row_peer,
        lambda i: ref.g_send.at[i],
        lambda i: ref.g_land.at[i],
        ref.g_land.at[pl.ds(1, n_rows - 1)],
    )
    scales = square_of(jnp.concatenate([norm0[s][2] for s in range(SCENES)], axis=0))
    scales = jnp.transpose(scales)[0:CH, :]

    k_waits = []
    ones = jnp.ones((8, LANES), F32)
    for pair in range(PAIRS):
        y_waits[pair].wait_recv()
        y_land = ref.y_land.at[pair].reshape(128 * 8, LANES)
        landed = [jnp.transpose(y_land[pl.ds(k, 128, stride=8), :]) for k in range(SLOTS)]
        landed = jnp.concatenate(landed, axis=1).astype(BF16)
        parts = [[], []]
        for half in range(2):
            s = 2 * pair + half
            pick = jnp.concatenate([hot[s * SLOTS + k] for k in range(SLOTS)], axis=0)
            grad = dot_nn(landed[half * CH : (half + 1) * CH, :], pick)
            ref.grads[s] = grad
            for kind in range(2):
                parts[kind].append(grad * ref.q_sum[s, kind])
        sums = [dot_nt(ones, jnp.concatenate(part, axis=0), HIGH)[0:1, :] for part in parts]
        k_waits.append(global_sums(8 + pair, *sums))

    scaled_grads = [ref.grads[s] * scales[:, s : s + 1] for s in range(SCENES)]
    weight_grad = jnp.zeros((CH, LANES), F32)
    for c in range(FEATS):
        product = scaled_grads[0] * ref.t_sum[0, c]
        for s in range(1, SCENES):
            product = product + scaled_grads[s] * ref.t_sum[s, c]
        weight_grad = jnp.where(lane == c, jnp.sum(product, axis=1, keepdims=True), weight_grad)
    ref.p_col[...] = weight_grad
    for i in range(n_rows):
        owner = lax.rem(row + i, n_rows)
        block = ref.p_col[pl.ds(pl.multiple_of(owner * 8, 8), 8), :]
        ref.p_send[i] = block
        if i == 0:
            ref.p_land[0] = block
    p_wait = wire.spread(
        n_rows,
        wire.row_peer,
        lambda i: ref.p_send.at[i],
        lambda i: ref.p_land.at[i],
        ref.p_land.at[pl.ds(1, n_rows - 1)],
    )
    g1_wait.wait_recv()
    block = jnp.sum(ref.g_land[...].astype(F32), axis=0).astype(BF16)
    ref.g2_send[...] = block
    ref.g2_land[0] = block
    g2_wait = wire.spread(
        n_cols,
        wire.col_peer,
        lambda i: ref.g2_send,
        lambda i: ref.g2_land.at[i],
        ref.g2_land.at[pl.ds(1, n_cols - 1)],
    )

    def update(s):
        scaled_w = w_row * norm0[s][2]
        coarse = low(scaled_w)
        matrix = jnp.where(first_half, coarse, roll64(scaled_w - coarse)).astype(BF16)
        grad = ref.grads[s]
        for j in range(DEPTH // 4):
            block = [(ref.share[s, 4 * j + t] * grad).astype(BF16) for t in range(4)]
            block = jnp.concatenate(block, axis=1)
            ref.upd[s, :, j * 4 * LANES : (j + 1) * 4 * LANES] = dot_nn(
                matrix, jnp.concatenate([block, block], axis=0)
            )

    update(0)
    update(1)
    p_wait.wait_recv()
    block = jnp.sum(ref.p_land[...], axis=0)
    ref.p2_send[...] = block
    ref.p2_land[0] = block
    p2_wait = wire.spread(
        n_cols,
        wire.col_peer,
        lambda i: ref.p2_send,
        lambda i: ref.p2_land.at[i],
        ref.p2_land.at[pl.ds(1, n_cols - 1)],
    )
    update(2)
    update(3)

    bias_sum, gain_sum = jnp.zeros((1, LANES), F32), jnp.zeros((1, LANES), F32)
    correction = jnp.zeros((16, LANES), F32)
    gain_safe = jnp.where(first_half, gain0, 1.0)
    for pair in range(PAIRS):
        k_waits[pair].wait_recv()
        sums = summed(8 + pair)
        for half in range(2):
            s = 2 * pair + half
            center, factor, scale, count, cross, products = norm0[s]
            own = jnp.where(first_half, roll64(sums) if half else sums, 0.0)
            grad_sum = own[0:1, :]
            scaled_sum = (own[1:2, :] - bias0 * grad_sum) / gain_safe
            bias_sum, gain_sum = bias_sum + grad_sum, gain_sum + scaled_sum
            grad_mean, scaled_mean = grad_sum / count, scaled_sum / count
            point_sums = products[:, 9:10]
            correction = correction + scale * (
                grad_mean * point_sums + scaled_mean * factor * (cross - center * point_sums)
            )
            unit = w_row * factor - jnp.where(feature_row == FEATS, center * factor, 0.0)
            unit = unit * scaled_mean + jnp.where(feature_row == FEATS, grad_mean, 0.0)
            mix = dot_nt(w_row * scale, unit, HIGH)
            coarse = low(mix)
            mix = jnp.concatenate([coarse, mix - coarse], axis=1).astype(BF16)
            out = ref.point_grads.at[s]
            for j in range(DEPTH // 4):
                lanes = slice(j * 4 * LANES, (j + 1) * 4 * LANES)
                points = aug[s, :, lanes]
                value = ref.upd[s, :, lanes] - dot_nn(
                    mix, jnp.concatenate([points, points], axis=0)
                )
                for t in range(4):
                    n = 4 * j + t
                    at = slice(t * LANES, (t + 1) * LANES)
                    out[pl.ds(n, 8, stride=DEPTH), :] = value[0:8, at]
                    out[8 * DEPTH + n : 8 * DEPTH + n + 1, :] = value[8:9, at]
        scenes = pl.ds(2 * pair, 2)
        outs.append(
            wire.local(ref.point_grads.at[scenes], results[1].at[scenes], out_sems, 1 + pair)
        )

    def own_lanes(values):
        return pltpu.roll(values, lax.rem(LANES - 8 * row, LANES), axis=1)

    def both_scenes(values, index):
        added = values[0][index : index + 1, :] + values[1][index : index + 1, :]
        return added + roll64(added)

    small = ref.small
    small[...] = jnp.zeros((8, LANES), F32)
    small[0:1, :] = bias_sum
    small[1:2, :] = both_scenes(total1, 0)
    small[2:3, :] = both_scenes(total2, 0)
    small[3:4, :] = gain_sum
    small[4:5, :] = both_scenes(total1, 1)
    small[5:6, :] = both_scenes(total2, 1)
    owned = own_lanes(small[...])
    ref.bias_grad[...] = owned[0:3, 0:8]
    ref.gain_grad[...] = owned[3:6, 0:8]
    outs.append(wire.local(ref.gain_grad, results[4], out_sems, 3))
    outs.append(wire.local(ref.bias_grad, results[5], out_sems, 4))
    correction = jnp.transpose(square_of(own_lanes(correction)))
    p2_wait.wait_recv()
    block = jnp.sum(ref.p2_land[...], axis=0)
    ref.pfn_grad[...] = (block - correction[0:8, :])[:, 0:FEATS]
    outs.append(wire.local(ref.pfn_grad, results[2], out_sems, 5))
    g2_wait.wait_recv()
    block = jnp.transpose(square_of(jnp.sum(ref.g2_land[...].astype(F32), axis=0)))
    ref.conv_grad[0] = block[0:CH, 0:OWN_ROWS]
    ref.conv_grad[1] = block[CH:LANES, 0:OWN_ROWS]
    outs.append(wire.local(ref.conv_grad, results[3], out_sems, 6))
    for copy in outs:
        copy.wait()
    wire.settle()


def result_kernel(*refs):
    given, results, held = refs[:RESULTS], refs[RESULTS : 2 * RESULTS], refs[2 * RESULTS : -2]
    in_sems, out_sems = refs[-2:]
    order = (1, 0, 3, 2, 4, 5)
    there = {i: pltpu.make_async_copy(given[i], held[i], in_sems.at[i]) for i in order}
    back = {i: pltpu.make_async_copy(held[i], results[i], out_sems.at[i]) for i in order}
    for i in order:
        there[i].start()
    for i in order:
        there[i].wait()
        back[i].start()
    for i in order:
        back[i].wait()


def body(points, counts, tiles, cells, pfn_weight, conv_weight, norm_gain, norm_bias, cotangent):
    scenes, feats, depth, pillars = points.shape
    n_rows, n_cols = lax.axis_size("rows"), lax.axis_size("cols")
    anywhere = pl.BlockSpec(memory_space=pl.ANY)
    shapes = [
        jax.ShapeDtypeStruct(cotangent.shape, BF16),
        jax.ShapeDtypeStruct((scenes, feats * depth, pillars), F32),
        jax.ShapeDtypeStruct(pfn_weight.shape[::-1], F32),
        jax.ShapeDtypeStruct((2, CH, OWN_ROWS), F32),
        jax.ShapeDtypeStruct(norm_gain.shape, F32),
        jax.ShapeDtypeStruct(norm_bias.shape, F32),
    ]
    results = pl.pallas_call(
        functools.partial(step_kernel, n_rows, n_cols),
        out_shape=shapes,
        in_specs=[anywhere] * INPUTS,
        out_specs=[anywhere] * RESULTS,
        scratch_shapes=[pltpu.VMEM(shape, dtype) for shape, dtype in SCRATCH.values()]
        + [
            pltpu.SemaphoreType.DMA((SEMS,)),
            pltpu.SemaphoreType.DMA((SEMS,)),
            pltpu.SemaphoreType.DMA((INPUTS,)),
            pltpu.SemaphoreType.DMA((8,)),
        ],
        compiler_params=pltpu.CompilerParams(
            collective_id=0, has_side_effects=True, vmem_limit_bytes=60 * 2**20
        ),
    )(
        points.reshape(scenes, feats * depth, pillars),
        counts,
        tiles.reshape(scenes, pillars),
        cells,
        pfn_weight.T,
        conv_weight.transpose(0, 2, 1),
        norm_gain,
        norm_bias,
        cotangent,
    )
    results = pl.pallas_call(
        result_kernel,
        out_shape=shapes,
        in_specs=[anywhere] * RESULTS,
        out_specs=[anywhere] * RESULTS,
        scratch_shapes=[pltpu.VMEM(shape.shape, shape.dtype) for shape in shapes]
        + [pltpu.SemaphoreType.DMA((RESULTS,)), pltpu.SemaphoreType.DMA((RESULTS,))],
    )(*results)
    return (
        results[0],
        results[1].reshape(points.shape),
        results[2].T,
        results[3].transpose(0, 2, 1),
        results[4],
        results[5],
    )


def solution(mesh):
    in_specs = (
        P(None, None, None, ("rows", "cols")),
        P(None, ("rows", "cols")),
        P(None, ("rows", "cols"), None),
        P(None, ("rows", "cols")),
        P(None, "rows"),
        P(None, "rows", None),
        P(None, "rows"),
        P(None, "rows"),
        P(None, "rows", "cols"),
    )
    out_specs = (
        P(None, "rows", "cols"),
        P(None, None, None, ("rows", "cols")),
        P(None, "rows"),
        P(None, "rows", None),
        P(None, "rows"),
        P(None, "rows"),
    )
    return jax.shard_map(body, mesh=mesh, in_specs=in_specs, out_specs=out_specs, check_vma=False)
```

```python
import functools
import types

import jax
import jax.numpy as jnp
from jax import lax
from jax.experimental import pallas as pl
from jax.experimental.pallas import tpu as pltpu
from jax.sharding import PartitionSpec as P

EPSILON = 1e-05
HIGH = lax.Precision.HIGHEST
MESH = pl.DeviceIdType.MESH
F32, BF16, I32 = jnp.float32, jnp.bfloat16, jnp.int32

SCENES = 4
PAIRS = 2
FEATS = 9
DEPTH = 32
PILLARS = 128
CH = 64
LANES = 128
HALF_ROWS = 32
HALF_COLS = 16
PIXELS = HALF_ROWS * HALF_COLS
SLOTS = 3
EDGE = 8
EXT_COLS = 32
EXT_ROWS = HALF_ROWS + 2
TAPS = 9
OWN_ROWS = 72
PAD_ROWS = 80


def dot_nn(a, b, precision=None):
    return lax.dot_general(
        a, b, (((1,), (0,)), ((), ())), precision=precision, preferred_element_type=F32
    )


def dot_nt(a, b, precision=None):
    return lax.dot_general(
        a, b, (((1,), (1,)), ((), ())), precision=precision, preferred_element_type=F32
    )


def dot_tn(a, b):
    return lax.dot_general(a, b, (((0,), (0,)), ((), ())), preferred_element_type=F32)


def iota(shape, dim):
    return lax.broadcasted_iota(I32, shape, dim)


def sigmoid(v):
    return 0.5 * jnp.tanh(0.5 * v) + 0.5


def low(v):
    return v.astype(BF16).astype(F32)


def one_hot(mask):
    return jnp.where(mask, 1.0, 0.0).astype(BF16)


def square_of(v):
    rows, cols = v.shape
    if cols < LANES:
        v = jnp.concatenate([v, jnp.zeros((rows, LANES - cols), v.dtype)], axis=1)
    return jnp.concatenate([v, jnp.zeros((LANES - rows, LANES), v.dtype)], axis=0)


def roll64(v):
    return pltpu.roll(v, CH, axis=1)


SCRATCH = dict(
    points=((SCENES, FEATS * DEPTH, LANES), BF16),
    counts=((SCENES, LANES), I32),
    tiles=((SCENES, LANES), I32),
    cells=((SCENES, LANES), I32),
    pfn=((8, FEATS), BF16),
    conv=((2, CH, OWN_ROWS), BF16),
    gain=((3, 8), BF16),
    bias=((3, 8), BF16),
    cotangent=((SCENES, HALF_ROWS, HALF_COLS * CH), BF16),
    square=((LANES, LANES), F32),
    w_tmp=((16, LANES), F32),
    w_send=((16, LANES), F32),
    w_land=((8, 16, LANES), F32),
    c_send=((PAD_ROWS, LANES), BF16),
    c_land=((8, PAD_ROWS, LANES), BF16),
    taps=((TAPS * CH, LANES), F32),
    wide1=((TAPS * LANES, LANES), BF16),
    side1=((3 * LANES, LANES), BF16),
    wide2=((TAPS * LANES, LANES), BF16),
    back2=((TAPS * LANES, LANES), BF16),
    back1=((4 * LANES, 4 * LANES), BF16),
    pts32=((SCENES, 16 * DEPTH, LANES), F32),
    aug=((SCENES, 16, DEPTH * LANES), BF16),
    hot=((SCENES * SLOTS, LANES, LANES), BF16),
    m_send=((2, 4, LANES), F32),
    m_land=((8, 4, LANES), F32),
    m2_land=((16, 4, LANES), F32),
    hello=((4, 4, LANES), F32),
    spots=((LANES, LANES), F32),
    cell_send=((8, 16, LANES), F32),
    cell_land=((8, 16, LANES), F32),
    cell2_send=((16, 8, LANES), F32),
    cell2_land=((16, 8, LANES), F32),
    gram=((SCENES, 16, LANES), F32),
    place=((PAIRS, PIXELS, 6 * LANES), BF16),
    rim=((PAIRS, 48, 6 * LANES), BF16),
    parity=((PAIRS, 6 * LANES, 4 * LANES), BF16),
    fetch=((PAIRS, 6 * LANES, PIXELS), BF16),
    pre=((SCENES, DEPTH, CH, LANES), F32),
    act=((SCENES, DEPTH, CH, LANES), F32),
    share=((SCENES, DEPTH, CH, LANES), F32),
    pil=((SCENES, CH, LANES), F32),
    t_sum=((SCENES, FEATS, CH, LANES), F32),
    q_sum=((SCENES, 2, CH, LANES), F32),
    x_send=((PAIRS, 128, 8, LANES), F32),
    x_land=((PAIRS, 128, 8, LANES), F32),
    y_send=((PAIRS, 128, 8, LANES), F32),
    y_land=((PAIRS, 128, 8, LANES), F32),
    rim_send=((PAIRS, 2, 48, LANES), F32),
    rim_land=((PAIRS, 2, 56, LANES), F32),
    im1=((PAIRS, PIXELS, TAPS * LANES), BF16),
    top1=((PAIRS, 16, 3 * LANES), BF16),
    left1=((PAIRS, 32, 3 * LANES), BF16),
    im2=((PAIRS, PIXELS, TAPS * LANES), BF16),
    y1=((PAIRS, PIXELS, LANES), F32),
    y2=((PAIRS, PIXELS, LANES), F32),
    x1=((PAIRS, PIXELS, LANES), F32),
    x2=((PAIRS, PIXELS, LANES), F32),
    s1=((PAIRS, PIXELS, LANES), F32),
    g1=((PAIRS, PIXELS, LANES), F32),
    g2=((PAIRS, PIXELS, LANES), F32),
    feat=((PAIRS, PIXELS, LANES), F32),
    cot=((PAIRS, PIXELS, LANES), F32),
    d1=((PAIRS, PIXELS, LANES), F32),
    d2=((PAIRS, PIXELS, LANES), BF16),
    cols=((4, PAIRS, 2, HALF_ROWS, LANES), F32),
    halo=((4, PAIRS, LANES, LANES), F32),
    ext=((3, PAIRS, EXT_ROWS * EXT_COLS, LANES), F32),
    st_send=((10, 2, LANES), F32),
    st_land=((10, 128, 2, LANES), F32),
    grads=((SCENES, CH, LANES), F32),
    p_col=((CH, LANES), F32),
    p_send=((8, 8, LANES), F32),
    p_land=((8, 8, LANES), F32),
    p2_send=((8, LANES), F32),
    p2_land=((16, 8, LANES), F32),
    dk=((TAPS * CH, LANES), F32),
    g_send=((8, PAD_ROWS, LANES), BF16),
    g_land=((8, PAD_ROWS, LANES), BF16),
    g2_send=((PAD_ROWS, LANES), BF16),
    g2_land=((16, PAD_ROWS, LANES), BF16),
    upd=((SCENES, 16, DEPTH * LANES), F32),
    small=((8, LANES), F32),
)
INPUTS = 9
RESULTS = 6
SEMS = 96


HIGH_BITS, LOW_BITS = 0b1010101, 0b0101010


def digits_add(a, b):
    carried = jnp.bitwise_and(a, LOW_BITS) + jnp.bitwise_and(b, LOW_BITS)
    return jnp.bitwise_xor(carried, jnp.bitwise_and(jnp.bitwise_xor(a, b), HIGH_BITS))


def digits_sub(a, b):
    borrowed = jnp.bitwise_or(a, HIGH_BITS) - jnp.bitwise_and(b, LOW_BITS)
    kept = jnp.bitwise_and(jnp.bitwise_xor(jnp.bitwise_xor(a, b), HIGH_BITS), HIGH_BITS)
    return jnp.bitwise_xor(borrowed, kept)


def far_first(step):
    return jnp.bitwise_xor(step, jnp.bitwise_and(jnp.right_shift(step, 1), LOW_BITS))


class Wire:
    def __init__(self, n_rows, n_cols, send_sems, recv_sems):
        self.n_rows, self.n_cols = n_rows, n_cols
        self.total = n_rows * n_cols
        self.row, self.col = lax.axis_index("rows"), lax.axis_index("cols")
        self.me = self.col * n_rows + self.row
        self.send_sems, self.recv_sems = send_sems, recv_sems
        self.used = 0
        self.sent = []

    def place(self, number):
        return (
            jnp.bitwise_and(number, self.n_rows - 1),
            jnp.right_shift(number, self.n_rows.bit_length() - 1),
        )

    def peer(self, step):
        return self.place(digits_add(self.me, step))

    def source(self, step):
        return self.place(digits_sub(self.me, step))

    def along_cols(self, step):
        return self.peer(step * self.n_rows)

    def near(self, down, right):
        return (
            lax.rem(self.row + down + self.n_rows, self.n_rows),
            lax.rem(self.col + right + self.n_cols, self.n_cols),
        )

    def copy(self, src, dst, sem, peer):
        return pltpu.make_async_remote_copy(
            src_ref=src,
            dst_ref=dst,
            send_sem=self.send_sems.at[sem],
            recv_sem=self.recv_sems.at[sem],
            device_id=peer,
            device_id_type=MESH,
        )

    def one(self, src, dst, peer):
        sem = self.used
        self.used += 1
        copy = self.copy(src, dst, sem, peer)
        copy.start()
        self.sent.append(copy)
        return copy

    def spread(self, count, peer_of, src_of, dst_of, whole):
        sem = self.used
        self.used += 1

        def step(j, carry):
            i = far_first(count - j)
            self.copy(src_of(i), dst_of(i), sem, peer_of(i)).start()
            return carry

        lax.fori_loop(1, count, step, 0, unroll=8)
        copy = self.copy(whole, whole, sem, peer_of(1))
        self.sent.append(copy)
        return copy

    def local(self, src, dst, sems, index):
        copy = pltpu.make_async_copy(src, dst, sems.at[index])
        copy.start()
        return copy

    def settle(self):
        for copy in self.sent:
            copy.wait_send()


def step_kernel(n_rows, n_cols, *refs):
    inputs, results = refs[:INPUTS], refs[INPUTS : INPUTS + RESULTS]
    ref = types.SimpleNamespace(**dict(zip(SCRATCH, refs[INPUTS + RESULTS :], strict=False)))
    ref.features, ref.point_grads, ref.pfn_grad, ref.conv_grad, ref.gain_grad, ref.bias_grad = results
    send_sems, recv_sems, in_sems = refs[-3:]
    wire = Wire(n_rows, n_cols, send_sems, recv_sems)
    total, row, col, me = wire.total, wire.row, wire.col, wire.me
    lane = iota((1, LANES), 1)
    first_half = lane < CH

    held = [
        ref.points, ref.counts, ref.tiles, ref.cells, ref.pfn, ref.conv, ref.gain, ref.bias,
        ref.cotangent,
    ]
    order = [1, 0, 2, 3, 4, 6, 7, 5, 8]
    loads = {i: wire.local(inputs[i], held[i], in_sems, i) for i in order}
    barrier = pltpu.get_barrier_semaphore()

    lines = [i for i in range(1, n_rows)] + [i * 8 for i in (1, 2, 3)] + [i * 32 for i in (1, 2, 3)]
    for step in lines:
        pl.semaphore_signal(barrier, inc=1, device_id=wire.peer(step), device_id_type=MESH)

    for i in range(INPUTS):
        loads[i].wait()
    pts32, aug = ref.pts32, ref.aug
    slot_number = iota((DEPTH, LANES), 0)
    for s in range(SCENES):
        valid = slot_number < ref.counts[s : s + 1, :]
        for c in range(FEATS):
            block = ref.points[s, c * DEPTH : (c + 1) * DEPTH, :].astype(F32)
            pts32[s, c * DEPTH : (c + 1) * DEPTH, :] = jnp.where(valid, block, 0.0)
        pts32[s, FEATS * DEPTH : (FEATS + 1) * DEPTH, :] = jnp.where(valid, 1.0, 0.0)
        pts32[s, (FEATS + 1) * DEPTH :, :] = jnp.zeros((6 * DEPTH, LANES), F32)
        scene_pts = pts32.at[s]
        for n in range(DEPTH):
            aug[s, :, n * LANES : (n + 1) * LANES] = scene_pts[pl.ds(n, 16, stride=DEPTH), :].astype(
                BF16
            )
    stacked = jnp.concatenate([aug[s] for s in range(SCENES)], axis=0)
    gram_all = dot_nt(stacked, jnp.concatenate([stacked, stacked], axis=0))
    moments = jnp.zeros((4, LANES), F32)
    for s in range(SCENES):
        for b in range(3):
            piece = gram_all[16 * s + 4 * b : 16 * s + 4 * b + 4, :]
            at = 40 * b + 10 * s
            piece = pltpu.roll(piece, (at - 16 * s) % LANES, axis=1)
            moments = moments + jnp.where((lane >= at) & (lane < at + 10), piece, 0.0)

    hot = ref.hot
    above = iota((LANES, LANES), 0) < iota((LANES, LANES), 1)
    slot_row = iota((LANES, LANES), 0).astype(F32) * 4.0
    for s in range(SCENES):
        tile = ref.tiles[s : s + 1, :]
        tile = jnp.bitwise_and(tile, n_cols - 1) * n_rows + jnp.right_shift(
            tile, n_cols.bit_length() - 1
        )
        tile = digits_sub(tile, me).astype(F32)
        wide = jnp.broadcast_to(tile, (LANES, LANES))
        same = (jnp.transpose(wide) == wide) & above
        rank = jnp.sum(jnp.where(same, 1.0, 0.0), axis=0, keepdims=True)
        code = tile * 4.0 + rank
        for k in range(SLOTS):
            hot[s * SLOTS + k] = one_hot(slot_row + float(k) == code)

    lane_row = iota((LANES, LANES), 0)
    spots = jnp.zeros((LANES, LANES), F32)
    for q in range(4):
        for pair in range(PAIRS):
            s = 2 * pair + q // 2
            cell = ref.cells[s : s + 1, :]
            spot = (jnp.bitwise_and(cell, 31) if q % 2 else jnp.right_shift(cell, 5)) + 1
            for k in range(SLOTS):
                at = jnp.where(lane_row == q * 8 + 3 * pair + k, spot.astype(F32), 0.0)
                spots = spots + dot_nt(hot[s * SLOTS + k], at.astype(BF16))
    ref.spots[...] = spots
    for i in range(n_rows):
        ref.cell_send[i] = ref.spots[pl.ds(i, n_cols, stride=n_rows), :]
    ref.cell_land[0] = ref.cell_send[0]
    ref.m_send[0] = moments
    ref.m_land[0] = moments
    ref.hello[0] = moments

    ref.square[...] = jnp.zeros((LANES, LANES), F32)
    ref.square[0:8, 0:FEATS] = ref.pfn[...].astype(F32)
    ref.w_tmp[...] = jnp.transpose(ref.square[...])[0:16, :]
    ref.w_tmp[9:12, 0:8] = ref.gain[...].astype(F32)
    ref.w_tmp[12:15, 0:8] = ref.bias[...].astype(F32)
    ref.w_send[...] = pltpu.roll(ref.w_tmp[...], row * 8, axis=1)
    ref.w_land[0] = ref.w_send[...]
    pl.semaphore_wait(barrier, len(lines))
    m_wait = wire.spread(
        n_rows,
        wire.peer,
        lambda i: ref.m_send.at[0],
        lambda i: ref.m_land.at[i],
        ref.m_land.at[pl.ds(1, n_rows - 1)],
    )
    hello_wait = wire.spread(
        4,
        lambda i: wire.peer(i * 8),
        lambda i: ref.hello.at[0],
        lambda i: ref.hello.at[i],
        ref.hello.at[pl.ds(1, 3)],
    )
    w_wait = wire.spread(
        n_rows,
        wire.peer,
        lambda i: ref.w_send,
        lambda i: ref.w_land.at[i],
        ref.w_land.at[pl.ds(1, n_rows - 1)],
    )
    cell_wait = wire.spread(
        n_rows,
        wire.peer,
        lambda i: ref.cell_send.at[i],
        lambda i: ref.cell_land.at[i],
        ref.cell_land.at[pl.ds(1, n_rows - 1)],
    )
    m_wait.wait_recv()
    hello_wait.wait_recv()
    moments = jnp.sum(ref.m_land[...], axis=0)
    ref.m_send[1] = moments
    ref.m2_land[0] = moments
    m2_wait = wire.spread(
        n_cols,
        wire.along_cols,
        lambda i: ref.m_send.at[1],
        lambda i: ref.m2_land.at[i],
        ref.m2_land.at[pl.ds(1, n_cols - 1)],
    )

    def halo_send(values, index, pair, full):
        cols, halo = ref.cols.at[index, pair], ref.halo.at[index, pair]
        inner = values.at[pair]
        for side in range(2 if full else 1):
            cols[side] = inner[pl.ds(side * (HALF_COLS - 1), HALF_ROWS, stride=HALF_COLS), :]

        def send(src, start, count, at, down, right):
            return wire.one(
                src.at[pl.ds(start, count)], halo.at[pl.ds(at, count)], wire.near(down, right)
            )

        waits = [
            send(inner, 0, 8, 120, -1, -1),
            send(cols.at[0], 0, 32, 64, 0, -1),
            send(inner, 0, 16, 16, -1, 0),
        ]
        if full:
            waits += [
                send(inner, 504, 8, 96, 1, 1),
                send(inner, 8, 8, 112, -1, 1),
                send(inner, 496, 8, 104, 1, -1),
                send(cols.at[1], 0, 32, 32, 0, 1),
                send(inner, 496, 16, 0, 1, 0),
            ]
        return waits

    def there(cond):
        return jnp.where(cond, 1.0, 0.0)

    up, down = there(row > 0), there(row < n_rows - 1)
    left, right = there(col > 0), there(col < n_cols - 1)
    spot = iota((LANES, LANES), 0)
    halo_mask = jnp.where(spot < 16, up, jnp.where(spot < 32, down, jnp.where(spot < 64, left, right)))
    halo_mask = jnp.where(spot < 96, halo_mask, jnp.where(spot < 112, up, down))
    halo_mask = jnp.where(
        spot < 96,
        halo_mask,
        halo_mask * jnp.where((spot < 104) | ((spot >= 112) & (spot < 120)), left, right),
    )

    def fill_ext(index, pair, inner, edge):
        grid = ref.ext.at[index, pair]
        for i in range(HALF_ROWS):
            at = (i + 1) * EXT_COLS + EDGE
            grid[at : at + HALF_COLS, :] = inner[i * HALF_COLS : (i + 1) * HALF_COLS, :]
        grid[EDGE : EDGE + HALF_COLS, :] = edge[0:16, :]
        last = (EXT_ROWS - 1) * EXT_COLS
        grid[last + EDGE : last + EDGE + HALF_COLS, :] = edge[16:32, :]
        grid[pl.ds(EXT_COLS + EDGE - 1, HALF_ROWS, stride=EXT_COLS), :] = edge[32:64, :]
        grid[pl.ds(EXT_COLS + EDGE + HALF_COLS, HALF_ROWS, stride=EXT_COLS), :] = edge[64:96, :]
        grid[EDGE - 1 : EDGE, :] = edge[103:104, :]
        grid[EDGE + HALF_COLS : EDGE + HALF_COLS + 1, :] = edge[104:105, :]
        grid[last + EDGE - 1 : last + EDGE, :] = edge[119:120, :]
        grid[last + EDGE + HALF_COLS : last + EDGE + HALF_COLS + 1, :] = edge[120:121, :]

    def shifted(index, pair, shift, rows):
        grid = ref.ext.at[index, pair]
        start = EDGE - 1 + shift
        return [
            grid[i * EXT_COLS + start : i * EXT_COLS + start + HALF_COLS, :].astype(BF16)
            for i in rows
        ]

    def column_sum(v):
        return jnp.sum(v, axis=0, keepdims=True)

    def global_sums(index, first, second):
        send, land = ref.st_send.at[index], ref.st_land.at[index]
        send[0:1, :] = first
        send[1:2, :] = second
        land[0] = send[...]
        return wire.spread(
            total,
            wire.peer,
            lambda i: send,
            lambda i: land.at[i],
            land.at[pl.ds(1, total - 1)],
        )

    def summed(index):
        return jnp.sum(ref.st_land[index], axis=0)

    pixel_total = float(PIXELS * total)

    def norm_of(sums):
        center = sums[0:1, :] / pixel_total
        spread = sums[1:2, :] / pixel_total - center * center
        return center, lax.rsqrt(spread + EPSILON)

    cot = ref.cot
    for pair in range(PAIRS):
        spread_to = cot.at[pair]
        for m in range(HALF_COLS // 2):
            a = ref.cotangent[2 * pair, :, m * LANES : (m + 1) * LANES].astype(F32)
            b = ref.cotangent[2 * pair + 1, :, m * LANES : (m + 1) * LANES].astype(F32)
            spread_to[pl.ds(2 * m, HALF_ROWS, stride=HALF_COLS), :] = jnp.where(
                first_half, a, roll64(b)
            )
            spread_to[pl.ds(2 * m + 1, HALF_ROWS, stride=HALF_COLS), :] = jnp.where(
                first_half, roll64(a), b
            )
    ref.square[:, 0:OWN_ROWS] = jnp.concatenate(
        [ref.conv[0].astype(F32), ref.conv[1].astype(F32)], axis=0
    )
    ref.c_send[...] = jnp.transpose(ref.square[...])[0:PAD_ROWS, :].astype(BF16)
    ref.c_land[0] = ref.c_send[...]
    cell_wait.wait_recv()
    cell_land = ref.cell_land.reshape(n_rows * n_cols, LANES)
    for i in range(n_cols):
        ref.cell2_send[i] = cell_land[pl.ds(i, n_rows, stride=n_cols), :]
    ref.cell2_land[0] = ref.cell2_send[0]
    cell2_wait = wire.spread(
        n_cols,
        wire.along_cols,
        lambda i: ref.cell2_send.at[i],
        lambda i: ref.cell2_land.at[i],
        ref.cell2_land.at[pl.ds(1, n_cols - 1)],
    )
    w_wait.wait_recv()
    m2_wait.wait_recv()

    c_wait = wire.spread(
        n_rows,
        wire.peer,
        lambda i: ref.c_send,
        lambda i: ref.c_land.at[i],
        ref.c_land.at[pl.ds(1, n_rows - 1)],
    )
    cot_waits = [wait for pair in range(PAIRS) for wait in halo_send(cot, 0, pair, True)]
    w_full = jnp.sum(ref.w_land[...], axis=0)
    feature_row = iota((16, LANES), 0)
    w_row = jnp.where(feature_row < FEATS, w_full, 0.0)

    def twice(v):
        return v + roll64(v)

    gain0, bias0 = w_full[9:10, :], w_full[12:13, :]
    gain1, bias1 = twice(w_full[10:11, :]), twice(w_full[13:14, :])
    gain2, bias2 = twice(w_full[11:12, :]), twice(w_full[14:15, :])
    moments = jnp.sum(ref.m2_land[...], axis=0)
    gram = ref.gram
    norm0, matrices = [], []
    for s in range(SCENES):
        gram[s] = jnp.zeros((16, LANES), F32)
        for b in range(3):
            piece = pltpu.roll(moments, (LANES - 40 * b - 10 * s) % LANES, axis=1)
            gram[s, 4 * b : 4 * b + 4, :] = jnp.where(lane < 10, piece, 0.0)
    for s in range(SCENES):
        products = gram[s]
        cross = dot_nn(products[:, 0:16], w_row, HIGH)
        count = products[9:10, 9:10]
        center = cross[9:10, :] / count
        spread = column_sum(w_row * cross) / count - center * center
        factor = lax.rsqrt(spread + EPSILON)
        scale = factor * gain0
        norm0.append((center, factor, scale, count, cross, products))
        folded = w_row * scale + jnp.where(feature_row == FEATS, bias0 - center * scale, 0.0)
        coarse = low(folded)
        both = square_of(jnp.concatenate([coarse, low(folded - coarse)], axis=0))
        matrices.append(jnp.transpose(both)[0:CH, 0:32].astype(BF16))

    STEP = 8
    x_waits = []
    for pair in range(PAIRS):
        for s in (2 * pair, 2 * pair + 1):
            bound = ref.counts[s : s + 1, :]
            matrix = matrices[s]

            peak = jnp.full((CH, LANES), -1e30, F32)
            for j in range(DEPTH // STEP):
                points = aug[s, :, j * STEP * LANES : (j + 1) * STEP * LANES]
                value = dot_nn(matrix, jnp.concatenate([points, points], axis=0))
                for t in range(STEP):
                    n = STEP * j + t
                    pre = value[:, t * LANES : (t + 1) * LANES]
                    active = jnp.where(n < bound, pre * sigmoid(pre), -1e30)
                    ref.pre[s, n] = pre
                    ref.act[s, n] = active
                    peak = jnp.maximum(peak, active)
            whole = jnp.zeros((CH, LANES), F32)
            for n in range(DEPTH):
                whole = whole + jnp.exp(ref.act[s, n] - peak)
            ref.pil[s] = peak + jnp.log(whole)
        x_send = ref.x_send.at[pair].reshape(128 * 8, LANES)
        a, b = ref.pil[2 * pair].astype(BF16), ref.pil[2 * pair + 1].astype(BF16)
        none = jnp.zeros((CH, LANES), BF16)
        both = jnp.concatenate(
            [jnp.concatenate([a, none], axis=1), jnp.concatenate([none, b], axis=1)], axis=0
        )
        for k in range(SLOTS):
            pick = jnp.concatenate(
                [hot[2 * pair * SLOTS + k], hot[(2 * pair + 1) * SLOTS + k]], axis=1
            )
            x_send[pl.ds(k, 128, stride=8), :] = dot_nt(pick, both)
        ref.x_land[pair, 0, 0:SLOTS, :] = ref.x_send[pair, 0, 0:SLOTS, :]
        x_waits.append(
            wire.spread(
                total,
                wire.peer,
                lambda i, pair=pair: ref.x_send.at[pair, i, pl.ds(0, SLOTS)],
                lambda i, pair=pair: ref.x_land.at[pair, i, pl.ds(0, SLOTS)],
                ref.x_land.at[pair, pl.ds(1, total - 1), pl.ds(0, SLOTS)],
            )
        )

    cell2_wait.wait_recv()
    along_all = ref.cell2_land[...].reshape(LANES, LANES)
    across_all = jnp.transpose(along_all)
    place, rim, parity, fetch = ref.place, ref.rim, ref.parity, ref.fetch

    def pixel_of(tall, wide):
        i, j = tall.astype(I32) - 1, wide.astype(I32) - 1
        pixel = jnp.right_shift(i, 1) * HALF_COLS + jnp.right_shift(j, 1)
        plane = 2 * jnp.bitwise_and(i, 1) + jnp.bitwise_and(j, 1)
        return jnp.where(i < 0, -1, pixel), jnp.where(i < 0, -1, plane)

    rim_pixel = iota((48, LANES), 0)
    rim_pixel = jnp.where(rim_pixel < 16, 496 + rim_pixel, rim_pixel * 16 - 241)
    for pair in range(PAIRS):
        for half in range(2):
            for k in range(SLOTS):
                at = 16 * half + 3 * pair + k
                block = (half * SLOTS + k) * LANES
                blocks = slice(block, block + LANES)
                across, _ = pixel_of(across_all[at : at + 1, :], across_all[at + 8 : at + 9, :])
                _, along = pixel_of(along_all[:, at : at + 1], along_all[:, at + 8 : at + 9])
                along = jnp.broadcast_to(along, (LANES, LANES))
                for m in range(4):
                    tile = slice(m * LANES, (m + 1) * LANES)
                    place[pair, tile, blocks] = one_hot(
                        iota((LANES, LANES), 0) + m * LANES == across
                    )
                    parity[pair, blocks, tile] = one_hot(along == m)
                rim[pair, :, blocks] = one_hot(rim_pixel == across)

    c_wait.wait_recv()
    taps = ref.taps
    for i in range(n_rows):
        owner = wire.source(i)[0]
        taps[pl.ds(pl.multiple_of(owner * OWN_ROWS, 8), OWN_ROWS), :] = ref.c_land[i].astype(F32)[
            0:OWN_ROWS, :
        ]
    ref.back1[...] = jnp.zeros((4 * LANES, 4 * LANES), BF16)
    for t in range(TAPS):
        both = taps[t * CH : (t + 1) * CH, :]
        swapped = roll64(both)
        at = t * LANES
        k1 = jnp.concatenate(
            [jnp.where(first_half, both, 0.0), jnp.where(first_half, 0.0, swapped)], axis=0
        )
        k2 = jnp.concatenate(
            [jnp.where(first_half, swapped, 0.0), jnp.where(first_half, 0.0, both)], axis=0
        )
        ref.wide1[at : at + LANES, :] = k1.astype(BF16)
        if t % 3 == 0:
            ref.side1[t // 3 * LANES : (t // 3 + 1) * LANES, :] = k1.astype(BF16)
        ref.wide2[at : at + LANES, :] = k2.astype(BF16)
        ref.back2[at : at + LANES, :] = jnp.transpose(k2).astype(BF16)
        a, b = t // 3, t % 3
        window = 2 * (a == 0) + (b == 0)
        plane = 2 * (a != 1) + (b != 1)
        ref.back1[
            window * LANES : (window + 1) * LANES, plane * LANES : (plane + 1) * LANES
        ] = jnp.transpose(k1).astype(BF16)

    planes_of, d_waits = [], []
    for pair in range(PAIRS):
        x_waits[pair].wait_recv()
        x_land = ref.x_land.at[pair].reshape(128 * 8, LANES)
        landed = [x_land[pl.ds(k, 128, stride=8), :] for k in range(SLOTS)]
        values = [jnp.where(first_half, v, 0.0) for v in landed]
        values += [jnp.where(first_half, 0.0, v) for v in landed]
        values = jnp.concatenate(values, axis=0).astype(BF16)
        values = jnp.concatenate([values] * 4, axis=1) * parity[pair]
        planes_of.append(values)
        edge = low(dot_nn(rim[pair], values))
        rim_send, rim_land = ref.rim_send.at[pair], ref.rim_land.at[pair]
        rim_send[0, 0:16, :] = edge[0:16, 2 * LANES : 3 * LANES]
        rim_send[1, 0:16, :] = edge[0:16, 3 * LANES :]
        rim_send[0, 16:48, :] = edge[16:48, LANES : 2 * LANES]
        rim_send[1, 16:48, :] = edge[16:48, 3 * LANES :]
        d_waits.append(
            [
                wire.one(rim_send.at[1, pl.ds(40, 8)], rim_land.at[0, pl.ds(48, 8)], wire.near(1, 1)),
                wire.one(
                    rim_send.at[:, pl.ds(16, 32)], rim_land.at[:, pl.ds(16, 32)], wire.near(0, 1)
                ),
                wire.one(rim_send.at[:, pl.ds(0, 16)], rim_land.at[:, pl.ds(0, 16)], wire.near(1, 0)),
            ]
        )

    y1 = ref.y1
    first_col = jnp.bitwise_and(iota((PIXELS, LANES), 0), HALF_COLS - 1) == 0
    no_row = jnp.zeros((HALF_COLS, LANES), BF16)
    for pair in range(PAIRS):
        grid = low(dot_nn(place[pair], planes_of[pair]))
        still = [grid[:, q * LANES : (q + 1) * LANES] for q in range(4)]
        moved = {q: jnp.where(first_col, 0.0, pltpu.roll(still[q], 1, axis=0)) for q in (1, 3)}
        for t in range(TAPS):
            a, b = t // 3, t % 3
            plane = 2 * (a != 1) + (b != 1)
            window = (moved[plane] if b == 0 else still[plane]).astype(BF16)
            if a == 0:
                window = jnp.concatenate([no_row, window[: PIXELS - HALF_COLS, :]], axis=0)
            ref.im1[pair, :, t * LANES : (t + 1) * LANES] = window
        y1[pair] = dot_nn(ref.im1[pair], ref.wide1[...])

    e_waits, e_edges = [], []
    for pair in range(PAIRS):
        for wait in d_waits[pair]:
            wait.wait_recv()
        rim_land = ref.rim_land.at[pair]
        rows_in = [rim_land[p, 0:16, :] * up for p in range(2)]
        cols_in = [rim_land[p, 16:48, :] * left for p in range(2)]
        corner = rim_land[0, 55:56, :] * (up * left)
        top = [
            jnp.where(iota((16, LANES), 0) == 0, corner, pltpu.roll(rows_in[1], 1, axis=0)),
            rows_in[0],
            rows_in[1],
        ]
        side = [
            jnp.where(iota((32, LANES), 0) == 0, 0.0, pltpu.roll(cols_in[1], 1, axis=0)),
            cols_in[0],
            cols_in[1],
        ]
        ref.top1[pair] = jnp.concatenate(top, axis=1).astype(BF16)
        ref.left1[pair] = jnp.concatenate(side, axis=1).astype(BF16)
        y1[pair, 0:16, :] += dot_nn(ref.top1[pair], ref.wide1[0 : 3 * LANES, :])
        beside = pl.ds(0, HALF_ROWS, stride=HALF_COLS)
        y1.at[pair][beside, :] += dot_nn(ref.left1[pair], ref.side1[...])
        value = y1[pair]
        e_waits.append(global_sums(pair, column_sum(value), column_sum(value * value)))
        e_edges.append(halo_send(y1, 1, pair, True))

    for pair in range(PAIRS):
        for half in range(2):
            for k in range(SLOTS):
                at = 16 * half + 3 * pair + k
                block = (half * SLOTS + k) * LANES
                along, _ = pixel_of(along_all[:, at : at + 1], along_all[:, at + 8 : at + 9])
                along = jnp.broadcast_to(along, (LANES, LANES))
                for m in range(4):
                    fetch[pair, block : block + LANES, m * LANES : (m + 1) * LANES] = one_hot(
                        iota((LANES, LANES), 1) + m * LANES == along
                    )
    for wait in cot_waits:
        wait.wait_recv()

    norm1, f_waits, f_edges = [], [], []
    y2 = ref.y2
    for pair in range(PAIRS):
        e_waits[pair].wait_recv()
        for wait in e_edges[pair]:
            wait.wait_recv()
        center, factor = norm_of(summed(pair))
        norm1.append((center, factor))
        scaled = (y1[pair] - center) * factor
        pre = scaled * gain1 + bias1
        sigma = sigmoid(pre)
        edge = (ref.halo[1, pair] - center) * factor * gain1 + bias1
        fill_ext(0, pair, low(pre * sigma), low(edge * sigmoid(edge)) * halo_mask)
        for b in range(3):
            window = shifted(0, pair, b, range(EXT_ROWS))
            for a in range(3):
                t = 3 * a + b
                ref.im2[pair, :, t * LANES : (t + 1) * LANES] = jnp.concatenate(
                    window[a : a + HALF_ROWS], axis=0
                )
        value = dot_nn(ref.im2[pair], ref.wide2[...])
        y2[pair] = value
        f_waits.append(global_sums(2 + pair, column_sum(value), column_sum(value * value)))
        f_edges.append(halo_send(y2, 2, pair, True))
        ref.x1[pair] = scaled
        ref.s1[pair] = sigma * (1.0 + pre * (1.0 - sigma))

    def slopes(step, carry):
        s, block = step // 4, lax.rem(step, 4)
        rows = pl.ds(pl.multiple_of(block * 16, 16), 16)
        top = ref.pil[s, rows, :]

        def inner(j, sums):
            sums = list(sums)
            for t in range(2):
                n = 2 * j + t
                pre, active = ref.pre[s, n, rows, :], ref.act[s, n, rows, :]
                sigma = sigmoid(pre)
                share = jnp.exp(active - top) * (sigma + active * (1.0 - sigma))
                ref.share[s, n, rows, :] = share
                sums[0] = sums[0] + share
                sums[1] = sums[1] + share * pre
                for c in range(FEATS):
                    sums[2 + c] = sums[2 + c] + share * pts32[s, pl.ds(c * DEPTH + n, 1), :]
            return tuple(sums)

        zero = jnp.zeros((16, LANES), F32)
        sums = lax.fori_loop(0, DEPTH // 2, inner, (zero,) * (2 + FEATS))
        ref.q_sum[s, 0, rows, :] = sums[0]
        ref.q_sum[s, 1, rows, :] = sums[1]
        for c in range(FEATS):
            ref.t_sum[s, c, rows, :] = sums[2 + c]
        return carry

    lax.fori_loop(0, 2 * SCENES, slopes, 0)

    norm2, g_waits = [], []
    for pair in range(PAIRS):
        f_waits[pair].wait_recv()
        center, factor = norm_of(summed(2 + pair))
        norm2.append((center, factor))
        scaled = (y2[pair] - center) * factor
        pre = scaled * gain2 + bias2
        sigma = sigmoid(pre)
        grad = cot[pair] * (sigma * (1.0 + pre * (1.0 - sigma)))
        g_waits.append(global_sums(4 + pair, column_sum(grad), column_sum(grad * scaled)))
        ref.x2[pair] = scaled
        ref.g2[pair] = grad
        ref.feat[pair] = pre * sigma

    for pair in range(PAIRS):
        grid = ref.feat.at[pair]
        for m in range(HALF_COLS // 2):
            a = grid[pl.ds(2 * m, HALF_ROWS, stride=HALF_COLS), :]
            b = grid[pl.ds(2 * m + 1, HALF_ROWS, stride=HALF_COLS), :]
            at = slice(m * LANES, (m + 1) * LANES)
            ref.features[2 * pair, :, at] = jnp.where(first_half, a, roll64(b)).astype(BF16)
            ref.features[2 * pair + 1, :, at] = jnp.where(first_half, roll64(a), b).astype(BF16)
    edges2 = []
    for pair in range(PAIRS):
        for wait in f_edges[pair]:
            wait.wait_recv()
        center, factor = norm2[pair]
        scaled = (ref.halo[2, pair] - center) * factor
        pre = scaled * gain2 + bias2
        sigma = sigmoid(pre)
        edges2.append((scaled, ref.halo[0, pair] * (sigma * (1.0 + pre * (1.0 - sigma)))))
    lax.fori_loop(2 * SCENES, 4 * SCENES, slopes, 0)

    total2, h_waits, h_edges = [], [], []
    for pair in range(PAIRS):
        g_waits[pair].wait_recv()
        sums = summed(4 + pair)
        total2.append(sums)
        scale = norm2[pair][1] * gain2
        mean_grad, mean_scaled = sums[0:1, :] / pixel_total, sums[1:2, :] / pixel_total
        inner = low(scale * (ref.g2[pair] - mean_grad - ref.x2[pair] * mean_scaled))
        edge_scaled, edge_grad = edges2[pair]
        edge = low(scale * (edge_grad - mean_grad - edge_scaled * mean_scaled)) * halo_mask
        ref.d2[pair] = inner.astype(BF16)
        fill_ext(1, pair, inner, edge)
        blocks = [None] * TAPS
        for b in range(3):
            window = shifted(1, pair, 2 - b, range(EXT_ROWS))
            for a in range(3):
                blocks[3 * a + b] = jnp.concatenate(window[2 - a : 2 - a + HALF_ROWS], axis=0)
        grad = dot_nn(jnp.concatenate(blocks, axis=1), ref.back2[...]) * ref.s1[pair]
        ref.g1[pair] = grad
        h_waits.append(global_sums(6 + pair, column_sum(grad), column_sum(grad * ref.x1[pair])))
        h_edges.append(halo_send(ref.g1, 3, pair, False))

    def both_halves(product):
        return product[0:CH, :] + roll64(product[CH:LANES, :])

    dk = ref.dk
    for t in range(TAPS):
        tap = slice(t * LANES, (t + 1) * LANES)
        product = dot_tn(ref.im2[0, :, tap], ref.d2[0]) + dot_tn(ref.im2[1, :, tap], ref.d2[1])
        dk[t * CH : (t + 1) * CH, :] = roll64(both_halves(product))

    total1, y_waits = [], []
    for pair in range(PAIRS):
        h_waits[pair].wait_recv()
        for wait in h_edges[pair]:
            wait.wait_recv()
        sums = summed(6 + pair)
        total1.append(sums)
        center, factor = norm1[pair]
        scale = factor * gain1
        mean_grad, mean_scaled = sums[0:1, :] / pixel_total, sums[1:2, :] / pixel_total
        inner = low(scale * (ref.g1[pair] - mean_grad - ref.x1[pair] * mean_scaled))
        edge_scaled = (ref.halo[1, pair] - center) * factor
        edge = low(scale * (ref.halo[3, pair] - mean_grad - edge_scaled * mean_scaled))
        edge = jnp.where(halo_mask > 0.0, edge, 0.0)
        ref.d1[pair] = inner
        fill_ext(2, pair, inner, edge)
        here = shifted(2, pair, 1, range(1, EXT_ROWS))
        beside = shifted(2, pair, 2, range(1, EXT_ROWS))
        windows = [here[:HALF_ROWS], beside[:HALF_ROWS], here[1:], beside[1:]]
        windows = jnp.concatenate([jnp.concatenate(w, axis=0) for w in windows], axis=1)
        value = dot_nn(windows, ref.back1[...]).astype(BF16)
        value = dot_nn(fetch[pair], value)
        y_send = ref.y_send.at[pair].reshape(128 * 8, LANES)
        chosen = []
        for block in range(2 * SLOTS):
            rows = slice(block * LANES, (block + 1) * LANES)
            picked = value[rows, 0:LANES] * parity[pair, rows, 0:LANES].astype(F32)
            for q in range(1, 4):
                tile = slice(q * LANES, (q + 1) * LANES)
                picked = picked + value[rows, tile] * parity[pair, rows, tile].astype(F32)
            chosen.append(picked)
        for k in range(SLOTS):
            y_send[pl.ds(k, 128, stride=8), :] = jnp.where(first_half, chosen[k], chosen[SLOTS + k])
        ref.y_land[pair, 0, 0:SLOTS, :] = ref.y_send[pair, 0, 0:SLOTS, :]
        y_waits.append(
            wire.spread(
                total,
                lambda i: wire.source(i),
                lambda i, pair=pair: ref.y_send.at[pair, i, pl.ds(0, SLOTS)],
                lambda i, pair=pair: ref.y_land.at[pair, i, pl.ds(0, SLOTS)],
                ref.y_land.at[pair, pl.ds(1, total - 1), pl.ds(0, SLOTS)],
            )
        )

    upper, lefts = jnp.zeros((3 * LANES, LANES), F32), jnp.zeros((3 * LANES, LANES), F32)
    own1 = [ref.d1[pair].astype(BF16) for pair in range(PAIRS)]
    for pair in range(PAIRS):
        beside = ref.d1.at[pair][pl.ds(0, HALF_ROWS, stride=HALF_COLS), :].astype(BF16)
        upper = upper + dot_tn(ref.top1[pair], own1[pair][0:HALF_COLS, :])
        lefts = lefts + dot_tn(ref.left1[pair], beside)
    for t in range(TAPS):
        tap = slice(t * LANES, (t + 1) * LANES)
        product = dot_tn(ref.im1[0, :, tap], own1[0]) + dot_tn(ref.im1[1, :, tap], own1[1])
        if t < 3:
            product = product + upper[tap, :]
        if t % 3 == 0:
            product = product + lefts[t // 3 * LANES : (t // 3 + 1) * LANES, :]
        at = slice(t * CH, (t + 1) * CH)
        dk[at, :] = jnp.where(first_half, both_halves(product), dk[at, :])
    padding = jnp.zeros((PAD_ROWS - OWN_ROWS, LANES), F32)
    for i in range(n_rows):
        owner = wire.peer(i)[0]
        block = dk[pl.ds(pl.multiple_of(owner * OWN_ROWS, 8), OWN_ROWS), :]
        block = jnp.concatenate([block, padding], axis=0).astype(BF16)
        ref.g_send[i] = block
        if i == 0:
            ref.g_land[0] = block
    g1_wait = wire.spread(
        n_rows,
        wire.peer,
        lambda i: ref.g_send.at[i],
        lambda i: ref.g_land.at[i],
        ref.g_land.at[pl.ds(1, n_rows - 1)],
    )
    scales = square_of(jnp.concatenate([norm0[s][2] for s in range(SCENES)], axis=0))
    scales = jnp.transpose(scales)[0:CH, :]

    k_waits = []
    ones = jnp.ones((8, LANES), F32)
    for pair in range(PAIRS):
        y_waits[pair].wait_recv()
        y_land = ref.y_land.at[pair].reshape(128 * 8, LANES)
        landed = [jnp.transpose(y_land[pl.ds(k, 128, stride=8), :]) for k in range(SLOTS)]
        landed = jnp.concatenate(landed, axis=1).astype(BF16)
        parts = [[], []]
        for half in range(2):
            s = 2 * pair + half
            pick = jnp.concatenate([hot[s * SLOTS + k] for k in range(SLOTS)], axis=0)
            grad = dot_nn(landed[half * CH : (half + 1) * CH, :], pick)
            ref.grads[s] = grad
            for kind in range(2):
                parts[kind].append(grad * ref.q_sum[s, kind])
        sums = [dot_nt(ones, jnp.concatenate(part, axis=0), HIGH)[0:1, :] for part in parts]
        k_waits.append(global_sums(8 + pair, *sums))

    scaled_grads = [ref.grads[s] * scales[:, s : s + 1] for s in range(SCENES)]
    weight_grad = jnp.zeros((CH, LANES), F32)
    for c in range(FEATS):
        product = scaled_grads[0] * ref.t_sum[0, c]
        for s in range(1, SCENES):
            product = product + scaled_grads[s] * ref.t_sum[s, c]
        weight_grad = jnp.where(lane == c, jnp.sum(product, axis=1, keepdims=True), weight_grad)
    ref.p_col[...] = weight_grad
    for i in range(n_rows):
        owner = wire.peer(i)[0]
        block = ref.p_col[pl.ds(pl.multiple_of(owner * 8, 8), 8), :]
        ref.p_send[i] = block
        if i == 0:
            ref.p_land[0] = block
    p_wait = wire.spread(
        n_rows,
        wire.peer,
        lambda i: ref.p_send.at[i],
        lambda i: ref.p_land.at[i],
        ref.p_land.at[pl.ds(1, n_rows - 1)],
    )
    g1_wait.wait_recv()
    block = jnp.sum(ref.g_land[...].astype(F32), axis=0).astype(BF16)
    ref.g2_send[...] = block
    ref.g2_land[0] = block
    g2_wait = wire.spread(
        n_cols,
        wire.along_cols,
        lambda i: ref.g2_send,
        lambda i: ref.g2_land.at[i],
        ref.g2_land.at[pl.ds(1, n_cols - 1)],
    )

    def update(s):
        scaled_w = w_row * norm0[s][2]
        coarse = low(scaled_w)
        matrix = jnp.where(first_half, coarse, roll64(scaled_w - coarse)).astype(BF16)
        grad = ref.grads[s]
        for j in range(DEPTH // 4):
            block = [(ref.share[s, 4 * j + t] * grad).astype(BF16) for t in range(4)]
            block = jnp.concatenate(block, axis=1)
            ref.upd[s, :, j * 4 * LANES : (j + 1) * 4 * LANES] = dot_nn(
                matrix, jnp.concatenate([block, block], axis=0)
            )

    update(0)
    update(1)
    p_wait.wait_recv()
    block = jnp.sum(ref.p_land[...], axis=0)
    ref.p2_send[...] = block
    ref.p2_land[0] = block
    p2_wait = wire.spread(
        n_cols,
        wire.along_cols,
        lambda i: ref.p2_send,
        lambda i: ref.p2_land.at[i],
        ref.p2_land.at[pl.ds(1, n_cols - 1)],
    )
    update(2)
    update(3)

    bias_sum, gain_sum = jnp.zeros((1, LANES), F32), jnp.zeros((1, LANES), F32)
    correction = jnp.zeros((16, LANES), F32)
    gain_safe = jnp.where(first_half, gain0, 1.0)
    for pair in range(PAIRS):
        k_waits[pair].wait_recv()
        sums = summed(8 + pair)
        for half in range(2):
            s = 2 * pair + half
            center, factor, scale, count, cross, products = norm0[s]
            own = jnp.where(first_half, roll64(sums) if half else sums, 0.0)
            grad_sum = own[0:1, :]
            scaled_sum = (own[1:2, :] - bias0 * grad_sum) / gain_safe
            bias_sum, gain_sum = bias_sum + grad_sum, gain_sum + scaled_sum
            grad_mean, scaled_mean = grad_sum / count, scaled_sum / count
            point_sums = products[:, 9:10]
            correction = correction + scale * (
                grad_mean * point_sums + scaled_mean * factor * (cross - center * point_sums)
            )
            unit = w_row * factor - jnp.where(feature_row == FEATS, center * factor, 0.0)
            unit = unit * scaled_mean + jnp.where(feature_row == FEATS, grad_mean, 0.0)
            mix = dot_nt(w_row * scale, unit, HIGH)
            coarse = low(mix)
            mix = jnp.concatenate([coarse, mix - coarse], axis=1).astype(BF16)
            out = ref.point_grads.at[s]
            for j in range(DEPTH // 4):
                lanes = slice(j * 4 * LANES, (j + 1) * 4 * LANES)
                points = aug[s, :, lanes]
                value = ref.upd[s, :, lanes] - dot_nn(
                    mix, jnp.concatenate([points, points], axis=0)
                )
                for t in range(4):
                    n = 4 * j + t
                    at = slice(t * LANES, (t + 1) * LANES)
                    out[pl.ds(n, 8, stride=DEPTH), :] = value[0:8, at]
                    out[8 * DEPTH + n : 8 * DEPTH + n + 1, :] = value[8:9, at]

    def own_lanes(values):
        return pltpu.roll(values, lax.rem(LANES - 8 * row, LANES), axis=1)

    def both_scenes(values, index):
        added = values[0][index : index + 1, :] + values[1][index : index + 1, :]
        return added + roll64(added)

    small = ref.small
    small[...] = jnp.zeros((8, LANES), F32)
    small[0:1, :] = bias_sum
    small[1:2, :] = both_scenes(total1, 0)
    small[2:3, :] = both_scenes(total2, 0)
    small[3:4, :] = gain_sum
    small[4:5, :] = both_scenes(total1, 1)
    small[5:6, :] = both_scenes(total2, 1)
    owned = own_lanes(small[...])
    ref.bias_grad[...] = owned[0:3, 0:8]
    ref.gain_grad[...] = owned[3:6, 0:8]
    correction = jnp.transpose(square_of(own_lanes(correction)))
    p2_wait.wait_recv()
    block = jnp.sum(ref.p2_land[...], axis=0)
    ref.pfn_grad[...] = (block - correction[0:8, :])[:, 0:FEATS]
    g2_wait.wait_recv()
    block = jnp.transpose(square_of(jnp.sum(ref.g2_land[...].astype(F32), axis=0)))
    ref.conv_grad[0] = block[0:CH, 0:OWN_ROWS]
    ref.conv_grad[1] = block[CH:LANES, 0:OWN_ROWS]
    wire.settle()


def result_kernel(*refs):
    sems = refs[-1]
    copies = [
        pltpu.make_async_copy(refs[i], refs[RESULTS + i], sems.at[i]) for i in range(RESULTS)
    ]
    for copy in copies:
        copy.start()
    for copy in copies:
        copy.wait()


def body(points, counts, tiles, cells, pfn_weight, conv_weight, norm_gain, norm_bias, cotangent):
    scenes, feats, depth, pillars = points.shape
    n_rows, n_cols = lax.axis_size("rows"), lax.axis_size("cols")
    anywhere = pl.BlockSpec(memory_space=pl.ANY)
    inside = pl.BlockSpec(memory_space=pltpu.VMEM)
    shapes = [
        jax.ShapeDtypeStruct(cotangent.shape, BF16),
        jax.ShapeDtypeStruct((scenes, feats * depth, pillars), F32),
        jax.ShapeDtypeStruct(pfn_weight.shape[::-1], F32),
        jax.ShapeDtypeStruct((2, CH, OWN_ROWS), F32),
        jax.ShapeDtypeStruct(norm_gain.shape, F32),
        jax.ShapeDtypeStruct(norm_bias.shape, F32),
    ]
    results = pl.pallas_call(
        functools.partial(step_kernel, n_rows, n_cols),
        out_shape=[pltpu.VMEM(shape.shape, shape.dtype) for shape in shapes],
        in_specs=[anywhere] * INPUTS,
        out_specs=[inside] * RESULTS,
        scratch_shapes=[pltpu.VMEM(shape, dtype) for shape, dtype in SCRATCH.values()]
        + [
            pltpu.SemaphoreType.DMA((SEMS,)),
            pltpu.SemaphoreType.DMA((SEMS,)),
            pltpu.SemaphoreType.DMA((INPUTS,)),
        ],
        compiler_params=pltpu.CompilerParams(
            collective_id=0, has_side_effects=True, vmem_limit_bytes=54 * 2**20
        ),
    )(
        points.reshape(scenes, feats * depth, pillars),
        counts,
        tiles.reshape(scenes, pillars),
        cells,
        pfn_weight.T,
        conv_weight.transpose(0, 2, 1),
        norm_gain,
        norm_bias,
        cotangent,
    )
    results = pl.pallas_call(
        result_kernel,
        out_shape=shapes,
        in_specs=[inside] * RESULTS,
        out_specs=[anywhere] * RESULTS,
        scratch_shapes=[pltpu.SemaphoreType.DMA((RESULTS,))],
    )(*[pltpu.with_memory_space_constraint(result, pltpu.VMEM) for result in results])
    return (
        results[0],
        results[1].reshape(points.shape),
        results[2].T,
        results[3].transpose(0, 2, 1),
        results[4],
        results[5],
    )


def solution(mesh):
    in_specs = (
        P(None, None, None, ("rows", "cols")),
        P(None, ("rows", "cols")),
        P(None, ("rows", "cols"), None),
        P(None, ("rows", "cols")),
        P(None, "rows"),
        P(None, "rows", None),
        P(None, "rows"),
        P(None, "rows"),
        P(None, "rows", "cols"),
    )
    out_specs = (
        P(None, "rows", "cols"),
        P(None, None, None, ("rows", "cols")),
        P(None, "rows"),
        P(None, "rows", None),
        P(None, "rows"),
        P(None, "rows"),
    )
    return jax.shard_map(body, mesh=mesh, in_specs=in_specs, out_specs=out_specs, check_vma=False)
```

```python
import functools
import types

import jax
import jax.numpy as jnp
from jax import lax
from jax.experimental import pallas as pl
from jax.experimental.pallas import tpu as pltpu
from jax.sharding import PartitionSpec as P

EPSILON = 1e-05
HIGH = lax.Precision.HIGHEST
MESH = pl.DeviceIdType.MESH
F32, BF16, I32 = jnp.float32, jnp.bfloat16, jnp.int32

SCENES = 4
PAIRS = 2
FEATS = 9
DEPTH = 32
PILLARS = 128
CH = 64
LANES = 128
HALF_ROWS = 32
HALF_COLS = 16
PIXELS = HALF_ROWS * HALF_COLS
SLOTS = 3
EDGE = 8
EXT_COLS = 32
EXT_ROWS = HALF_ROWS + 2
TAPS = 9
OWN_ROWS = 72
PAD_ROWS = 80
PIECE = 40
UNROLL = 4
PARTS = (0, 4, 10, 13)
BLOCK = 48


def dot_nn(a, b, precision=None):
    return lax.dot_general(
        a, b, (((1,), (0,)), ((), ())), precision=precision, preferred_element_type=F32
    )


def dot_nt(a, b, precision=None):
    return lax.dot_general(
        a, b, (((1,), (1,)), ((), ())), precision=precision, preferred_element_type=F32
    )


def dot_tn(a, b):
    return lax.dot_general(a, b, (((0,), (0,)), ((), ())), preferred_element_type=F32)


def iota(shape, dim):
    return lax.broadcasted_iota(I32, shape, dim)


def sigmoid(v):
    return 0.5 * jnp.tanh(0.5 * v) + 0.5


def low(v):
    return v.astype(BF16).astype(F32)


def one_hot(mask):
    return jnp.where(mask, 1.0, 0.0).astype(BF16)


def square_of(v):
    rows, cols = v.shape
    if cols < LANES:
        v = jnp.concatenate([v, jnp.zeros((rows, LANES - cols), v.dtype)], axis=1)
    return jnp.concatenate([v, jnp.zeros((LANES - rows, LANES), v.dtype)], axis=0)


def roll64(v):
    return pltpu.roll(v, CH, axis=1)


SCRATCH = dict(
    points=((SCENES, FEATS * DEPTH, LANES), BF16),
    counts=((SCENES, LANES), I32),
    tiles=((SCENES, LANES), I32),
    cells=((SCENES, LANES), I32),
    pfn=((8, FEATS), BF16),
    conv=((2, CH, OWN_ROWS), BF16),
    gain=((3, 8), BF16),
    bias=((3, 8), BF16),
    cotangent=((SCENES, HALF_ROWS, HALF_COLS * CH), BF16),
    square=((LANES, LANES), F32),
    w_tmp=((16, LANES), F32),
    w_send=((16, LANES), F32),
    w_land=((8, 16, LANES), F32),
    c_send=((PAD_ROWS, LANES), BF16),
    c_land=((8, PAD_ROWS, LANES), BF16),
    taps=((TAPS * CH, LANES), F32),
    wide1=((TAPS * LANES, LANES), BF16),
    side1=((3 * LANES, LANES), BF16),
    wide2=((TAPS * LANES, LANES), BF16),
    back2=((TAPS * LANES, LANES), BF16),
    back1=((4 * LANES, 4 * LANES), BF16),
    pts32=((SCENES, 16 * DEPTH, LANES), F32),
    aug=((SCENES, 16, DEPTH * LANES), BF16),
    hot=((SCENES * SLOTS, LANES, LANES), BF16),
    m_send=((2, 4, LANES), F32),
    m_land=((8, 4, LANES), F32),
    m2_land=((16, 4, LANES), F32),
    hello=((4, 4, LANES), F32),
    spots=((LANES, LANES), F32),
    cell_send=((8, 16, LANES), F32),
    cell_land=((8, 16, LANES), F32),
    cell2_send=((16, 8, LANES), F32),
    cell2_land=((16, 8, LANES), F32),
    gram=((SCENES * 16, LANES), F32),
    place=((PAIRS, PIXELS, 6 * LANES), BF16),
    rim=((PAIRS, 48, 6 * LANES), BF16),
    parity=((PAIRS, 6 * LANES, 4 * LANES), BF16),
    fetch=((PAIRS, 6 * LANES, PIXELS), BF16),
    linear=((SCENES, DEPTH, CH, LANES), F32),
    halves=((SCENES, 2, CH, LANES), F32),
    act=((SCENES, DEPTH, CH, LANES), F32),
    share=((SCENES, DEPTH, CH, LANES), F32),
    pil=((SCENES, CH, LANES), F32),
    t_sum=((SCENES, FEATS, CH, LANES), F32),
    q_sum=((SCENES, 2, CH, LANES), F32),
    x_send=((PAIRS, 128, 8, LANES), F32),
    x_land=((PAIRS, 128, 8, LANES), F32),
    y_send=((PAIRS, 128, 8, LANES), F32),
    y_land=((PAIRS, 128, 8, LANES), F32),
    rim_send=((PAIRS, 2, 48, LANES), F32),
    rim_land=((PAIRS, 2, 56, LANES), F32),
    im1=((PAIRS, PIXELS, TAPS * LANES), BF16),
    top1=((PAIRS, 16, 3 * LANES), BF16),
    left1=((PAIRS, 32, 3 * LANES), BF16),
    im2=((PAIRS, PIXELS, TAPS * LANES), BF16),
    im3=((PAIRS, PIXELS, TAPS * LANES), BF16),
    im4=((PAIRS, PIXELS, 4 * LANES), BF16),
    back=((PAIRS, PIXELS, 4 * LANES), BF16),
    pick_c=((FEATS * LANES, LANES), BF16),
    y1=((PAIRS, PIXELS, LANES), F32),
    y2=((PAIRS, PIXELS, LANES), F32),
    x1=((PAIRS, PIXELS, LANES), F32),
    x2=((PAIRS, PIXELS, LANES), F32),
    s1=((PAIRS, PIXELS, LANES), F32),
    g1=((PAIRS, PIXELS, LANES), F32),
    g2=((PAIRS, PIXELS, LANES), F32),
    feat=((PAIRS, PIXELS, LANES), F32),
    cot=((PAIRS, PIXELS, LANES), F32),
    d1=((PAIRS, PIXELS, LANES), F32),
    d2=((PAIRS, PIXELS, LANES), BF16),
    cols=((4, PAIRS, 2, HALF_ROWS, LANES), F32),
    halo=((4, PAIRS, LANES, LANES), F32),
    ext=((3, PAIRS, EXT_ROWS * EXT_COLS, LANES), F32),
    st_send=((10, 2, LANES), F32),
    st_land=((10, 128, 2, LANES), F32),
    grads=((SCENES, CH, LANES), F32),
    p_col=((CH, LANES), F32),
    k_send=((8, 4, LANES), F32),
    k_land=((128, 4, LANES), F32),
    dk=((2, TAPS * CH, LANES), F32),
    g_send=((2, 8, BLOCK, LANES), BF16),
    g_land=((2, 8, BLOCK, LANES), BF16),
    gx_land=((4, BLOCK, LANES), BF16),
    gz_land=((4, BLOCK, LANES), BF16),
    gc_land=((16, BLOCK, LANES), BF16),
    upd=((SCENES, 16, DEPTH * LANES), F32),
    small=((8, LANES), F32),
)
INPUTS = 9
RESULTS = 6
SEMS = 96


HIGH_BITS, LOW_BITS = 0b1010101, 0b0101010


def digits_add(a, b):
    carried = jnp.bitwise_and(a, LOW_BITS) + jnp.bitwise_and(b, LOW_BITS)
    return jnp.bitwise_xor(carried, jnp.bitwise_and(jnp.bitwise_xor(a, b), HIGH_BITS))


def digits_sub(a, b):
    borrowed = jnp.bitwise_or(a, HIGH_BITS) - jnp.bitwise_and(b, LOW_BITS)
    kept = jnp.bitwise_and(jnp.bitwise_xor(jnp.bitwise_xor(a, b), HIGH_BITS), HIGH_BITS)
    return jnp.bitwise_xor(borrowed, kept)


def far_first(step):
    return jnp.bitwise_xor(step, jnp.bitwise_and(jnp.right_shift(step, 1), LOW_BITS))


class Wire:
    def __init__(self, n_rows, n_cols, send_sems, recv_sems):
        self.n_rows, self.n_cols = n_rows, n_cols
        self.total = n_rows * n_cols
        self.row, self.col = lax.axis_index("rows"), lax.axis_index("cols")
        self.me = self.col * n_rows + self.row
        self.send_sems, self.recv_sems = send_sems, recv_sems
        self.used = 0
        self.sent = []

    def place(self, number):
        return (
            jnp.bitwise_and(number, self.n_rows - 1),
            jnp.right_shift(number, self.n_rows.bit_length() - 1),
        )

    def peer(self, step):
        return self.place(digits_add(self.me, step))

    def source(self, step):
        return self.place(digits_sub(self.me, step))

    def along_cols(self, step):
        return self.peer(step * self.n_rows)

    def near(self, down, right):
        return (
            lax.rem(self.row + down + self.n_rows, self.n_rows),
            lax.rem(self.col + right + self.n_cols, self.n_cols),
        )

    def copy(self, src, dst, sem, peer):
        return pltpu.make_async_remote_copy(
            src_ref=src,
            dst_ref=dst,
            send_sem=self.send_sems.at[sem],
            recv_sem=self.recv_sems.at[sem],
            device_id=peer,
            device_id_type=MESH,
        )

    def one(self, src, dst, peer):
        sem = self.used
        self.used += 1
        copy = self.copy(src, dst, sem, peer)
        copy.start()
        self.sent.append(copy)
        return copy

    def spread(self, count, peer_of, src_of, dst_of, whole):
        sem = self.used
        self.used += 1

        def step(j, carry):
            i = far_first(count - j)
            self.copy(src_of(i), dst_of(i), sem, peer_of(i)).start()
            return carry

        lax.fori_loop(1, count, step, 0, unroll=8)
        copy = self.copy(whole, whole, sem, peer_of(1))
        self.sent.append(copy)
        return copy

    def local(self, src, dst, sems, index):
        copy = pltpu.make_async_copy(src, dst, sems.at[index])
        copy.start()
        return copy

    def settle(self):
        for copy in self.sent:
            copy.wait_send()


def step_kernel(n_rows, n_cols, *refs):
    inputs, results = refs[:INPUTS], refs[INPUTS : INPUTS + RESULTS]
    ref = types.SimpleNamespace(**dict(zip(SCRATCH, refs[INPUTS + RESULTS :], strict=False)))
    ref.features, ref.point_grads, ref.pfn_grad, ref.conv_grad, ref.gain_grad, ref.bias_grad = results
    send_sems, recv_sems, in_sems = refs[-3:]
    wire = Wire(n_rows, n_cols, send_sems, recv_sems)
    total, row, col, me = wire.total, wire.row, wire.col, wire.me
    lane = iota((1, LANES), 1)
    first_half = lane < CH

    barrier = pltpu.get_barrier_semaphore()

    lines = [i for i in range(1, n_rows)] + [i * 8 for i in (1, 2, 3)] + [i * 32 for i in (1, 2, 3)]
    for step in lines:
        pl.semaphore_signal(barrier, inc=1, device_id=wire.peer(step), device_id_type=MESH)
    held = [
        ref.points, ref.counts, ref.tiles, ref.cells, ref.pfn, ref.conv, ref.gain, ref.bias,
        ref.cotangent,
    ]
    order = [1, 0, 2, 3, 4, 6, 7, 5, 8]
    loads = {i: wire.local(inputs[i], held[i], in_sems, i) for i in order}
    for i in range(INPUTS):
        loads[i].wait()
    pts32, aug = ref.pts32, ref.aug
    slot_number = iota((DEPTH, LANES), 0)
    for s in range(SCENES):
        valid = slot_number < ref.counts[s : s + 1, :]
        for c in range(FEATS):
            block = ref.points[s, c * DEPTH : (c + 1) * DEPTH, :].astype(F32)
            pts32[s, c * DEPTH : (c + 1) * DEPTH, :] = jnp.where(valid, block, 0.0)
        pts32[s, FEATS * DEPTH : (FEATS + 1) * DEPTH, :] = jnp.where(valid, 1.0, 0.0)
        pts32[s, (FEATS + 1) * DEPTH :, :] = jnp.zeros((6 * DEPTH, LANES), F32)
        scene_pts = pts32.at[s]
        for n in range(DEPTH):
            aug[s, :, n * LANES : (n + 1) * LANES] = scene_pts[pl.ds(n, 16, stride=DEPTH), :].astype(
                BF16
            )
    stacked = jnp.concatenate([aug[s] for s in range(SCENES)], axis=0)
    gram_all = dot_nt(stacked, jnp.concatenate([stacked, stacked], axis=0))
    moments = jnp.zeros((4, LANES), F32)
    for s in range(SCENES):
        for b in range(3):
            piece = gram_all[16 * s + 4 * b : 16 * s + 4 * b + 4, :]
            at = 40 * b + 10 * s
            piece = pltpu.roll(piece, (at - 16 * s) % LANES, axis=1)
            moments = moments + jnp.where((lane >= at) & (lane < at + 10), piece, 0.0)

    hot = ref.hot
    above = iota((LANES, LANES), 0) < iota((LANES, LANES), 1)
    slot_row = iota((LANES, LANES), 0).astype(F32) * 4.0
    for s in range(SCENES):
        tile = ref.tiles[s : s + 1, :]
        tile = jnp.bitwise_and(tile, n_cols - 1) * n_rows + jnp.right_shift(
            tile, n_cols.bit_length() - 1
        )
        tile = digits_sub(tile, me).astype(F32)
        wide = jnp.broadcast_to(tile, (LANES, LANES))
        same = (jnp.transpose(wide) == wide) & above
        rank = jnp.sum(jnp.where(same, 1.0, 0.0), axis=0, keepdims=True)
        code = tile * 4.0 + rank
        for k in range(SLOTS):
            hot[s * SLOTS + k] = one_hot(slot_row + float(k) == code)

    lane_row = iota((LANES, LANES), 0)
    spots = jnp.zeros((LANES, LANES), F32)
    for q in range(4):
        for pair in range(PAIRS):
            s = 2 * pair + q // 2
            cell = ref.cells[s : s + 1, :]
            spot = (jnp.bitwise_and(cell, 31) if q % 2 else jnp.right_shift(cell, 5)) + 1
            for k in range(SLOTS):
                at = jnp.where(lane_row == q * 8 + 3 * pair + k, spot.astype(F32), 0.0)
                spots = spots + dot_nt(hot[s * SLOTS + k], at.astype(BF16))
    ref.spots[...] = spots
    for i in range(n_rows):
        ref.cell_send[i] = ref.spots[pl.ds(i, n_cols, stride=n_rows), :]
    ref.cell_land[0] = ref.cell_send[0]
    ref.m_send[0] = moments
    ref.m_land[0] = moments
    ref.hello[0] = moments

    ref.square[...] = jnp.zeros((LANES, LANES), F32)
    ref.square[0:8, 0:FEATS] = ref.pfn[...].astype(F32)
    ref.w_tmp[...] = jnp.transpose(ref.square[...])[0:16, :]
    ref.w_tmp[9:12, 0:8] = ref.gain[...].astype(F32)
    ref.w_tmp[12:15, 0:8] = ref.bias[...].astype(F32)
    ref.w_send[...] = pltpu.roll(ref.w_tmp[...], row * 8, axis=1)
    ref.w_land[0] = ref.w_send[...]
    pl.semaphore_wait(barrier, len(lines))
    m_wait = wire.spread(
        n_rows,
        wire.peer,
        lambda i: ref.m_send.at[0],
        lambda i: ref.m_land.at[i],
        ref.m_land.at[pl.ds(1, n_rows - 1)],
    )
    hello_wait = wire.spread(
        4,
        lambda i: wire.peer(i * 8),
        lambda i: ref.hello.at[0],
        lambda i: ref.hello.at[i],
        ref.hello.at[pl.ds(1, 3)],
    )
    w_wait = wire.spread(
        n_rows,
        wire.peer,
        lambda i: ref.w_send,
        lambda i: ref.w_land.at[i],
        ref.w_land.at[pl.ds(1, n_rows - 1)],
    )
    m_wait.wait_recv()
    hello_wait.wait_recv()
    moments = jnp.sum(ref.m_land[...], axis=0)
    ref.m_send[1] = moments
    ref.m2_land[0] = moments
    m2_wait = wire.spread(
        n_cols,
        wire.along_cols,
        lambda i: ref.m_send.at[1],
        lambda i: ref.m2_land.at[i],
        ref.m2_land.at[pl.ds(1, n_cols - 1)],
    )

    cell_wait = wire.spread(
        n_rows,
        wire.peer,
        lambda i: ref.cell_send.at[i],
        lambda i: ref.cell_land.at[i],
        ref.cell_land.at[pl.ds(1, n_rows - 1)],
    )

    def halo_send(values, index, pair, full):
        cols, halo = ref.cols.at[index, pair], ref.halo.at[index, pair]
        inner = values.at[pair]
        for side in range(2 if full else 1):
            cols[side] = inner[pl.ds(side * (HALF_COLS - 1), HALF_ROWS, stride=HALF_COLS), :]

        def send(src, start, count, at, down, right):
            return wire.one(
                src.at[pl.ds(start, count)], halo.at[pl.ds(at, count)], wire.near(down, right)
            )

        waits = [
            send(inner, 0, 8, 120, -1, -1),
            send(cols.at[0], 0, 32, 64, 0, -1),
            send(inner, 0, 16, 16, -1, 0),
        ]
        if full:
            waits += [
                send(inner, 504, 8, 96, 1, 1),
                send(inner, 8, 8, 112, -1, 1),
                send(inner, 496, 8, 104, 1, -1),
                send(cols.at[1], 0, 32, 32, 0, 1),
                send(inner, 496, 16, 0, 1, 0),
            ]
        return waits

    def there(cond):
        return jnp.where(cond, 1.0, 0.0)

    up, down = there(row > 0), there(row < n_rows - 1)
    left, right = there(col > 0), there(col < n_cols - 1)
    spot = iota((LANES, LANES), 0)
    halo_mask = jnp.where(spot < 16, up, jnp.where(spot < 32, down, jnp.where(spot < 64, left, right)))
    halo_mask = jnp.where(spot < 96, halo_mask, jnp.where(spot < 112, up, down))
    halo_mask = jnp.where(
        spot < 96,
        halo_mask,
        halo_mask * jnp.where((spot < 104) | ((spot >= 112) & (spot < 120)), left, right),
    )

    def fill_ext(index, pair, inner, edge):
        grid = ref.ext.at[index, pair]
        for i in range(HALF_ROWS):
            at = (i + 1) * EXT_COLS + EDGE
            grid[at : at + HALF_COLS, :] = inner[i * HALF_COLS : (i + 1) * HALF_COLS, :]
        grid[EDGE : EDGE + HALF_COLS, :] = edge[0:16, :]
        last = (EXT_ROWS - 1) * EXT_COLS
        grid[last + EDGE : last + EDGE + HALF_COLS, :] = edge[16:32, :]
        grid[pl.ds(EXT_COLS + EDGE - 1, HALF_ROWS, stride=EXT_COLS), :] = edge[32:64, :]
        grid[pl.ds(EXT_COLS + EDGE + HALF_COLS, HALF_ROWS, stride=EXT_COLS), :] = edge[64:96, :]
        grid[EDGE - 1 : EDGE, :] = edge[103:104, :]
        grid[EDGE + HALF_COLS : EDGE + HALF_COLS + 1, :] = edge[104:105, :]
        grid[last + EDGE - 1 : last + EDGE, :] = edge[119:120, :]
        grid[last + EDGE + HALF_COLS : last + EDGE + HALF_COLS + 1, :] = edge[120:121, :]

    def shifted(index, pair, shift, rows):
        grid = ref.ext.at[index, pair]
        start = EDGE - 1 + shift
        return [
            grid[i * EXT_COLS + start : i * EXT_COLS + start + HALF_COLS, :].astype(BF16)
            for i in rows
        ]

    def column_sum(v):
        return jnp.sum(v, axis=0, keepdims=True)

    def global_sums(index, first, second):
        send, land = ref.st_send.at[index], ref.st_land.at[index]
        send[0:1, :] = first
        send[1:2, :] = second
        land[0] = send[...]
        return wire.spread(
            total,
            wire.peer,
            lambda i: send,
            lambda i: land.at[i],
            land.at[pl.ds(1, total - 1)],
        )

    def summed(index):
        return jnp.sum(ref.st_land[index], axis=0)

    pixel_total = float(PIXELS * total)

    def norm_of(sums):
        center = sums[0:1, :] / pixel_total
        spread = sums[1:2, :] / pixel_total - center * center
        return center, lax.rsqrt(spread + EPSILON)

    ref.square[:, 0:OWN_ROWS] = jnp.concatenate(
        [ref.conv[0].astype(F32), ref.conv[1].astype(F32)], axis=0
    )
    ref.c_send[...] = jnp.transpose(ref.square[...])[0:PAD_ROWS, :].astype(BF16)
    ref.c_land[0] = ref.c_send[...]
    w_wait.wait_recv()
    w_full = jnp.sum(ref.w_land[...], axis=0)
    feature_row = iota((16, LANES), 0)
    w_row = jnp.where(feature_row < FEATS, w_full, 0.0)
    matrix = jnp.transpose(square_of(w_row))[0:CH, 0:16].astype(BF16)
    STEP = 8
    for s in range(SCENES):
        for j in range(DEPTH // STEP):
            value = dot_nn(matrix, aug[s, :, j * STEP * LANES : (j + 1) * STEP * LANES])
            for t in range(STEP):
                ref.linear[s, STEP * j + t] = value[:, t * LANES : (t + 1) * LANES]
    cell_wait.wait_recv()
    cell_land = ref.cell_land.reshape(n_rows * n_cols, LANES)
    for i in range(n_cols):
        ref.cell2_send[i] = cell_land[pl.ds(i, n_rows, stride=n_cols), :]
    ref.cell2_land[0] = ref.cell2_send[0]
    cell2_wait = wire.spread(
        n_cols,
        wire.along_cols,
        lambda i: ref.cell2_send.at[i],
        lambda i: ref.cell2_land.at[i],
        ref.cell2_land.at[pl.ds(1, n_cols - 1)],
    )
    m2_wait.wait_recv()


    def twice(v):
        return v + roll64(v)

    gain0, bias0 = w_full[9:10, :], w_full[12:13, :]
    gain1, bias1 = twice(w_full[10:11, :]), twice(w_full[13:14, :])
    gain2, bias2 = twice(w_full[11:12, :]), twice(w_full[14:15, :])
    moments = jnp.sum(ref.m2_land[...], axis=0)
    gram = ref.gram
    gram[...] = jnp.zeros((SCENES * 16, LANES), F32)
    for s in range(SCENES):
        for b in range(3):
            piece = pltpu.roll(moments, (LANES - 40 * b - 10 * s) % LANES, axis=1)
            at = 16 * s + 4 * b
            gram[at : at + 4, :] = jnp.where(lane < 10, piece, 0.0)
    crosses = dot_nn(gram[:, 0:16], w_row, HIGH)
    norm0, columns = [], []
    for s in range(SCENES):
        products, cross = gram[16 * s : 16 * s + 16, :], crosses[16 * s : 16 * s + 16, :]
        count = products[9:10, 9:10]
        center = cross[9:10, :] / count
        spread = column_sum(w_row * cross) / count - center * center
        factor = lax.rsqrt(spread + EPSILON)
        scale = factor * gain0
        norm0.append((center, factor, scale, count, cross, products))
        columns += [scale, 0.5 * scale, 0.5 * (bias0 - center * scale)]
    columns = jnp.transpose(square_of(jnp.concatenate(columns, axis=0)))[0:CH, :]
    for s in range(SCENES):
        for kind in range(2):
            at = 3 * s + 1 + kind
            ref.halves[s, kind] = jnp.broadcast_to(columns[:, at : at + 1], (CH, LANES))

    x_waits = []
    for pair in range(PAIRS):
        for s in (2 * pair, 2 * pair + 1):
            bound = ref.counts[s : s + 1, :]
            half_scale, half_shift = ref.halves[s, 0], ref.halves[s, 1]
            peak = jnp.full((CH, LANES), -1e30, F32)
            for n in range(DEPTH):
                half = ref.linear[s, n] * half_scale + half_shift
                active = jnp.where(n < bound, half * jnp.tanh(half) + half, -1e30)
                ref.act[s, n] = active
                peak = jnp.maximum(peak, active)
            whole = jnp.zeros((CH, LANES), F32)
            for n in range(DEPTH):
                whole = whole + jnp.exp(ref.act[s, n] - peak)
            ref.pil[s] = peak + jnp.log(whole)
        x_send = ref.x_send.at[pair].reshape(128 * 8, LANES)
        a, b = ref.pil[2 * pair].astype(BF16), ref.pil[2 * pair + 1].astype(BF16)
        none = jnp.zeros((CH, LANES), BF16)
        both = jnp.concatenate(
            [jnp.concatenate([a, none], axis=1), jnp.concatenate([none, b], axis=1)], axis=0
        )
        for k in range(SLOTS):
            pick = jnp.concatenate(
                [hot[2 * pair * SLOTS + k], hot[(2 * pair + 1) * SLOTS + k]], axis=1
            )
            x_send[pl.ds(k, 128, stride=8), :] = dot_nt(pick, both)
        ref.x_land[pair, 0, 0:SLOTS, :] = ref.x_send[pair, 0, 0:SLOTS, :]
        x_waits.append(
            wire.spread(
                total,
                wire.peer,
                lambda i, pair=pair: ref.x_send.at[pair, i, pl.ds(0, SLOTS)],
                lambda i, pair=pair: ref.x_land.at[pair, i, pl.ds(0, SLOTS)],
                ref.x_land.at[pair, pl.ds(1, total - 1), pl.ds(0, SLOTS)],
            )
        )

    c_wait = wire.spread(
        n_rows,
        wire.peer,
        lambda i: ref.c_send,
        lambda i: ref.c_land.at[i],
        ref.c_land.at[pl.ds(1, n_rows - 1)],
    )

    def slopes(step, carry):
        s, block = step // 4, lax.rem(step, 4)
        rows = pl.ds(pl.multiple_of(block * 16, 16), 16)
        top = ref.pil[s, rows, :]
        half_scale, half_shift = ref.halves[s, 0, rows, :], ref.halves[s, 1, rows, :]

        def inner(j, sums):
            sums = list(sums)
            for t in range(UNROLL):
                n = UNROLL * j + t
                line, active = ref.linear[s, n, rows, :], ref.act[s, n, rows, :]
                half = line * half_scale + half_shift
                turn = jnp.tanh(half)
                share = jnp.exp(active - top) * ((0.5 + 0.5 * turn) * (1.0 + half * (1.0 - turn)))
                ref.share[s, n, rows, :] = share
                sums[0] = sums[0] + share
                sums[1] = sums[1] + share * line
                for c in range(FEATS):
                    sums[2 + c] = sums[2 + c] + share * pts32[s, pl.ds(c * DEPTH + n, 1), :]
            return tuple(sums)

        zero = jnp.zeros((16, LANES), F32)
        sums = lax.fori_loop(0, DEPTH // UNROLL, inner, (zero,) * (2 + FEATS))
        ref.q_sum[s, 0, rows, :] = sums[0]
        ref.q_sum[s, 1, rows, :] = sums[1]
        for c in range(FEATS):
            ref.t_sum[s, c, rows, :] = sums[2 + c] * (2.0 * half_scale)
        return carry

    cell2_wait.wait_recv()
    along_all = ref.cell2_land[...].reshape(LANES, LANES)
    across_all = jnp.transpose(along_all)
    place, rim, parity, fetch = ref.place, ref.rim, ref.parity, ref.fetch

    def pixel_of(tall, wide):
        i, j = tall.astype(I32) - 1, wide.astype(I32) - 1
        pixel = jnp.right_shift(i, 1) * HALF_COLS + jnp.right_shift(j, 1)
        plane = 2 * jnp.bitwise_and(i, 1) + jnp.bitwise_and(j, 1)
        return jnp.where(i < 0, -1, pixel), jnp.where(i < 0, -1, plane)

    rim_pixel = iota((48, LANES), 0)
    rim_pixel = jnp.where(rim_pixel < 16, 496 + rim_pixel, rim_pixel * 16 - 241)
    for pair in range(PAIRS):
        for half in range(2):
            for k in range(SLOTS):
                at = 16 * half + 3 * pair + k
                block = (half * SLOTS + k) * LANES
                blocks = slice(block, block + LANES)
                across, _ = pixel_of(across_all[at : at + 1, :], across_all[at + 8 : at + 9, :])
                _, along = pixel_of(along_all[:, at : at + 1], along_all[:, at + 8 : at + 9])
                along = jnp.broadcast_to(along, (LANES, LANES))
                for m in range(4):
                    tile = slice(m * LANES, (m + 1) * LANES)
                    place[pair, tile, blocks] = one_hot(
                        iota((LANES, LANES), 0) + m * LANES == across
                    )
                    parity[pair, blocks, tile] = one_hot(along == m)
                rim[pair, :, blocks] = one_hot(rim_pixel == across)

    lax.fori_loop(0, PARTS[0], slopes, 0)

    planes_of, d_waits = [], []
    for pair in range(PAIRS):
        x_waits[pair].wait_recv()
        x_land = ref.x_land.at[pair].reshape(128 * 8, LANES)
        landed = [x_land[pl.ds(k, 128, stride=8), :] for k in range(SLOTS)]
        values = [jnp.where(first_half, v, 0.0) for v in landed]
        values += [jnp.where(first_half, 0.0, v) for v in landed]
        values = jnp.concatenate(values, axis=0).astype(BF16)
        values = jnp.concatenate([values] * 4, axis=1) * parity[pair]
        planes_of.append(values)
        edge = low(dot_nn(rim[pair], values))
        rim_send, rim_land = ref.rim_send.at[pair], ref.rim_land.at[pair]
        rim_send[0, 0:16, :] = edge[0:16, 2 * LANES : 3 * LANES]
        rim_send[1, 0:16, :] = edge[0:16, 3 * LANES :]
        rim_send[0, 16:48, :] = edge[16:48, LANES : 2 * LANES]
        rim_send[1, 16:48, :] = edge[16:48, 3 * LANES :]
        d_waits.append(
            [
                wire.one(rim_send.at[1, pl.ds(40, 8)], rim_land.at[0, pl.ds(48, 8)], wire.near(1, 1)),
                wire.one(
                    rim_send.at[:, pl.ds(16, 32)], rim_land.at[:, pl.ds(16, 32)], wire.near(0, 1)
                ),
                wire.one(rim_send.at[:, pl.ds(0, 16)], rim_land.at[:, pl.ds(0, 16)], wire.near(1, 0)),
            ]
        )

    c_wait.wait_recv()
    taps = ref.taps
    for i in range(n_rows):
        owner = wire.source(i)[0]
        taps[pl.ds(pl.multiple_of(owner * OWN_ROWS, 8), OWN_ROWS), :] = ref.c_land[i].astype(F32)[
            0:OWN_ROWS, :
        ]
    ref.back1[...] = jnp.zeros((4 * LANES, 4 * LANES), BF16)
    for t in range(TAPS):
        both = taps[t * CH : (t + 1) * CH, :]
        swapped = roll64(both)
        at = t * LANES
        k1 = jnp.concatenate(
            [jnp.where(first_half, both, 0.0), jnp.where(first_half, 0.0, swapped)], axis=0
        )
        k2 = jnp.concatenate(
            [jnp.where(first_half, swapped, 0.0), jnp.where(first_half, 0.0, both)], axis=0
        )
        ref.wide1[at : at + LANES, :] = k1.astype(BF16)
        if t % 3 == 0:
            ref.side1[t // 3 * LANES : (t // 3 + 1) * LANES, :] = k1.astype(BF16)
        ref.wide2[at : at + LANES, :] = k2.astype(BF16)
        ref.back2[at : at + LANES, :] = jnp.transpose(k2).astype(BF16)
        a, b = t // 3, t % 3
        window = 2 * (a == 0) + (b == 0)
        plane = 2 * (a != 1) + (b != 1)
        ref.back1[
            window * LANES : (window + 1) * LANES, plane * LANES : (plane + 1) * LANES
        ] = jnp.transpose(k1).astype(BF16)

    y1 = ref.y1
    first_col = jnp.bitwise_and(iota((PIXELS, LANES), 0), HALF_COLS - 1) == 0
    no_row = jnp.zeros((HALF_COLS, LANES), BF16)
    for pair in range(PAIRS):
        grid = low(dot_nn(place[pair], planes_of[pair]))
        still = [grid[:, q * LANES : (q + 1) * LANES] for q in range(4)]
        moved = {q: jnp.where(first_col, 0.0, pltpu.roll(still[q], 1, axis=0)) for q in (1, 3)}
        for t in range(TAPS):
            a, b = t // 3, t % 3
            plane = 2 * (a != 1) + (b != 1)
            window = (moved[plane] if b == 0 else still[plane]).astype(BF16)
            if a == 0:
                window = jnp.concatenate([no_row, window[: PIXELS - HALF_COLS, :]], axis=0)
            ref.im1[pair, :, t * LANES : (t + 1) * LANES] = window
        y1[pair] = dot_nn(ref.im1[pair], ref.wide1[...])

    e_waits, e_edges = [], []
    for pair in range(PAIRS):
        for wait in d_waits[pair]:
            wait.wait_recv()
        rim_land = ref.rim_land.at[pair]
        rows_in = [rim_land[p, 0:16, :] * up for p in range(2)]
        cols_in = [rim_land[p, 16:48, :] * left for p in range(2)]
        corner = rim_land[0, 55:56, :] * (up * left)
        top = [
            jnp.where(iota((16, LANES), 0) == 0, corner, pltpu.roll(rows_in[1], 1, axis=0)),
            rows_in[0],
            rows_in[1],
        ]
        side = [
            jnp.where(iota((32, LANES), 0) == 0, 0.0, pltpu.roll(cols_in[1], 1, axis=0)),
            cols_in[0],
            cols_in[1],
        ]
        ref.top1[pair] = jnp.concatenate(top, axis=1).astype(BF16)
        ref.left1[pair] = jnp.concatenate(side, axis=1).astype(BF16)
        y1[pair, 0:16, :] += dot_nn(ref.top1[pair], ref.wide1[0 : 3 * LANES, :])
        beside = pl.ds(0, HALF_ROWS, stride=HALF_COLS)
        y1.at[pair][beside, :] += dot_nn(ref.left1[pair], ref.side1[...])
        value = y1[pair]
        e_waits.append(global_sums(pair, column_sum(value), column_sum(value * value)))
        e_edges.append(halo_send(y1, 1, pair, True))

    cot = ref.cot
    for pair in range(PAIRS):
        spread_to = cot.at[pair]
        for m in range(HALF_COLS // 2):
            a = ref.cotangent[2 * pair, :, m * LANES : (m + 1) * LANES].astype(F32)
            b = ref.cotangent[2 * pair + 1, :, m * LANES : (m + 1) * LANES].astype(F32)
            spread_to[pl.ds(2 * m, HALF_ROWS, stride=HALF_COLS), :] = jnp.where(
                first_half, a, roll64(b)
            )
            spread_to[pl.ds(2 * m + 1, HALF_ROWS, stride=HALF_COLS), :] = jnp.where(
                first_half, roll64(a), b
            )
    cot_waits = [wait for pair in range(PAIRS) for wait in halo_send(cot, 0, pair, True)]

    for c in range(FEATS):
        ref.pick_c[c * LANES : (c + 1) * LANES, :] = one_hot(iota((LANES, LANES), 1) == c)
    for pair in range(PAIRS):
        for half in range(2):
            for k in range(SLOTS):
                at = 16 * half + 3 * pair + k
                block = (half * SLOTS + k) * LANES
                along, _ = pixel_of(along_all[:, at : at + 1], along_all[:, at + 8 : at + 9])
                along = jnp.broadcast_to(along, (LANES, LANES))
                for m in range(4):
                    fetch[pair, block : block + LANES, m * LANES : (m + 1) * LANES] = one_hot(
                        iota((LANES, LANES), 1) + m * LANES == along
                    )
    lax.fori_loop(PARTS[0], PARTS[1], slopes, 0)

    norm1, f_waits, f_edges = [], [], []
    y2 = ref.y2
    for pair in range(PAIRS):
        e_waits[pair].wait_recv()
        for wait in e_edges[pair]:
            wait.wait_recv()
        center, factor = norm_of(summed(pair))
        norm1.append((center, factor))
        scaled = (y1[pair] - center) * factor
        pre = scaled * gain1 + bias1
        sigma = sigmoid(pre)
        edge = (ref.halo[1, pair] - center) * factor * gain1 + bias1
        fill_ext(0, pair, low(pre * sigma), low(edge * sigmoid(edge)) * halo_mask)
        for b in range(3):
            window = shifted(0, pair, b, range(EXT_ROWS))
            for a in range(3):
                t = 3 * a + b
                ref.im2[pair, :, t * LANES : (t + 1) * LANES] = jnp.concatenate(
                    window[a : a + HALF_ROWS], axis=0
                )
        value = dot_nn(ref.im2[pair], ref.wide2[...])
        y2[pair] = value
        f_waits.append(global_sums(2 + pair, column_sum(value), column_sum(value * value)))
        f_edges.append(halo_send(y2, 2, pair, True))
        ref.x1[pair] = scaled
        ref.s1[pair] = sigma * (1.0 + pre * (1.0 - sigma))

    lax.fori_loop(PARTS[1], PARTS[2], slopes, 0)

    norm2, g_waits = [], []
    for pair in range(PAIRS):
        f_waits[pair].wait_recv()
        center, factor = norm_of(summed(2 + pair))
        norm2.append((center, factor))
        scaled = (y2[pair] - center) * factor
        pre = scaled * gain2 + bias2
        sigma = sigmoid(pre)
        grad = cot[pair] * (sigma * (1.0 + pre * (1.0 - sigma)))
        g_waits.append(global_sums(4 + pair, column_sum(grad), column_sum(grad * scaled)))
        ref.x2[pair] = scaled
        ref.g2[pair] = grad
        ref.feat[pair] = pre * sigma

    for pair in range(PAIRS):
        grid = ref.feat.at[pair]
        for m in range(HALF_COLS // 2):
            a = grid[pl.ds(2 * m, HALF_ROWS, stride=HALF_COLS), :]
            b = grid[pl.ds(2 * m + 1, HALF_ROWS, stride=HALF_COLS), :]
            at = slice(m * LANES, (m + 1) * LANES)
            ref.features[2 * pair, :, at] = jnp.where(first_half, a, roll64(b)).astype(BF16)
            ref.features[2 * pair + 1, :, at] = jnp.where(first_half, roll64(a), b).astype(BF16)
    edges2 = []
    for pair in range(PAIRS):
        for wait in f_edges[pair] + cot_waits[8 * pair : 8 * pair + 8]:
            wait.wait_recv()
        center, factor = norm2[pair]
        scaled = (ref.halo[2, pair] - center) * factor
        pre = scaled * gain2 + bias2
        sigma = sigmoid(pre)
        edges2.append((scaled, ref.halo[0, pair] * (sigma * (1.0 + pre * (1.0 - sigma)))))
    lax.fori_loop(PARTS[2], PARTS[3], slopes, 0)

    total2, h_waits, h_edges = [], [], []
    for pair in range(PAIRS):
        g_waits[pair].wait_recv()
        sums = summed(4 + pair)
        total2.append(sums)
        scale = norm2[pair][1] * gain2
        mean_grad, mean_scaled = sums[0:1, :] / pixel_total, sums[1:2, :] / pixel_total
        inner = low(scale * (ref.g2[pair] - mean_grad - ref.x2[pair] * mean_scaled))
        edge_scaled, edge_grad = edges2[pair]
        edge = low(scale * (edge_grad - mean_grad - edge_scaled * mean_scaled)) * halo_mask
        ref.d2[pair] = inner.astype(BF16)
        fill_ext(1, pair, inner, edge)
        for b in range(3):
            window = shifted(1, pair, 2 - b, range(EXT_ROWS))
            for a in range(3):
                t = 3 * a + b
                ref.im3[pair, :, t * LANES : (t + 1) * LANES] = jnp.concatenate(
                    window[2 - a : 2 - a + HALF_ROWS], axis=0
                )
        grad = dot_nn(ref.im3[pair], ref.back2[...]) * ref.s1[pair]
        ref.g1[pair] = grad
        h_waits.append(global_sums(6 + pair, column_sum(grad), column_sum(grad * ref.x1[pair])))
        h_edges.append(halo_send(ref.g1, 3, pair, False))

    def kernel_grad(grads, windows):
        product = sum(dot_tn(grads[pair], windows[pair]) for pair in range(PAIRS))
        taps = [product[:, t * LANES : (t + 1) * LANES] for t in range(windows[0].shape[1] // LANES)]
        return [tap[0:CH, :] + roll64(tap[CH:LANES, :]) for tap in taps]

    def to_owners(index, grads):
        dk = ref.dk.at[index]
        for t in range(0, TAPS, 2):
            both = [grads[t], grads[min(t + 1, TAPS - 1)]]
            both = jnp.transpose(jnp.concatenate(both, axis=0))[0:CH, :]
            dk[t * CH : (t + 1) * CH, :] = both
            if t + 1 < TAPS:
                dk[(t + 1) * CH : (t + 2) * CH, :] = roll64(both)
        none = jnp.zeros((BLOCK - PIECE, LANES), F32)
        for i in range(n_rows):
            at = wire.peer(i)[0] * OWN_ROWS
            first = dk[pl.ds(pl.multiple_of(at, 8), PIECE), :]
            second = dk[pl.ds(pl.multiple_of(at + OWN_ROWS - PIECE, 8), PIECE), :]
            block = jnp.where(first_half, first, roll64(second))
            ref.g_send[index, i] = jnp.concatenate([block, none], axis=0).astype(BF16)
        ref.g_land[index, 0] = ref.g_send[index, 0]
        return wire.spread(
            n_rows,
            wire.peer,
            lambda i: ref.g_send.at[index, i],
            lambda i: ref.g_land.at[index, i],
            ref.g_land.at[index, pl.ds(1, n_rows - 1)],
        )

    lax.fori_loop(PARTS[3], 4 * SCENES, slopes, 0)
    grads2 = kernel_grad([ref.d2[0], ref.d2[1]], [ref.im2[0], ref.im2[1]])
    g_waits = [to_owners(1, grads2)]

    total1, y_waits = [], []
    for pair in range(PAIRS):
        h_waits[pair].wait_recv()
        for wait in h_edges[pair]:
            wait.wait_recv()
        sums = summed(6 + pair)
        total1.append(sums)
        center, factor = norm1[pair]
        scale = factor * gain1
        mean_grad, mean_scaled = sums[0:1, :] / pixel_total, sums[1:2, :] / pixel_total
        inner = low(scale * (ref.g1[pair] - mean_grad - ref.x1[pair] * mean_scaled))
        edge_scaled = (ref.halo[1, pair] - center) * factor
        edge = low(scale * (ref.halo[3, pair] - mean_grad - edge_scaled * mean_scaled))
        edge = jnp.where(halo_mask > 0.0, edge, 0.0)
        ref.d1[pair] = inner
        fill_ext(2, pair, inner, edge)
        here = shifted(2, pair, 1, range(1, EXT_ROWS))
        beside = shifted(2, pair, 2, range(1, EXT_ROWS))
        windows = [here[:HALF_ROWS], beside[:HALF_ROWS], here[1:], beside[1:]]
        for w in range(4):
            ref.im4[pair, :, w * LANES : (w + 1) * LANES] = jnp.concatenate(windows[w], axis=0)
        ref.back[pair] = dot_nn(ref.im4[pair], ref.back1[...]).astype(BF16)
        value = dot_nn(fetch[pair], ref.back[pair])
        y_send = ref.y_send.at[pair].reshape(128 * 8, LANES)
        chosen = []
        for block in range(2 * SLOTS):
            rows = slice(block * LANES, (block + 1) * LANES)
            picked = value[rows, 0:LANES] * parity[pair, rows, 0:LANES].astype(F32)
            for q in range(1, 4):
                tile = slice(q * LANES, (q + 1) * LANES)
                picked = picked + value[rows, tile] * parity[pair, rows, tile].astype(F32)
            chosen.append(picked)
        for k in range(SLOTS):
            y_send[pl.ds(k, 128, stride=8), :] = jnp.where(first_half, chosen[k], chosen[SLOTS + k])
        ref.y_land[pair, 0, 0:SLOTS, :] = ref.y_send[pair, 0, 0:SLOTS, :]
        y_waits.append(
            wire.spread(
                total,
                lambda i: wire.source(i),
                lambda i, pair=pair: ref.y_send.at[pair, i, pl.ds(0, SLOTS)],
                lambda i, pair=pair: ref.y_land.at[pair, i, pl.ds(0, SLOTS)],
                ref.y_land.at[pair, pl.ds(1, total - 1), pl.ds(0, SLOTS)],
            )
        )

    def owned_sum(index):
        return jnp.sum(ref.g_land[index].astype(F32), axis=0).astype(BF16)

    g_waits[0].wait_recv()
    ref.gx_land[0] = owned_sum(1)
    gx_wait = wire.spread(
        4,
        lambda i: wire.peer(i * 8),
        lambda i: ref.gx_land.at[0],
        lambda i: ref.gx_land.at[i],
        ref.gx_land.at[pl.ds(1, 3)],
    )
    own1 = [ref.d1[pair].astype(BF16) for pair in range(PAIRS)]
    beside1 = [
        ref.d1.at[pair][pl.ds(0, HALF_ROWS, stride=HALF_COLS), :].astype(BF16)
        for pair in range(PAIRS)
    ]
    grads = kernel_grad(own1, [ref.im1[0], ref.im1[1]])
    upper = kernel_grad([own[0:HALF_COLS, :] for own in own1], [ref.top1[0], ref.top1[1]])
    lefts = kernel_grad(beside1, [ref.left1[0], ref.left1[1]])
    for t in range(3):
        grads[t] = grads[t] + upper[t]
        grads[3 * t] = grads[3 * t] + lefts[t]
    g_waits.append(to_owners(0, grads))

    k_waits = []
    ones = jnp.ones((16, 2 * LANES), BF16)
    for pair in range(PAIRS):
        y_waits[pair].wait_recv()
        y_land = ref.y_land.at[pair].reshape(128 * 8, LANES)
        landed = [jnp.transpose(y_land[pl.ds(k, 128, stride=8), :]) for k in range(SLOTS)]
        landed = jnp.concatenate(landed, axis=1).astype(BF16)
        parts = [[], []]
        for half in range(2):
            s = 2 * pair + half
            pick = jnp.concatenate([hot[s * SLOTS + k] for k in range(SLOTS)], axis=0)
            grad = dot_nn(landed[half * CH : (half + 1) * CH, :], pick)
            ref.grads[s] = grad
            for kind in range(2):
                parts[kind].append(grad * ref.q_sum[s, kind])
        products = jnp.concatenate(parts[0] + parts[1], axis=0)
        coarse = low(products)
        products = jnp.concatenate([coarse, products - coarse], axis=1).astype(BF16)
        sums = dot_nt(ones, products)
        sums = (sums[0:1, 0:LANES], sums[0:1, LANES:])
        if pair == 0:
            k_waits.append(global_sums(8, *sums))
            for c in range(FEATS):
                ref.t_sum[0, c] = ref.grads[0] * ref.t_sum[0, c] + ref.grads[1] * ref.t_sum[1, c]
            gx_wait.wait_recv()
            ref.gz_land[0] = jnp.sum(ref.gx_land[...].astype(F32), axis=0).astype(BF16)
            gz_wait = wire.spread(
                4,
                lambda i: wire.peer(i * 32),
                lambda i: ref.gz_land.at[0],
                lambda i: ref.gz_land.at[i],
                ref.gz_land.at[pl.ds(1, 3)],
            )

    split = [[], []]
    for c in range(FEATS):
        product = ref.t_sum[0, c]
        for s in range(2, SCENES):
            product = product + ref.grads[s] * ref.t_sum[s, c]
        coarse = low(product)
        split[0].append(coarse)
        split[1].append(product - coarse)
    weight_grad = jnp.zeros((CH, LANES), F32)
    for part in split:
        weight_grad = weight_grad + dot_nn(
            jnp.concatenate(part, axis=1).astype(BF16), ref.pick_c[...]
        )
    ref.p_col[...] = weight_grad
    packed = jnp.zeros((8, LANES), F32)
    for k in range(8):
        packed = packed + pltpu.roll(ref.p_col[pl.ds(k, 8, stride=8), :], 16 * k, axis=1)
    for r in range(n_rows):
        ref.k_send[r, 0:1, :] = sums[0]
        ref.k_send[r, 1:2, :] = sums[1]
        ref.k_send[r, 2:3, :] = packed[r : r + 1, :]
        ref.k_send[r, 3:4, :] = packed[r : r + 1, :]
    ref.k_land[0] = ref.k_send[row]
    k_waits.append(
        wire.spread(
            total,
            wire.peer,
            lambda i: ref.k_send.at[wire.peer(i)[0]],
            lambda i: ref.k_land.at[i],
            ref.k_land.at[pl.ds(1, total - 1)],
        )
    )
    g_waits[1].wait_recv()
    ref.gc_land[0] = owned_sum(0)
    gc_wait = wire.spread(
        n_cols,
        wire.along_cols,
        lambda i: ref.gc_land.at[0],
        lambda i: ref.gc_land.at[i],
        ref.gc_land.at[pl.ds(1, n_cols - 1)],
    )

    def update(s):
        scaled_w = w_row * norm0[s][2]
        coarse = low(scaled_w)
        matrix = jnp.where(first_half, coarse, roll64(scaled_w - coarse)).astype(BF16)
        grad = ref.grads[s]
        for j in range(DEPTH // 4):
            block = [(ref.share[s, 4 * j + t] * grad).astype(BF16) for t in range(4)]
            block = jnp.concatenate(block, axis=1)
            ref.upd[s, :, j * 4 * LANES : (j + 1) * 4 * LANES] = dot_nn(
                matrix, jnp.concatenate([block, block], axis=0)
            )

    for s in range(SCENES):
        update(s)

    bias_sum, gain_sum = jnp.zeros((1, LANES), F32), jnp.zeros((1, LANES), F32)
    correction = jnp.zeros((16, LANES), F32)
    for pair in range(PAIRS):
        k_waits[pair].wait_recv()
        sums = jnp.sum(ref.k_land[...], axis=0) if pair else summed(8)
        for half in range(2):
            s = 2 * pair + half
            center, factor, scale, count, cross, products = norm0[s]
            own = jnp.where(first_half, roll64(sums) if half else sums, 0.0)
            grad_sum = own[0:1, :]
            scaled_sum = factor * (own[1:2, :] - center * grad_sum)
            bias_sum, gain_sum = bias_sum + grad_sum, gain_sum + scaled_sum
            grad_mean, scaled_mean = grad_sum / count, scaled_sum / count
            point_sums = products[:, 9:10]
            correction = correction + scale * (
                grad_mean * point_sums + scaled_mean * factor * (cross - center * point_sums)
            )
            unit = w_row * factor - jnp.where(feature_row == FEATS, center * factor, 0.0)
            unit = unit * scaled_mean + jnp.where(feature_row == FEATS, grad_mean, 0.0)
            mix = dot_nt(w_row * scale, unit, HIGH)
            coarse = low(mix)
            mix = jnp.concatenate([coarse, mix - coarse], axis=1).astype(BF16)
            out = ref.point_grads.at[s]
            points = aug[s]
            value = ref.upd[s] - dot_nn(mix, jnp.concatenate([points, points], axis=0))
            for n in range(DEPTH):
                at = slice(n * LANES, (n + 1) * LANES)
                out[pl.ds(n, 8, stride=DEPTH), :] = value[0:8, at]
                out[8 * DEPTH + n : 8 * DEPTH + n + 1, :] = value[8:9, at]

    def own_lanes(values):
        return pltpu.roll(values, lax.rem(LANES - 8 * row, LANES), axis=1)

    def both_scenes(values, index):
        added = values[0][index : index + 1, :] + values[1][index : index + 1, :]
        return added + roll64(added)

    small = ref.small
    small[...] = jnp.zeros((8, LANES), F32)
    small[0:1, :] = bias_sum
    small[1:2, :] = both_scenes(total1, 0)
    small[2:3, :] = both_scenes(total2, 0)
    small[3:4, :] = gain_sum
    small[4:5, :] = both_scenes(total1, 1)
    small[5:6, :] = both_scenes(total2, 1)
    owned = own_lanes(small[...])
    ref.bias_grad[...] = owned[0:3, 0:8]
    ref.gain_grad[...] = owned[3:6, 0:8]
    correction = jnp.transpose(square_of(own_lanes(correction)))
    block = [pltpu.roll(sums[2:3, :], (LANES - 16 * k) % LANES, axis=1) for k in range(8)]
    block = jnp.concatenate(block, axis=0)
    ref.pfn_grad[...] = (block - correction[0:8, :])[:, 0:FEATS]
    for index, (wait, land) in enumerate([(gc_wait, ref.gc_land), (gz_wait, ref.gz_land)]):
        wait.wait_recv()
        block = jnp.transpose(square_of(jnp.sum(land[...].astype(F32), axis=0)))
        ref.conv_grad[index, :, 0:PIECE] = block[0:CH, 0:PIECE]
        ref.conv_grad[index, :, OWN_ROWS - PIECE :] = block[CH:LANES, 0:PIECE]
    wire.settle()


def result_kernel(*refs):
    sems = refs[-1]
    copies = [
        pltpu.make_async_copy(refs[i], refs[RESULTS + i], sems.at[i]) for i in range(RESULTS)
    ]
    for copy in copies:
        copy.start()
    for copy in copies:
        copy.wait()


def body(points, counts, tiles, cells, pfn_weight, conv_weight, norm_gain, norm_bias, cotangent):
    scenes, feats, depth, pillars = points.shape
    n_rows, n_cols = lax.axis_size("rows"), lax.axis_size("cols")
    anywhere = pl.BlockSpec(memory_space=pl.ANY)
    inside = pl.BlockSpec(memory_space=pltpu.VMEM)
    shapes = [
        jax.ShapeDtypeStruct(cotangent.shape, BF16),
        jax.ShapeDtypeStruct((scenes, feats * depth, pillars), F32),
        jax.ShapeDtypeStruct(pfn_weight.shape[::-1], F32),
        jax.ShapeDtypeStruct((2, CH, OWN_ROWS), F32),
        jax.ShapeDtypeStruct(norm_gain.shape, F32),
        jax.ShapeDtypeStruct(norm_bias.shape, F32),
    ]
    results = pl.pallas_call(
        functools.partial(step_kernel, n_rows, n_cols),
        out_shape=[pltpu.VMEM(shape.shape, shape.dtype) for shape in shapes],
        in_specs=[anywhere] * INPUTS,
        out_specs=[inside] * RESULTS,
        scratch_shapes=[pltpu.VMEM(shape, dtype) for shape, dtype in SCRATCH.values()]
        + [
            pltpu.SemaphoreType.DMA((SEMS,)),
            pltpu.SemaphoreType.DMA((SEMS,)),
            pltpu.SemaphoreType.DMA((INPUTS,)),
        ],
        compiler_params=pltpu.CompilerParams(
            collective_id=0, has_side_effects=True, vmem_limit_bytes=54 * 2**20
        ),
    )(
        points.reshape(scenes, feats * depth, pillars),
        counts,
        tiles.reshape(scenes, pillars),
        cells,
        pfn_weight.T,
        conv_weight.transpose(0, 2, 1),
        norm_gain,
        norm_bias,
        cotangent,
    )
    results = pl.pallas_call(
        result_kernel,
        out_shape=shapes,
        in_specs=[inside] * RESULTS,
        out_specs=[anywhere] * RESULTS,
        scratch_shapes=[pltpu.SemaphoreType.DMA((RESULTS,))],
    )(*[pltpu.with_memory_space_constraint(result, pltpu.VMEM) for result in results])
    return (
        results[0],
        results[1].reshape(points.shape),
        results[2].T,
        results[3].transpose(0, 2, 1),
        results[4],
        results[5],
    )


def solution(mesh):
    in_specs = (
        P(None, None, None, ("rows", "cols")),
        P(None, ("rows", "cols")),
        P(None, ("rows", "cols"), None),
        P(None, ("rows", "cols")),
        P(None, "rows"),
        P(None, "rows", None),
        P(None, "rows"),
        P(None, "rows"),
        P(None, "rows", "cols"),
    )
    out_specs = (
        P(None, "rows", "cols"),
        P(None, None, None, ("rows", "cols")),
        P(None, "rows"),
        P(None, "rows", None),
        P(None, "rows"),
        P(None, "rows"),
    )
    return jax.shard_map(body, mesh=mesh, in_specs=in_specs, out_specs=out_specs, check_vma=False)
```

```python
import functools
import types

import jax
import jax.numpy as jnp
from jax import lax
from jax.experimental import pallas as pl
from jax.experimental.pallas import tpu as pltpu
from jax.sharding import PartitionSpec as P

EPSILON = 1e-05
HIGH = lax.Precision.HIGHEST
MESH = pl.DeviceIdType.MESH
F32, BF16, I32 = jnp.float32, jnp.bfloat16, jnp.int32

SCENES = 4
PAIRS = 2
FEATS = 9
DEPTH = 32
PILLARS = 128
CH = 64
LANES = 128
HALF_ROWS = 32
HALF_COLS = 16
PIXELS = HALF_ROWS * HALF_COLS
SLOTS = 3
EDGE = 8
EXT_COLS = 32
EXT_ROWS = HALF_ROWS + 2
TAPS = 9
OWN_ROWS = 72
PAD_ROWS = 80
PIECE = 40
UNROLL = 4
PARTS = (0, 4, 10, 13)
BLOCK = 48


def dot_nn(a, b, precision=None):
    return lax.dot_general(
        a, b, (((1,), (0,)), ((), ())), precision=precision, preferred_element_type=F32
    )


def dot_nt(a, b, precision=None):
    return lax.dot_general(
        a, b, (((1,), (1,)), ((), ())), precision=precision, preferred_element_type=F32
    )


def dot_tn(a, b):
    return lax.dot_general(a, b, (((0,), (0,)), ((), ())), preferred_element_type=F32)


def iota(shape, dim):
    return lax.broadcasted_iota(I32, shape, dim)


def sigmoid(v):
    return 0.5 * jnp.tanh(0.5 * v) + 0.5


def low(v):
    return v.astype(BF16).astype(F32)


def one_hot(mask):
    return jnp.where(mask, 1.0, 0.0).astype(BF16)


def square_of(v):
    rows, cols = v.shape
    if cols < LANES:
        v = jnp.concatenate([v, jnp.zeros((rows, LANES - cols), v.dtype)], axis=1)
    return jnp.concatenate([v, jnp.zeros((LANES - rows, LANES), v.dtype)], axis=0)


def roll64(v):
    return pltpu.roll(v, CH, axis=1)


SCRATCH = dict(
    points=((SCENES, FEATS * DEPTH, LANES), BF16),
    counts=((SCENES, LANES), I32),
    tiles=((SCENES, LANES), I32),
    cells=((SCENES, LANES), I32),
    pfn=((8, FEATS), BF16),
    conv=((2, CH, OWN_ROWS), BF16),
    gain=((3, 8), BF16),
    bias=((3, 8), BF16),
    cotangent=((SCENES, HALF_ROWS, HALF_COLS * CH), BF16),
    square=((LANES, LANES), F32),
    w_tmp=((16, LANES), F32),
    w_send=((16, LANES), F32),
    w_land=((8, 16, LANES), F32),
    c_send=((PAD_ROWS, LANES), BF16),
    c_land=((8, PAD_ROWS, LANES), BF16),
    taps=((TAPS * CH, LANES), F32),
    wide1=((TAPS * LANES, LANES), BF16),
    side1=((3 * LANES, LANES), BF16),
    wide2=((TAPS * LANES, LANES), BF16),
    back2=((TAPS * LANES, LANES), BF16),
    back1=((4 * LANES, 4 * LANES), BF16),
    pts32=((SCENES, 16 * DEPTH, LANES), F32),
    aug=((SCENES, 16, DEPTH * LANES), BF16),
    hot=((SCENES * SLOTS, LANES, LANES), BF16),
    m_send=((2, 4, LANES), F32),
    m_land=((8, 4, LANES), F32),
    m2_land=((16, 4, LANES), F32),
    hello=((4, 4, LANES), F32),
    spots=((LANES, LANES), F32),
    cell_send=((8, 16, LANES), F32),
    cell_land=((8, 16, LANES), F32),
    cell2_send=((16, 8, LANES), F32),
    cell2_land=((16, 8, LANES), F32),
    gram=((SCENES * 16, LANES), F32),
    place=((PAIRS, PIXELS, 6 * LANES), BF16),
    rim=((PAIRS, 48, 6 * LANES), BF16),
    parity=((PAIRS, 6 * LANES, 4 * LANES), BF16),
    fetch=((PAIRS, 6 * LANES, PIXELS), BF16),
    linear=((SCENES, DEPTH, CH, LANES), F32),
    halves=((SCENES, 2, CH, LANES), F32),
    act=((SCENES, DEPTH, CH, LANES), F32),
    share=((SCENES, DEPTH, CH, LANES), F32),
    pil=((SCENES, CH, LANES), F32),
    t_sum=((SCENES, FEATS, CH, LANES), F32),
    q_sum=((SCENES, 2, CH, LANES), F32),
    x_send=((PAIRS, 128, 8, LANES), F32),
    x_land=((PAIRS, 128, 8, LANES), F32),
    y_send=((PAIRS, 128, 8, LANES), F32),
    y_land=((PAIRS, 128, 8, LANES), F32),
    rim_send=((PAIRS, 2, 48, LANES), F32),
    rim_land=((PAIRS, 2, 56, LANES), F32),
    im1=((PAIRS, PIXELS, TAPS * LANES), BF16),
    top1=((PAIRS, 16, 3 * LANES), BF16),
    left1=((PAIRS, 32, 3 * LANES), BF16),
    im2=((PAIRS, PIXELS, TAPS * LANES), BF16),
    im3=((PAIRS, PIXELS, TAPS * LANES), BF16),
    im4=((PAIRS, PIXELS, 4 * LANES), BF16),
    back=((PAIRS, PIXELS, 4 * LANES), BF16),
    pick_c=((FEATS * LANES, LANES), BF16),
    y1=((PAIRS, PIXELS, LANES), F32),
    y2=((PAIRS, PIXELS, LANES), F32),
    x1=((PAIRS, PIXELS, LANES), F32),
    x2=((PAIRS, PIXELS, LANES), F32),
    s1=((PAIRS, PIXELS, LANES), F32),
    g1=((PAIRS, PIXELS, LANES), F32),
    g2=((PAIRS, PIXELS, LANES), F32),
    feat=((PAIRS, PIXELS, LANES), F32),
    cot=((PAIRS, PIXELS, LANES), F32),
    d1=((PAIRS, PIXELS, LANES), F32),
    d2=((PAIRS, PIXELS, LANES), BF16),
    cols=((4, PAIRS, 2, HALF_ROWS, LANES), F32),
    halo=((4, PAIRS, LANES, LANES), F32),
    ext=((3, PAIRS, EXT_ROWS * EXT_COLS, LANES), F32),
    st_send=((10, 2, LANES), F32),
    st_land=((10, 128, 2, LANES), F32),
    grads=((SCENES, CH, LANES), F32),
    p_col=((CH, LANES), F32),
    k_send=((8, 8, LANES), F32),
    k_land=((128, 8, LANES), F32),
    dk=((2, TAPS * CH, LANES), F32),
    g_send=((2, 8, BLOCK, LANES), BF16),
    g_land=((2, 8, BLOCK, LANES), BF16),
    gx_land=((4, BLOCK, LANES), BF16),
    gz_land=((4, BLOCK, LANES), BF16),
    gc_land=((16, BLOCK, LANES), BF16),
    upd=((SCENES, 16, DEPTH * LANES), F32),
    small=((8, LANES), F32),
)
INPUTS = 9
RESULTS = 6
SEMS = 96


HIGH_BITS, LOW_BITS = 0b1010101, 0b0101010


def digits_add(a, b):
    carried = jnp.bitwise_and(a, LOW_BITS) + jnp.bitwise_and(b, LOW_BITS)
    return jnp.bitwise_xor(carried, jnp.bitwise_and(jnp.bitwise_xor(a, b), HIGH_BITS))


def digits_sub(a, b):
    borrowed = jnp.bitwise_or(a, HIGH_BITS) - jnp.bitwise_and(b, LOW_BITS)
    kept = jnp.bitwise_and(jnp.bitwise_xor(jnp.bitwise_xor(a, b), HIGH_BITS), HIGH_BITS)
    return jnp.bitwise_xor(borrowed, kept)


def far_first(step):
    return jnp.bitwise_xor(step, jnp.bitwise_and(jnp.right_shift(step, 1), LOW_BITS))


class Wire:
    def __init__(self, n_rows, n_cols, send_sems, recv_sems):
        self.n_rows, self.n_cols = n_rows, n_cols
        self.total = n_rows * n_cols
        self.row, self.col = lax.axis_index("rows"), lax.axis_index("cols")
        self.me = self.col * n_rows + self.row
        self.send_sems, self.recv_sems = send_sems, recv_sems
        self.used = 0
        self.sent = []

    def place(self, number):
        return (
            jnp.bitwise_and(number, self.n_rows - 1),
            jnp.right_shift(number, self.n_rows.bit_length() - 1),
        )

    def peer(self, step):
        return self.place(digits_add(self.me, step))

    def source(self, step):
        return self.place(digits_sub(self.me, step))

    def along_cols(self, step):
        return self.peer(step * self.n_rows)

    def near(self, down, right):
        return (
            lax.rem(self.row + down + self.n_rows, self.n_rows),
            lax.rem(self.col + right + self.n_cols, self.n_cols),
        )

    def copy(self, src, dst, sem, peer):
        return pltpu.make_async_remote_copy(
            src_ref=src,
            dst_ref=dst,
            send_sem=self.send_sems.at[sem],
            recv_sem=self.recv_sems.at[sem],
            device_id=peer,
            device_id_type=MESH,
        )

    def one(self, src, dst, peer):
        sem = self.used
        self.used += 1
        copy = self.copy(src, dst, sem, peer)
        copy.start()
        self.sent.append(copy)
        return copy

    def spread(self, count, peer_of, src_of, dst_of, whole):
        sem = self.used
        self.used += 1

        def step(j, carry):
            i = far_first(count - j)
            self.copy(src_of(i), dst_of(i), sem, peer_of(i)).start()
            return carry

        lax.fori_loop(1, count, step, 0, unroll=8)
        copy = self.copy(whole, whole, sem, peer_of(1))
        self.sent.append(copy)
        return copy

    def local(self, src, dst, sems, index):
        copy = pltpu.make_async_copy(src, dst, sems.at[index])
        copy.start()
        return copy

    def settle(self):
        for copy in self.sent:
            copy.wait_send()


def step_kernel(n_rows, n_cols, *refs):
    inputs, results = refs[:INPUTS], refs[INPUTS : INPUTS + RESULTS]
    ref = types.SimpleNamespace(**dict(zip(SCRATCH, refs[INPUTS + RESULTS :], strict=False)))
    ref.features, ref.point_grads, ref.pfn_grad, ref.conv_grad, ref.gain_grad, ref.bias_grad = results
    send_sems, recv_sems, in_sems = refs[-3:]
    wire = Wire(n_rows, n_cols, send_sems, recv_sems)
    total, row, col, me = wire.total, wire.row, wire.col, wire.me
    lane = iota((1, LANES), 1)
    first_half = lane < CH

    barrier = pltpu.get_barrier_semaphore()

    lines = [i for i in range(1, n_rows)] + [i * 8 for i in (1, 2, 3)] + [i * 32 for i in (1, 2, 3)]
    for step in lines:
        pl.semaphore_signal(barrier, inc=1, device_id=wire.peer(step), device_id_type=MESH)
    held = [
        ref.points, ref.counts, ref.tiles, ref.cells, ref.pfn, ref.conv, ref.gain, ref.bias,
        ref.cotangent,
    ]
    order = [1, 0, 2, 3, 4, 6, 7, 5, 8]
    loads = {i: wire.local(inputs[i], held[i], in_sems, i) for i in order}
    for i in range(INPUTS):
        loads[i].wait()
    pts32, aug = ref.pts32, ref.aug
    slot_number = iota((DEPTH, LANES), 0)
    for s in range(SCENES):
        valid = slot_number < ref.counts[s : s + 1, :]
        for c in range(FEATS):
            block = ref.points[s, c * DEPTH : (c + 1) * DEPTH, :].astype(F32)
            pts32[s, c * DEPTH : (c + 1) * DEPTH, :] = jnp.where(valid, block, 0.0)
        pts32[s, FEATS * DEPTH : (FEATS + 1) * DEPTH, :] = jnp.where(valid, 1.0, 0.0)
        pts32[s, (FEATS + 1) * DEPTH :, :] = jnp.zeros((6 * DEPTH, LANES), F32)
        scene_pts = pts32.at[s]
        for n in range(DEPTH):
            aug[s, :, n * LANES : (n + 1) * LANES] = scene_pts[pl.ds(n, 16, stride=DEPTH), :].astype(
                BF16
            )
    stacked = jnp.concatenate([aug[s] for s in range(SCENES)], axis=0)
    gram_all = dot_nt(stacked, jnp.concatenate([stacked, stacked], axis=0))
    moments = jnp.zeros((4, LANES), F32)
    for s in range(SCENES):
        for b in range(3):
            piece = gram_all[16 * s + 4 * b : 16 * s + 4 * b + 4, :]
            at = 40 * b + 10 * s
            piece = pltpu.roll(piece, (at - 16 * s) % LANES, axis=1)
            moments = moments + jnp.where((lane >= at) & (lane < at + 10), piece, 0.0)

    hot = ref.hot
    above = iota((LANES, LANES), 0) < iota((LANES, LANES), 1)
    slot_row = iota((LANES, LANES), 0).astype(F32) * 4.0
    for s in range(SCENES):
        tile = ref.tiles[s : s + 1, :]
        tile = jnp.bitwise_and(tile, n_cols - 1) * n_rows + jnp.right_shift(
            tile, n_cols.bit_length() - 1
        )
        tile = digits_sub(tile, me).astype(F32)
        wide = jnp.broadcast_to(tile, (LANES, LANES))
        same = (jnp.transpose(wide) == wide) & above
        rank = jnp.sum(jnp.where(same, 1.0, 0.0), axis=0, keepdims=True)
        code = tile * 4.0 + rank
        for k in range(SLOTS):
            hot[s * SLOTS + k] = one_hot(slot_row + float(k) == code)

    lane_row = iota((LANES, LANES), 0)
    spots = jnp.zeros((LANES, LANES), F32)
    for q in range(4):
        for pair in range(PAIRS):
            s = 2 * pair + q // 2
            cell = ref.cells[s : s + 1, :]
            spot = (jnp.bitwise_and(cell, 31) if q % 2 else jnp.right_shift(cell, 5)) + 1
            for k in range(SLOTS):
                at = jnp.where(lane_row == q * 8 + 3 * pair + k, spot.astype(F32), 0.0)
                spots = spots + dot_nt(hot[s * SLOTS + k], at.astype(BF16))
    ref.spots[...] = spots
    for i in range(n_rows):
        ref.cell_send[i] = ref.spots[pl.ds(i, n_cols, stride=n_rows), :]
    ref.cell_land[0] = ref.cell_send[0]
    ref.m_send[0] = moments
    ref.m_land[0] = moments
    ref.hello[0] = moments

    ref.square[...] = jnp.zeros((LANES, LANES), F32)
    ref.square[0:8, 0:FEATS] = ref.pfn[...].astype(F32)
    ref.w_tmp[...] = jnp.transpose(ref.square[...])[0:16, :]
    ref.w_tmp[9:12, 0:8] = ref.gain[...].astype(F32)
    ref.w_tmp[12:15, 0:8] = ref.bias[...].astype(F32)
    ref.w_send[...] = pltpu.roll(ref.w_tmp[...], row * 8, axis=1)
    ref.w_land[0] = ref.w_send[...]
    pl.semaphore_wait(barrier, len(lines))
    m_wait = wire.spread(
        n_rows,
        wire.peer,
        lambda i: ref.m_send.at[0],
        lambda i: ref.m_land.at[i],
        ref.m_land.at[pl.ds(1, n_rows - 1)],
    )
    hello_wait = wire.spread(
        4,
        lambda i: wire.peer(i * 8),
        lambda i: ref.hello.at[0],
        lambda i: ref.hello.at[i],
        ref.hello.at[pl.ds(1, 3)],
    )
    w_wait = wire.spread(
        n_rows,
        wire.peer,
        lambda i: ref.w_send,
        lambda i: ref.w_land.at[i],
        ref.w_land.at[pl.ds(1, n_rows - 1)],
    )
    m_wait.wait_recv()
    hello_wait.wait_recv()
    moments = jnp.sum(ref.m_land[...], axis=0)
    ref.m_send[1] = moments
    ref.m2_land[0] = moments
    m2_wait = wire.spread(
        n_cols,
        wire.along_cols,
        lambda i: ref.m_send.at[1],
        lambda i: ref.m2_land.at[i],
        ref.m2_land.at[pl.ds(1, n_cols - 1)],
    )

    cell_wait = wire.spread(
        n_rows,
        wire.peer,
        lambda i: ref.cell_send.at[i],
        lambda i: ref.cell_land.at[i],
        ref.cell_land.at[pl.ds(1, n_rows - 1)],
    )

    def halo_send(values, index, pair, full):
        cols, halo = ref.cols.at[index, pair], ref.halo.at[index, pair]
        inner = values.at[pair]
        for side in range(2 if full else 1):
            cols[side] = inner[pl.ds(side * (HALF_COLS - 1), HALF_ROWS, stride=HALF_COLS), :]

        def send(src, start, count, at, down, right):
            return wire.one(
                src.at[pl.ds(start, count)], halo.at[pl.ds(at, count)], wire.near(down, right)
            )

        waits = [
            send(inner, 0, 8, 120, -1, -1),
            send(cols.at[0], 0, 32, 64, 0, -1),
            send(inner, 0, 16, 16, -1, 0),
        ]
        if full:
            waits += [
                send(inner, 504, 8, 96, 1, 1),
                send(inner, 8, 8, 112, -1, 1),
                send(inner, 496, 8, 104, 1, -1),
                send(cols.at[1], 0, 32, 32, 0, 1),
                send(inner, 496, 16, 0, 1, 0),
            ]
        return waits

    def there(cond):
        return jnp.where(cond, 1.0, 0.0)

    up, down = there(row > 0), there(row < n_rows - 1)
    left, right = there(col > 0), there(col < n_cols - 1)
    spot = iota((LANES, LANES), 0)
    halo_mask = jnp.where(spot < 16, up, jnp.where(spot < 32, down, jnp.where(spot < 64, left, right)))
    halo_mask = jnp.where(spot < 96, halo_mask, jnp.where(spot < 112, up, down))
    halo_mask = jnp.where(
        spot < 96,
        halo_mask,
        halo_mask * jnp.where((spot < 104) | ((spot >= 112) & (spot < 120)), left, right),
    )

    def fill_ext(index, pair, inner, edge):
        grid = ref.ext.at[index, pair]
        for i in range(HALF_ROWS):
            at = (i + 1) * EXT_COLS + EDGE
            grid[at : at + HALF_COLS, :] = inner[i * HALF_COLS : (i + 1) * HALF_COLS, :]
        grid[EDGE : EDGE + HALF_COLS, :] = edge[0:16, :]
        last = (EXT_ROWS - 1) * EXT_COLS
        grid[last + EDGE : last + EDGE + HALF_COLS, :] = edge[16:32, :]
        grid[pl.ds(EXT_COLS + EDGE - 1, HALF_ROWS, stride=EXT_COLS), :] = edge[32:64, :]
        grid[pl.ds(EXT_COLS + EDGE + HALF_COLS, HALF_ROWS, stride=EXT_COLS), :] = edge[64:96, :]
        grid[EDGE - 1 : EDGE, :] = edge[103:104, :]
        grid[EDGE + HALF_COLS : EDGE + HALF_COLS + 1, :] = edge[104:105, :]
        grid[last + EDGE - 1 : last + EDGE, :] = edge[119:120, :]
        grid[last + EDGE + HALF_COLS : last + EDGE + HALF_COLS + 1, :] = edge[120:121, :]

    def shifted(index, pair, shift, rows):
        grid = ref.ext.at[index, pair]
        start = EDGE - 1 + shift
        return [
            grid[i * EXT_COLS + start : i * EXT_COLS + start + HALF_COLS, :].astype(BF16)
            for i in rows
        ]

    def column_sum(v):
        return jnp.sum(v, axis=0, keepdims=True)

    def global_sums(index, first, second):
        send, land = ref.st_send.at[index], ref.st_land.at[index]
        send[0:1, :] = first
        send[1:2, :] = second
        land[0] = send[...]
        return wire.spread(
            total,
            wire.peer,
            lambda i: send,
            lambda i: land.at[i],
            land.at[pl.ds(1, total - 1)],
        )

    def summed(index):
        return jnp.sum(ref.st_land[index], axis=0)

    pixel_total = float(PIXELS * total)

    def norm_of(sums):
        center = sums[0:1, :] / pixel_total
        spread = sums[1:2, :] / pixel_total - center * center
        return center, lax.rsqrt(spread + EPSILON)

    ref.square[:, 0:OWN_ROWS] = jnp.concatenate(
        [ref.conv[0].astype(F32), ref.conv[1].astype(F32)], axis=0
    )
    ref.c_send[...] = jnp.transpose(ref.square[...])[0:PAD_ROWS, :].astype(BF16)
    ref.c_land[0] = ref.c_send[...]
    w_wait.wait_recv()
    w_full = jnp.sum(ref.w_land[...], axis=0)
    feature_row = iota((16, LANES), 0)
    w_row = jnp.where(feature_row < FEATS, w_full, 0.0)
    matrix = jnp.transpose(square_of(w_row))[0:CH, 0:16].astype(BF16)
    STEP = 8
    for s in range(SCENES):
        for j in range(DEPTH // STEP):
            value = dot_nn(matrix, aug[s, :, j * STEP * LANES : (j + 1) * STEP * LANES])
            for t in range(STEP):
                ref.linear[s, STEP * j + t] = value[:, t * LANES : (t + 1) * LANES]
    cell_wait.wait_recv()
    cell_land = ref.cell_land.reshape(n_rows * n_cols, LANES)
    for i in range(n_cols):
        ref.cell2_send[i] = cell_land[pl.ds(i, n_rows, stride=n_cols), :]
    ref.cell2_land[0] = ref.cell2_send[0]
    cell2_wait = wire.spread(
        n_cols,
        wire.along_cols,
        lambda i: ref.cell2_send.at[i],
        lambda i: ref.cell2_land.at[i],
        ref.cell2_land.at[pl.ds(1, n_cols - 1)],
    )
    m2_wait.wait_recv()


    def twice(v):
        return v + roll64(v)

    gain0, bias0 = w_full[9:10, :], w_full[12:13, :]
    gain1, bias1 = twice(w_full[10:11, :]), twice(w_full[13:14, :])
    gain2, bias2 = twice(w_full[11:12, :]), twice(w_full[14:15, :])
    moments = jnp.sum(ref.m2_land[...], axis=0)
    gram = ref.gram
    gram[...] = jnp.zeros((SCENES * 16, LANES), F32)
    for s in range(SCENES):
        for b in range(3):
            piece = pltpu.roll(moments, (LANES - 40 * b - 10 * s) % LANES, axis=1)
            at = 16 * s + 4 * b
            gram[at : at + 4, :] = jnp.where(lane < 10, piece, 0.0)
    crosses = dot_nn(gram[:, 0:16], w_row, HIGH)
    norm0, columns = [], []
    for s in range(SCENES):
        products, cross = gram[16 * s : 16 * s + 16, :], crosses[16 * s : 16 * s + 16, :]
        count = products[9:10, 9:10]
        center = cross[9:10, :] / count
        spread = column_sum(w_row * cross) / count - center * center
        factor = lax.rsqrt(spread + EPSILON)
        scale = factor * gain0
        norm0.append((center, factor, scale, count, cross, products))
        columns += [scale, 0.5 * scale, 0.5 * (bias0 - center * scale)]
    columns = jnp.transpose(square_of(jnp.concatenate(columns, axis=0)))[0:CH, :]
    for s in range(SCENES):
        for kind in range(2):
            at = 3 * s + 1 + kind
            ref.halves[s, kind] = jnp.broadcast_to(columns[:, at : at + 1], (CH, LANES))

    x_waits = []
    for pair in range(PAIRS):
        for s in (2 * pair, 2 * pair + 1):
            bound = ref.counts[s : s + 1, :]
            half_scale, half_shift = ref.halves[s, 0], ref.halves[s, 1]
            peak = jnp.full((CH, LANES), -1e30, F32)
            for n in range(DEPTH):
                half = ref.linear[s, n] * half_scale + half_shift
                active = jnp.where(n < bound, half * jnp.tanh(half) + half, -1e30)
                ref.act[s, n] = active
                peak = jnp.maximum(peak, active)
            whole = jnp.zeros((CH, LANES), F32)
            for n in range(DEPTH):
                whole = whole + jnp.exp(ref.act[s, n] - peak)
            ref.pil[s] = peak + jnp.log(whole)
        x_send = ref.x_send.at[pair].reshape(128 * 8, LANES)
        a, b = ref.pil[2 * pair].astype(BF16), ref.pil[2 * pair + 1].astype(BF16)
        none = jnp.zeros((CH, LANES), BF16)
        both = jnp.concatenate(
            [jnp.concatenate([a, none], axis=1), jnp.concatenate([none, b], axis=1)], axis=0
        )
        for k in range(SLOTS):
            pick = jnp.concatenate(
                [hot[2 * pair * SLOTS + k], hot[(2 * pair + 1) * SLOTS + k]], axis=1
            )
            x_send[pl.ds(k, 128, stride=8), :] = dot_nt(pick, both)
        ref.x_land[pair, 0, 0:SLOTS, :] = ref.x_send[pair, 0, 0:SLOTS, :]
        x_waits.append(
            wire.spread(
                total,
                wire.peer,
                lambda i, pair=pair: ref.x_send.at[pair, i, pl.ds(0, SLOTS)],
                lambda i, pair=pair: ref.x_land.at[pair, i, pl.ds(0, SLOTS)],
                ref.x_land.at[pair, pl.ds(1, total - 1), pl.ds(0, SLOTS)],
            )
        )

    c_wait = wire.spread(
        n_rows,
        wire.peer,
        lambda i: ref.c_send,
        lambda i: ref.c_land.at[i],
        ref.c_land.at[pl.ds(1, n_rows - 1)],
    )

    def slopes(step, carry):
        s, block = step // 4, lax.rem(step, 4)
        rows = pl.ds(pl.multiple_of(block * 16, 16), 16)
        top = ref.pil[s, rows, :]
        half_scale, half_shift = ref.halves[s, 0, rows, :], ref.halves[s, 1, rows, :]

        def inner(j, sums):
            sums = list(sums)
            for t in range(UNROLL):
                n = UNROLL * j + t
                line, active = ref.linear[s, n, rows, :], ref.act[s, n, rows, :]
                half = line * half_scale + half_shift
                turn = jnp.tanh(half)
                share = jnp.exp(active - top) * ((0.5 + 0.5 * turn) * (1.0 + half * (1.0 - turn)))
                ref.share[s, n, rows, :] = share
                sums[0] = sums[0] + share
                sums[1] = sums[1] + share * line
                for c in range(FEATS):
                    sums[2 + c] = sums[2 + c] + share * pts32[s, pl.ds(c * DEPTH + n, 1), :]
            return tuple(sums)

        zero = jnp.zeros((16, LANES), F32)
        sums = lax.fori_loop(0, DEPTH // UNROLL, inner, (zero,) * (2 + FEATS))
        ref.q_sum[s, 0, rows, :] = sums[0]
        ref.q_sum[s, 1, rows, :] = sums[1]
        for c in range(FEATS):
            ref.t_sum[s, c, rows, :] = sums[2 + c] * (2.0 * half_scale)
        return carry

    cell2_wait.wait_recv()
    along_all = ref.cell2_land[...].reshape(LANES, LANES)
    across_all = jnp.transpose(along_all)
    place, rim, parity, fetch = ref.place, ref.rim, ref.parity, ref.fetch

    def pixel_of(tall, wide):
        i, j = tall.astype(I32) - 1, wide.astype(I32) - 1
        pixel = jnp.right_shift(i, 1) * HALF_COLS + jnp.right_shift(j, 1)
        plane = 2 * jnp.bitwise_and(i, 1) + jnp.bitwise_and(j, 1)
        return jnp.where(i < 0, -1, pixel), jnp.where(i < 0, -1, plane)

    rim_pixel = iota((48, LANES), 0)
    rim_pixel = jnp.where(rim_pixel < 16, 496 + rim_pixel, rim_pixel * 16 - 241)
    for pair in range(PAIRS):
        for half in range(2):
            for k in range(SLOTS):
                at = 16 * half + 3 * pair + k
                block = (half * SLOTS + k) * LANES
                blocks = slice(block, block + LANES)
                across, _ = pixel_of(across_all[at : at + 1, :], across_all[at + 8 : at + 9, :])
                _, along = pixel_of(along_all[:, at : at + 1], along_all[:, at + 8 : at + 9])
                along = jnp.broadcast_to(along, (LANES, LANES))
                for m in range(4):
                    tile = slice(m * LANES, (m + 1) * LANES)
                    place[pair, tile, blocks] = one_hot(
                        iota((LANES, LANES), 0) + m * LANES == across
                    )
                    parity[pair, blocks, tile] = one_hot(along == m)
                rim[pair, :, blocks] = one_hot(rim_pixel == across)

    lax.fori_loop(0, PARTS[0], slopes, 0)

    planes_of, d_waits = [], []
    for pair in range(PAIRS):
        x_waits[pair].wait_recv()
        x_land = ref.x_land.at[pair].reshape(128 * 8, LANES)
        landed = [x_land[pl.ds(k, 128, stride=8), :] for k in range(SLOTS)]
        values = [jnp.where(first_half, v, 0.0) for v in landed]
        values += [jnp.where(first_half, 0.0, v) for v in landed]
        values = jnp.concatenate(values, axis=0).astype(BF16)
        values = jnp.concatenate([values] * 4, axis=1) * parity[pair]
        planes_of.append(values)
        edge = low(dot_nn(rim[pair], values))
        rim_send, rim_land = ref.rim_send.at[pair], ref.rim_land.at[pair]
        rim_send[0, 0:16, :] = edge[0:16, 2 * LANES : 3 * LANES]
        rim_send[1, 0:16, :] = edge[0:16, 3 * LANES :]
        rim_send[0, 16:48, :] = edge[16:48, LANES : 2 * LANES]
        rim_send[1, 16:48, :] = edge[16:48, 3 * LANES :]
        d_waits.append(
            [
                wire.one(rim_send.at[1, pl.ds(40, 8)], rim_land.at[0, pl.ds(48, 8)], wire.near(1, 1)),
                wire.one(
                    rim_send.at[:, pl.ds(16, 32)], rim_land.at[:, pl.ds(16, 32)], wire.near(0, 1)
                ),
                wire.one(rim_send.at[:, pl.ds(0, 16)], rim_land.at[:, pl.ds(0, 16)], wire.near(1, 0)),
            ]
        )

    c_wait.wait_recv()
    taps = ref.taps
    for i in range(n_rows):
        owner = wire.source(i)[0]
        taps[pl.ds(pl.multiple_of(owner * OWN_ROWS, 8), OWN_ROWS), :] = ref.c_land[i].astype(F32)[
            0:OWN_ROWS, :
        ]
    ref.back1[...] = jnp.zeros((4 * LANES, 4 * LANES), BF16)
    for t in range(TAPS):
        both = taps[t * CH : (t + 1) * CH, :]
        swapped = roll64(both)
        at = t * LANES
        k1 = jnp.concatenate(
            [jnp.where(first_half, both, 0.0), jnp.where(first_half, 0.0, swapped)], axis=0
        )
        k2 = jnp.concatenate(
            [jnp.where(first_half, swapped, 0.0), jnp.where(first_half, 0.0, both)], axis=0
        )
        ref.wide1[at : at + LANES, :] = k1.astype(BF16)
        if t % 3 == 0:
            ref.side1[t // 3 * LANES : (t // 3 + 1) * LANES, :] = k1.astype(BF16)
        ref.wide2[at : at + LANES, :] = k2.astype(BF16)
        ref.back2[at : at + LANES, :] = jnp.transpose(k2).astype(BF16)
        a, b = t // 3, t % 3
        window = 2 * (a == 0) + (b == 0)
        plane = 2 * (a != 1) + (b != 1)
        ref.back1[
            window * LANES : (window + 1) * LANES, plane * LANES : (plane + 1) * LANES
        ] = jnp.transpose(k1).astype(BF16)

    y1 = ref.y1
    first_col = jnp.bitwise_and(iota((PIXELS, LANES), 0), HALF_COLS - 1) == 0
    no_row = jnp.zeros((HALF_COLS, LANES), BF16)
    for pair in range(PAIRS):
        grid = low(dot_nn(place[pair], planes_of[pair]))
        still = [grid[:, q * LANES : (q + 1) * LANES] for q in range(4)]
        moved = {q: jnp.where(first_col, 0.0, pltpu.roll(still[q], 1, axis=0)) for q in (1, 3)}
        for t in range(TAPS):
            a, b = t // 3, t % 3
            plane = 2 * (a != 1) + (b != 1)
            window = (moved[plane] if b == 0 else still[plane]).astype(BF16)
            if a == 0:
                window = jnp.concatenate([no_row, window[: PIXELS - HALF_COLS, :]], axis=0)
            ref.im1[pair, :, t * LANES : (t + 1) * LANES] = window
        y1[pair] = dot_nn(ref.im1[pair], ref.wide1[...])

    e_waits, e_edges = [], []
    for pair in range(PAIRS):
        for wait in d_waits[pair]:
            wait.wait_recv()
        rim_land = ref.rim_land.at[pair]
        rows_in = [rim_land[p, 0:16, :] * up for p in range(2)]
        cols_in = [rim_land[p, 16:48, :] * left for p in range(2)]
        corner = rim_land[0, 55:56, :] * (up * left)
        top = [
            jnp.where(iota((16, LANES), 0) == 0, corner, pltpu.roll(rows_in[1], 1, axis=0)),
            rows_in[0],
            rows_in[1],
        ]
        side = [
            jnp.where(iota((32, LANES), 0) == 0, 0.0, pltpu.roll(cols_in[1], 1, axis=0)),
            cols_in[0],
            cols_in[1],
        ]
        ref.top1[pair] = jnp.concatenate(top, axis=1).astype(BF16)
        ref.left1[pair] = jnp.concatenate(side, axis=1).astype(BF16)
        y1[pair, 0:16, :] += dot_nn(ref.top1[pair], ref.wide1[0 : 3 * LANES, :])
        beside = pl.ds(0, HALF_ROWS, stride=HALF_COLS)
        y1.at[pair][beside, :] += dot_nn(ref.left1[pair], ref.side1[...])
        value = y1[pair]
        e_waits.append(global_sums(pair, column_sum(value), column_sum(value * value)))
        e_edges.append(halo_send(y1, 1, pair, True))

    cot = ref.cot
    for pair in range(PAIRS):
        spread_to = cot.at[pair]
        for m in range(HALF_COLS // 2):
            a = ref.cotangent[2 * pair, :, m * LANES : (m + 1) * LANES].astype(F32)
            b = ref.cotangent[2 * pair + 1, :, m * LANES : (m + 1) * LANES].astype(F32)
            spread_to[pl.ds(2 * m, HALF_ROWS, stride=HALF_COLS), :] = jnp.where(
                first_half, a, roll64(b)
            )
            spread_to[pl.ds(2 * m + 1, HALF_ROWS, stride=HALF_COLS), :] = jnp.where(
                first_half, roll64(a), b
            )
    cot_waits = [wait for pair in range(PAIRS) for wait in halo_send(cot, 0, pair, True)]

    for c in range(FEATS):
        ref.pick_c[c * LANES : (c + 1) * LANES, :] = one_hot(iota((LANES, LANES), 1) == c)
    for pair in range(PAIRS):
        for half in range(2):
            for k in range(SLOTS):
                at = 16 * half + 3 * pair + k
                block = (half * SLOTS + k) * LANES
                along, _ = pixel_of(along_all[:, at : at + 1], along_all[:, at + 8 : at + 9])
                along = jnp.broadcast_to(along, (LANES, LANES))
                for m in range(4):
                    fetch[pair, block : block + LANES, m * LANES : (m + 1) * LANES] = one_hot(
                        iota((LANES, LANES), 1) + m * LANES == along
                    )
    lax.fori_loop(PARTS[0], PARTS[1], slopes, 0)

    norm1, f_waits, f_edges = [], [], []
    y2 = ref.y2
    for pair in range(PAIRS):
        e_waits[pair].wait_recv()
        for wait in e_edges[pair]:
            wait.wait_recv()
        center, factor = norm_of(summed(pair))
        norm1.append((center, factor))
        scaled = (y1[pair] - center) * factor
        pre = scaled * gain1 + bias1
        sigma = sigmoid(pre)
        edge = (ref.halo[1, pair] - center) * factor * gain1 + bias1
        fill_ext(0, pair, low(pre * sigma), low(edge * sigmoid(edge)) * halo_mask)
        for b in range(3):
            window = shifted(0, pair, b, range(EXT_ROWS))
            for a in range(3):
                t = 3 * a + b
                ref.im2[pair, :, t * LANES : (t + 1) * LANES] = jnp.concatenate(
                    window[a : a + HALF_ROWS], axis=0
                )
        value = dot_nn(ref.im2[pair], ref.wide2[...])
        y2[pair] = value
        f_waits.append(global_sums(2 + pair, column_sum(value), column_sum(value * value)))
        f_edges.append(halo_send(y2, 2, pair, True))
        ref.x1[pair] = scaled
        ref.s1[pair] = sigma * (1.0 + pre * (1.0 - sigma))

    lax.fori_loop(PARTS[1], PARTS[2], slopes, 0)

    norm2, g_waits = [], []
    for pair in range(PAIRS):
        f_waits[pair].wait_recv()
        center, factor = norm_of(summed(2 + pair))
        norm2.append((center, factor))
        scaled = (y2[pair] - center) * factor
        pre = scaled * gain2 + bias2
        sigma = sigmoid(pre)
        grad = cot[pair] * (sigma * (1.0 + pre * (1.0 - sigma)))
        g_waits.append(global_sums(4 + pair, column_sum(grad), column_sum(grad * scaled)))
        ref.x2[pair] = scaled
        ref.g2[pair] = grad
        ref.feat[pair] = pre * sigma

    for pair in range(PAIRS):
        grid = ref.feat.at[pair]
        for m in range(HALF_COLS // 2):
            a = grid[pl.ds(2 * m, HALF_ROWS, stride=HALF_COLS), :]
            b = grid[pl.ds(2 * m + 1, HALF_ROWS, stride=HALF_COLS), :]
            at = slice(m * LANES, (m + 1) * LANES)
            ref.features[2 * pair, :, at] = jnp.where(first_half, a, roll64(b)).astype(BF16)
            ref.features[2 * pair + 1, :, at] = jnp.where(first_half, roll64(a), b).astype(BF16)
    edges2 = []
    for pair in range(PAIRS):
        for wait in f_edges[pair] + cot_waits[8 * pair : 8 * pair + 8]:
            wait.wait_recv()
        center, factor = norm2[pair]
        scaled = (ref.halo[2, pair] - center) * factor
        pre = scaled * gain2 + bias2
        sigma = sigmoid(pre)
        edges2.append((scaled, ref.halo[0, pair] * (sigma * (1.0 + pre * (1.0 - sigma)))))
    lax.fori_loop(PARTS[2], PARTS[3], slopes, 0)

    total2, h_waits, h_edges = [], [], []
    for pair in range(PAIRS):
        g_waits[pair].wait_recv()
        sums = summed(4 + pair)
        total2.append(sums)
        scale = norm2[pair][1] * gain2
        mean_grad, mean_scaled = sums[0:1, :] / pixel_total, sums[1:2, :] / pixel_total
        inner = low(scale * (ref.g2[pair] - mean_grad - ref.x2[pair] * mean_scaled))
        edge_scaled, edge_grad = edges2[pair]
        edge = low(scale * (edge_grad - mean_grad - edge_scaled * mean_scaled)) * halo_mask
        ref.d2[pair] = inner.astype(BF16)
        fill_ext(1, pair, inner, edge)
        for b in range(3):
            window = shifted(1, pair, 2 - b, range(EXT_ROWS))
            for a in range(3):
                t = 3 * a + b
                ref.im3[pair, :, t * LANES : (t + 1) * LANES] = jnp.concatenate(
                    window[2 - a : 2 - a + HALF_ROWS], axis=0
                )
        grad = dot_nn(ref.im3[pair], ref.back2[...]) * ref.s1[pair]
        ref.g1[pair] = grad
        h_waits.append(global_sums(6 + pair, column_sum(grad), column_sum(grad * ref.x1[pair])))
        h_edges.append(halo_send(ref.g1, 3, pair, False))

    def kernel_grad(grads, windows):
        product = sum(dot_tn(grads[pair], windows[pair]) for pair in range(PAIRS))
        taps = [product[:, t * LANES : (t + 1) * LANES] for t in range(windows[0].shape[1] // LANES)]
        return [tap[0:CH, :] + roll64(tap[CH:LANES, :]) for tap in taps]

    def to_owners(index, grads):
        dk = ref.dk.at[index]
        for t in range(0, TAPS, 2):
            both = [grads[t], grads[min(t + 1, TAPS - 1)]]
            both = jnp.transpose(jnp.concatenate(both, axis=0))[0:CH, :]
            dk[t * CH : (t + 1) * CH, :] = both
            if t + 1 < TAPS:
                dk[(t + 1) * CH : (t + 2) * CH, :] = roll64(both)
        none = jnp.zeros((BLOCK - PIECE, LANES), F32)
        for i in range(n_rows):
            at = wire.peer(i)[0] * OWN_ROWS
            first = dk[pl.ds(pl.multiple_of(at, 8), PIECE), :]
            second = dk[pl.ds(pl.multiple_of(at + OWN_ROWS - PIECE, 8), PIECE), :]
            block = jnp.where(first_half, first, roll64(second))
            ref.g_send[index, i] = jnp.concatenate([block, none], axis=0).astype(BF16)
        ref.g_land[index, 0] = ref.g_send[index, 0]
        return wire.spread(
            n_rows,
            wire.peer,
            lambda i: ref.g_send.at[index, i],
            lambda i: ref.g_land.at[index, i],
            ref.g_land.at[index, pl.ds(1, n_rows - 1)],
        )

    lax.fori_loop(PARTS[3], 4 * SCENES, slopes, 0)
    grads2 = kernel_grad([ref.d2[0], ref.d2[1]], [ref.im2[0], ref.im2[1]])
    g_waits = [to_owners(1, grads2)]

    total1, y_waits = [], []
    for pair in range(PAIRS):
        h_waits[pair].wait_recv()
        for wait in h_edges[pair]:
            wait.wait_recv()
        sums = summed(6 + pair)
        total1.append(sums)
        center, factor = norm1[pair]
        scale = factor * gain1
        mean_grad, mean_scaled = sums[0:1, :] / pixel_total, sums[1:2, :] / pixel_total
        inner = low(scale * (ref.g1[pair] - mean_grad - ref.x1[pair] * mean_scaled))
        edge_scaled = (ref.halo[1, pair] - center) * factor
        edge = low(scale * (ref.halo[3, pair] - mean_grad - edge_scaled * mean_scaled))
        edge = jnp.where(halo_mask > 0.0, edge, 0.0)
        ref.d1[pair] = inner
        fill_ext(2, pair, inner, edge)
        here = shifted(2, pair, 1, range(1, EXT_ROWS))
        beside = shifted(2, pair, 2, range(1, EXT_ROWS))
        windows = [here[:HALF_ROWS], beside[:HALF_ROWS], here[1:], beside[1:]]
        for w in range(4):
            ref.im4[pair, :, w * LANES : (w + 1) * LANES] = jnp.concatenate(windows[w], axis=0)
        ref.back[pair] = dot_nn(ref.im4[pair], ref.back1[...]).astype(BF16)
        value = dot_nn(fetch[pair], ref.back[pair])
        y_send = ref.y_send.at[pair].reshape(128 * 8, LANES)
        chosen = []
        for block in range(2 * SLOTS):
            rows = slice(block * LANES, (block + 1) * LANES)
            picked = value[rows, 0:LANES] * parity[pair, rows, 0:LANES].astype(F32)
            for q in range(1, 4):
                tile = slice(q * LANES, (q + 1) * LANES)
                picked = picked + value[rows, tile] * parity[pair, rows, tile].astype(F32)
            chosen.append(picked)
        for k in range(SLOTS):
            y_send[pl.ds(k, 128, stride=8), :] = jnp.where(first_half, chosen[k], chosen[SLOTS + k])
        ref.y_land[pair, 0, 0:SLOTS, :] = ref.y_send[pair, 0, 0:SLOTS, :]
        y_waits.append(
            wire.spread(
                total,
                lambda i: wire.source(i),
                lambda i, pair=pair: ref.y_send.at[pair, i, pl.ds(0, SLOTS)],
                lambda i, pair=pair: ref.y_land.at[pair, i, pl.ds(0, SLOTS)],
                ref.y_land.at[pair, pl.ds(1, total - 1), pl.ds(0, SLOTS)],
            )
        )

    def owned_sum(index):
        return jnp.sum(ref.g_land[index].astype(F32), axis=0).astype(BF16)

    g_waits[0].wait_recv()
    ref.gx_land[0] = owned_sum(1)
    gx_wait = wire.spread(
        4,
        lambda i: wire.peer(i * 8),
        lambda i: ref.gx_land.at[0],
        lambda i: ref.gx_land.at[i],
        ref.gx_land.at[pl.ds(1, 3)],
    )
    own1 = [ref.d1[pair].astype(BF16) for pair in range(PAIRS)]
    beside1 = [
        ref.d1.at[pair][pl.ds(0, HALF_ROWS, stride=HALF_COLS), :].astype(BF16)
        for pair in range(PAIRS)
    ]
    grads = kernel_grad(own1, [ref.im1[0], ref.im1[1]])
    upper = kernel_grad([own[0:HALF_COLS, :] for own in own1], [ref.top1[0], ref.top1[1]])
    lefts = kernel_grad(beside1, [ref.left1[0], ref.left1[1]])
    for t in range(3):
        grads[t] = grads[t] + upper[t]
        grads[3 * t] = grads[3 * t] + lefts[t]
    g_waits.append(to_owners(0, grads))

    k_waits = []
    ones = jnp.ones((16, 2 * LANES), BF16)
    for pair in range(PAIRS):
        y_waits[pair].wait_recv()
        y_land = ref.y_land.at[pair].reshape(128 * 8, LANES)
        landed = [jnp.transpose(y_land[pl.ds(k, 128, stride=8), :]) for k in range(SLOTS)]
        landed = jnp.concatenate(landed, axis=1).astype(BF16)
        parts = [[], []]
        for half in range(2):
            s = 2 * pair + half
            pick = jnp.concatenate([hot[s * SLOTS + k] for k in range(SLOTS)], axis=0)
            grad = dot_nn(landed[half * CH : (half + 1) * CH, :], pick)
            ref.grads[s] = grad
            for kind in range(2):
                parts[kind].append(grad * ref.q_sum[s, kind])
        products = jnp.concatenate(parts[0] + parts[1], axis=0)
        coarse = low(products)
        products = jnp.concatenate([coarse, products - coarse], axis=1).astype(BF16)
        sums = dot_nt(ones, products)
        sums = (sums[0:1, 0:LANES], sums[0:1, LANES:])
        if pair == 0:
            k_waits.append(global_sums(8, *sums))
            for c in range(FEATS):
                ref.t_sum[0, c] = ref.grads[0] * ref.t_sum[0, c] + ref.grads[1] * ref.t_sum[1, c]
    split = [[], []]
    for c in range(FEATS):
        product = ref.t_sum[0, c]
        for s in range(2, SCENES):
            product = product + ref.grads[s] * ref.t_sum[s, c]
        coarse = low(product)
        split[0].append(coarse)
        split[1].append(product - coarse)
    weight_grad = jnp.zeros((CH, LANES), F32)
    for part in split:
        weight_grad = weight_grad + dot_nn(
            jnp.concatenate(part, axis=1).astype(BF16), ref.pick_c[...]
        )
    ref.p_col[...] = weight_grad
    packed = jnp.zeros((8, LANES), F32)
    for k in range(8):
        packed = packed + pltpu.roll(ref.p_col[pl.ds(k, 8, stride=8), :], 16 * k, axis=1)
    for r in range(n_rows):
        ref.k_send[r, 0:1, :] = sums[0]
        ref.k_send[r, 1:2, :] = sums[1]
        ref.k_send[r, 2:3, :] = packed[r : r + 1, :]
    ref.k_land[0, 0:3, :] = ref.k_send[row, 0:3, :]
    k_waits.append(
        wire.spread(
            total,
            wire.peer,
            lambda i: ref.k_send.at[wire.peer(i)[0], pl.ds(0, 3)],
            lambda i: ref.k_land.at[i, pl.ds(0, 3)],
            ref.k_land.at[pl.ds(1, total - 1), pl.ds(0, 3)],
        )
    )
    gx_wait.wait_recv()
    ref.gz_land[0] = jnp.sum(ref.gx_land[...].astype(F32), axis=0).astype(BF16)
    gz_wait = wire.spread(
        4,
        lambda i: wire.peer(i * 32),
        lambda i: ref.gz_land.at[0],
        lambda i: ref.gz_land.at[i],
        ref.gz_land.at[pl.ds(1, 3)],
    )

    g_waits[1].wait_recv()
    ref.gc_land[0] = owned_sum(0)
    gc_wait = wire.spread(
        n_cols,
        wire.along_cols,
        lambda i: ref.gc_land.at[0],
        lambda i: ref.gc_land.at[i],
        ref.gc_land.at[pl.ds(1, n_cols - 1)],
    )

    def update(s):
        scaled_w = w_row * norm0[s][2]
        coarse = low(scaled_w)
        matrix = jnp.where(first_half, coarse, roll64(scaled_w - coarse)).astype(BF16)
        grad = ref.grads[s]
        for j in range(DEPTH // 4):
            block = [(ref.share[s, 4 * j + t] * grad).astype(BF16) for t in range(4)]
            block = jnp.concatenate(block, axis=1)
            ref.upd[s, :, j * 4 * LANES : (j + 1) * 4 * LANES] = dot_nn(
                matrix, jnp.concatenate([block, block], axis=0)
            )

    for s in range(SCENES):
        update(s)

    bias_sum, gain_sum = jnp.zeros((1, LANES), F32), jnp.zeros((1, LANES), F32)
    correction = jnp.zeros((16, LANES), F32)
    for pair in range(PAIRS):
        k_waits[pair].wait_recv()
        sums = jnp.sum(ref.k_land[:, 0:3, :], axis=0) if pair else summed(8)
        for half in range(2):
            s = 2 * pair + half
            center, factor, scale, count, cross, products = norm0[s]
            own = jnp.where(first_half, roll64(sums) if half else sums, 0.0)
            grad_sum = own[0:1, :]
            scaled_sum = factor * (own[1:2, :] - center * grad_sum)
            bias_sum, gain_sum = bias_sum + grad_sum, gain_sum + scaled_sum
            grad_mean, scaled_mean = grad_sum / count, scaled_sum / count
            point_sums = products[:, 9:10]
            correction = correction + scale * (
                grad_mean * point_sums + scaled_mean * factor * (cross - center * point_sums)
            )
            unit = w_row * factor - jnp.where(feature_row == FEATS, center * factor, 0.0)
            unit = unit * scaled_mean + jnp.where(feature_row == FEATS, grad_mean, 0.0)
            mix = dot_nt(w_row * scale, unit, HIGH)
            coarse = low(mix)
            mix = jnp.concatenate([coarse, mix - coarse], axis=1).astype(BF16)
            out = ref.point_grads.at[s]
            points = aug[s]
            value = ref.upd[s] - dot_nn(mix, jnp.concatenate([points, points], axis=0))
            for n in range(DEPTH):
                at = slice(n * LANES, (n + 1) * LANES)
                out[pl.ds(n, 8, stride=DEPTH), :] = value[0:8, at]
                out[8 * DEPTH + n : 8 * DEPTH + n + 1, :] = value[8:9, at]

    def own_lanes(values):
        return pltpu.roll(values, lax.rem(LANES - 8 * row, LANES), axis=1)

    def both_scenes(values, index):
        added = values[0][index : index + 1, :] + values[1][index : index + 1, :]
        return added + roll64(added)

    small = ref.small
    small[...] = jnp.zeros((8, LANES), F32)
    small[0:1, :] = bias_sum
    small[1:2, :] = both_scenes(total1, 0)
    small[2:3, :] = both_scenes(total2, 0)
    small[3:4, :] = gain_sum
    small[4:5, :] = both_scenes(total1, 1)
    small[5:6, :] = both_scenes(total2, 1)
    owned = own_lanes(small[...])
    ref.bias_grad[...] = owned[0:3, 0:8]
    ref.gain_grad[...] = owned[3:6, 0:8]
    correction = jnp.transpose(square_of(own_lanes(correction)))
    block = [pltpu.roll(sums[2:3, :], (LANES - 16 * k) % LANES, axis=1) for k in range(8)]
    block = jnp.concatenate(block, axis=0)
    ref.pfn_grad[...] = (block - correction[0:8, :])[:, 0:FEATS]
    for index, (wait, land) in enumerate([(gc_wait, ref.gc_land), (gz_wait, ref.gz_land)]):
        wait.wait_recv()
        block = jnp.transpose(square_of(jnp.sum(land[...].astype(F32), axis=0)))
        ref.conv_grad[index, :, 0:PIECE] = block[0:CH, 0:PIECE]
        ref.conv_grad[index, :, OWN_ROWS - PIECE :] = block[CH:LANES, 0:PIECE]
    wire.settle()


def result_kernel(*refs):
    sems = refs[-1]
    copies = [
        pltpu.make_async_copy(refs[i], refs[RESULTS + i], sems.at[i]) for i in range(RESULTS)
    ]
    for copy in copies:
        copy.start()
    for copy in copies:
        copy.wait()


def body(points, counts, tiles, cells, pfn_weight, conv_weight, norm_gain, norm_bias, cotangent):
    scenes, feats, depth, pillars = points.shape
    n_rows, n_cols = lax.axis_size("rows"), lax.axis_size("cols")
    anywhere = pl.BlockSpec(memory_space=pl.ANY)
    inside = pl.BlockSpec(memory_space=pltpu.VMEM)
    shapes = [
        jax.ShapeDtypeStruct(cotangent.shape, BF16),
        jax.ShapeDtypeStruct((scenes, feats * depth, pillars), F32),
        jax.ShapeDtypeStruct(pfn_weight.shape[::-1], F32),
        jax.ShapeDtypeStruct((2, CH, OWN_ROWS), F32),
        jax.ShapeDtypeStruct(norm_gain.shape, F32),
        jax.ShapeDtypeStruct(norm_bias.shape, F32),
    ]
    results = pl.pallas_call(
        functools.partial(step_kernel, n_rows, n_cols),
        out_shape=[pltpu.VMEM(shape.shape, shape.dtype) for shape in shapes],
        in_specs=[anywhere] * INPUTS,
        out_specs=[inside] * RESULTS,
        scratch_shapes=[pltpu.VMEM(shape, dtype) for shape, dtype in SCRATCH.values()]
        + [
            pltpu.SemaphoreType.DMA((SEMS,)),
            pltpu.SemaphoreType.DMA((SEMS,)),
            pltpu.SemaphoreType.DMA((INPUTS,)),
        ],
        compiler_params=pltpu.CompilerParams(
            collective_id=0, has_side_effects=True, vmem_limit_bytes=54 * 2**20
        ),
    )(
        points.reshape(scenes, feats * depth, pillars),
        counts,
        tiles.reshape(scenes, pillars),
        cells,
        pfn_weight.T,
        conv_weight.transpose(0, 2, 1),
        norm_gain,
        norm_bias,
        cotangent,
    )
    results = pl.pallas_call(
        result_kernel,
        out_shape=shapes,
        in_specs=[inside] * RESULTS,
        out_specs=[anywhere] * RESULTS,
        scratch_shapes=[pltpu.SemaphoreType.DMA((RESULTS,))],
    )(*[pltpu.with_memory_space_constraint(result, pltpu.VMEM) for result in results])
    return (
        results[0],
        results[1].reshape(points.shape),
        results[2].T,
        results[3].transpose(0, 2, 1),
        results[4],
        results[5],
    )


def solution(mesh):
    in_specs = (
        P(None, None, None, ("rows", "cols")),
        P(None, ("rows", "cols")),
        P(None, ("rows", "cols"), None),
        P(None, ("rows", "cols")),
        P(None, "rows"),
        P(None, "rows", None),
        P(None, "rows"),
        P(None, "rows"),
        P(None, "rows", "cols"),
    )
    out_specs = (
        P(None, "rows", "cols"),
        P(None, None, None, ("rows", "cols")),
        P(None, "rows"),
        P(None, "rows", None),
        P(None, "rows"),
        P(None, "rows"),
    )
    return jax.shard_map(body, mesh=mesh, in_specs=in_specs, out_specs=out_specs, check_vma=False)
```

```python
import functools
import types

import jax
import jax.numpy as jnp
from jax import lax
from jax.experimental import pallas as pl
from jax.experimental.pallas import tpu as pltpu
from jax.sharding import PartitionSpec as P

EPSILON = 1e-05
HIGH = lax.Precision.HIGHEST
MESH = pl.DeviceIdType.MESH
F32, BF16, I32 = jnp.float32, jnp.bfloat16, jnp.int32

SCENES = 4
PAIRS = 2
FEATS = 9
DEPTH = 32
PILLARS = 128
CH = 64
LANES = 128
HALF_ROWS = 32
HALF_COLS = 16
PIXELS = HALF_ROWS * HALF_COLS
SLOTS = 3
EDGE = 8
EXT_COLS = 32
EXT_ROWS = HALF_ROWS + 2
TAPS = 9
OWN_ROWS = 72
PAD_ROWS = 80
PIECE = 40
UNROLL = 4
PARTS = (0, 4, 10, 13)
BLOCK = 48


def dot_nn(a, b, precision=None):
    return lax.dot_general(
        a, b, (((1,), (0,)), ((), ())), precision=precision, preferred_element_type=F32
    )


def dot_nt(a, b, precision=None):
    return lax.dot_general(
        a, b, (((1,), (1,)), ((), ())), precision=precision, preferred_element_type=F32
    )


def dot_tn(a, b):
    return lax.dot_general(a, b, (((0,), (0,)), ((), ())), preferred_element_type=F32)


def iota(shape, dim):
    return lax.broadcasted_iota(I32, shape, dim)


def sigmoid(v):
    return 0.5 * jnp.tanh(0.5 * v) + 0.5


def low(v):
    return v.astype(BF16).astype(F32)


def one_hot(mask):
    return jnp.where(mask, 1.0, 0.0).astype(BF16)


def square_of(v):
    rows, cols = v.shape
    if cols < LANES:
        v = jnp.concatenate([v, jnp.zeros((rows, LANES - cols), v.dtype)], axis=1)
    return jnp.concatenate([v, jnp.zeros((LANES - rows, LANES), v.dtype)], axis=0)


def roll64(v):
    return pltpu.roll(v, CH, axis=1)


SCRATCH = dict(
    points=((SCENES, FEATS * DEPTH, LANES), BF16),
    counts=((SCENES, LANES), I32),
    tiles=((SCENES, LANES), I32),
    cells=((SCENES, LANES), I32),
    pfn=((8, FEATS), BF16),
    conv=((2, CH, OWN_ROWS), BF16),
    gain=((3, 8), BF16),
    bias=((3, 8), BF16),
    cotangent=((SCENES, HALF_ROWS, HALF_COLS * CH), BF16),
    square=((LANES, LANES), F32),
    w_tmp=((16, LANES), F32),
    w_send=((16, LANES), F32),
    w_land=((8, 16, LANES), F32),
    c_send=((PAD_ROWS, LANES), BF16),
    c_land=((8, PAD_ROWS, LANES), BF16),
    taps=((TAPS * CH, LANES), F32),
    wide1=((TAPS * LANES, LANES), BF16),
    side1=((3 * LANES, LANES), BF16),
    wide2=((TAPS * LANES, LANES), BF16),
    back2=((TAPS * LANES, LANES), BF16),
    back1=((4 * LANES, 4 * LANES), BF16),
    pts32=((SCENES, 16 * DEPTH, LANES), F32),
    aug=((SCENES, 16, DEPTH * LANES), BF16),
    hot=((SCENES * SLOTS, LANES, LANES), BF16),
    m_send=((2, 4, LANES), F32),
    m_land=((8, 4, LANES), F32),
    m2_land=((16, 4, LANES), F32),
    hello=((4, 4, LANES), F32),
    spots=((LANES, LANES), F32),
    cell_send=((8, 16, LANES), F32),
    cell_land=((8, 16, LANES), F32),
    cell2_send=((16, 8, LANES), F32),
    cell2_land=((16, 8, LANES), F32),
    gram=((SCENES * 16, LANES), F32),
    place=((PAIRS, PIXELS, 6 * LANES), BF16),
    rim=((PAIRS, 48, 6 * LANES), BF16),
    parity=((PAIRS, 6 * LANES, 4 * LANES), BF16),
    fetch=((PAIRS, 6 * LANES, PIXELS), BF16),
    linear=((SCENES, DEPTH, CH, LANES), F32),
    halves=((SCENES, 2, CH, LANES), F32),
    act=((SCENES, DEPTH, CH, LANES), F32),
    share=((SCENES, DEPTH, CH, LANES), F32),
    pil=((SCENES, CH, LANES), F32),
    t_sum=((SCENES, FEATS, CH, LANES), F32),
    q_sum=((SCENES, 2, CH, LANES), F32),
    x_send=((PAIRS, 128, 8, LANES), F32),
    x_land=((PAIRS, 128, 8, LANES), F32),
    y_send=((PAIRS, 128, 8, LANES), F32),
    y_land=((PAIRS, 128, 8, LANES), F32),
    rim_send=((PAIRS, 2, 48, LANES), F32),
    rim_land=((PAIRS, 2, 56, LANES), F32),
    im1=((PAIRS, PIXELS, TAPS * LANES), BF16),
    top1=((PAIRS, 16, 3 * LANES), BF16),
    left1=((PAIRS, 32, 3 * LANES), BF16),
    im2=((PAIRS, PIXELS, TAPS * LANES), BF16),
    im3=((PAIRS, PIXELS, TAPS * LANES), BF16),
    im4=((PAIRS, PIXELS, 4 * LANES), BF16),
    back=((PAIRS, PIXELS, 4 * LANES), BF16),
    pick_c=((FEATS * LANES, LANES), BF16),
    y1=((PAIRS, PIXELS, LANES), F32),
    y2=((PAIRS, PIXELS, LANES), F32),
    x1=((PAIRS, PIXELS, LANES), F32),
    x2=((PAIRS, PIXELS, LANES), F32),
    s1=((PAIRS, PIXELS, LANES), F32),
    g1=((PAIRS, PIXELS, LANES), F32),
    g2=((PAIRS, PIXELS, LANES), F32),
    feat=((PAIRS, PIXELS, LANES), F32),
    cot=((PAIRS, PIXELS, LANES), F32),
    d1=((PAIRS, PIXELS, LANES), F32),
    d2=((PAIRS, PIXELS, LANES), BF16),
    cols=((4, PAIRS, 2, HALF_ROWS, LANES), F32),
    halo=((4, PAIRS, LANES, LANES), F32),
    ext=((3, PAIRS, EXT_ROWS * EXT_COLS, LANES), F32),
    st_send=((10, 2, LANES), F32),
    st_land=((10, 128, 2, LANES), F32),
    grads=((SCENES, CH, LANES), F32),
    p_col=((CH, LANES), F32),
    k_send=((8, 8, LANES), F32),
    k_land=((128, 8, LANES), F32),
    dk=((2, TAPS * CH, LANES), F32),
    g_send=((2, 8, BLOCK, LANES), BF16),
    g_land=((2, 8, BLOCK, LANES), BF16),
    gx_land=((4, BLOCK, LANES), BF16),
    gz_land=((4, BLOCK, LANES), BF16),
    gc_land=((16, BLOCK, LANES), BF16),
    upd=((SCENES, 16, DEPTH * LANES), F32),
    small=((8, LANES), F32),
)
INPUTS = 9
RESULTS = 6
SEMS = 96


HIGH_BITS, LOW_BITS = 0b1010101, 0b0101010


def digits_add(a, b):
    carried = jnp.bitwise_and(a, LOW_BITS) + jnp.bitwise_and(b, LOW_BITS)
    return jnp.bitwise_xor(carried, jnp.bitwise_and(jnp.bitwise_xor(a, b), HIGH_BITS))


def digits_sub(a, b):
    borrowed = jnp.bitwise_or(a, HIGH_BITS) - jnp.bitwise_and(b, LOW_BITS)
    kept = jnp.bitwise_and(jnp.bitwise_xor(jnp.bitwise_xor(a, b), HIGH_BITS), HIGH_BITS)
    return jnp.bitwise_xor(borrowed, kept)


def far_first(step):
    return jnp.bitwise_xor(step, jnp.bitwise_and(jnp.right_shift(step, 1), LOW_BITS))


class Wire:
    def __init__(self, n_rows, n_cols, send_sems, recv_sems):
        self.n_rows, self.n_cols = n_rows, n_cols
        self.total = n_rows * n_cols
        self.row, self.col = lax.axis_index("rows"), lax.axis_index("cols")
        self.me = self.col * n_rows + self.row
        self.send_sems, self.recv_sems = send_sems, recv_sems
        self.used = 0
        self.sent = []

    def place(self, number):
        return (
            jnp.bitwise_and(number, self.n_rows - 1),
            jnp.right_shift(number, self.n_rows.bit_length() - 1),
        )

    def peer(self, step):
        return self.place(digits_add(self.me, step))

    def source(self, step):
        return self.place(digits_sub(self.me, step))

    def along_cols(self, step):
        return self.peer(step * self.n_rows)

    def near(self, down, right):
        return (
            lax.rem(self.row + down + self.n_rows, self.n_rows),
            lax.rem(self.col + right + self.n_cols, self.n_cols),
        )

    def copy(self, src, dst, sem, peer):
        return pltpu.make_async_remote_copy(
            src_ref=src,
            dst_ref=dst,
            send_sem=self.send_sems.at[sem],
            recv_sem=self.recv_sems.at[sem],
            device_id=peer,
            device_id_type=MESH,
        )

    def one(self, src, dst, peer):
        sem = self.used
        self.used += 1
        copy = self.copy(src, dst, sem, peer)
        copy.start()
        self.sent.append(copy)
        return copy

    def spread(self, count, peer_of, src_of, dst_of, whole):
        sem = self.used
        self.used += 1

        def step(j, carry):
            i = far_first(count - j)
            self.copy(src_of(i), dst_of(i), sem, peer_of(i)).start()
            return carry

        lax.fori_loop(1, count, step, 0, unroll=8)
        copy = self.copy(whole, whole, sem, peer_of(1))
        self.sent.append(copy)
        return copy

    def local(self, src, dst, sems, index):
        copy = pltpu.make_async_copy(src, dst, sems.at[index])
        copy.start()
        return copy

    def settle(self):
        for copy in self.sent:
            copy.wait_send()


def step_kernel(n_rows, n_cols, *refs):
    inputs, results = refs[:INPUTS], refs[INPUTS : INPUTS + RESULTS]
    ref = types.SimpleNamespace(**dict(zip(SCRATCH, refs[INPUTS + RESULTS :], strict=False)))
    ref.features, ref.point_grads, ref.pfn_grad, ref.conv_grad, ref.gain_grad, ref.bias_grad = results
    send_sems, recv_sems, in_sems = refs[-3:]
    wire = Wire(n_rows, n_cols, send_sems, recv_sems)
    total, row, col, me = wire.total, wire.row, wire.col, wire.me
    lane = iota((1, LANES), 1)
    first_half = lane < CH

    barrier = pltpu.get_barrier_semaphore()

    lines = [i for i in range(1, n_rows)] + [i * 8 for i in (1, 2, 3)] + [i * 32 for i in (1, 2, 3)]
    for step in lines:
        pl.semaphore_signal(barrier, inc=1, device_id=wire.peer(step), device_id_type=MESH)
    held = [
        ref.points, ref.counts, ref.tiles, ref.cells, ref.pfn, ref.conv, ref.gain, ref.bias,
        ref.cotangent,
    ]
    order = [1, 0, 2, 3, 4, 6, 7, 5, 8]
    loads = {i: wire.local(inputs[i], held[i], in_sems, i) for i in order}
    for i in range(INPUTS):
        loads[i].wait()
    pts32, aug = ref.pts32, ref.aug
    slot_number = iota((DEPTH, LANES), 0)
    for s in range(SCENES):
        valid = slot_number < ref.counts[s : s + 1, :]
        for c in range(FEATS):
            block = ref.points[s, c * DEPTH : (c + 1) * DEPTH, :].astype(F32)
            pts32[s, c * DEPTH : (c + 1) * DEPTH, :] = jnp.where(valid, block, 0.0)
        pts32[s, FEATS * DEPTH : (FEATS + 1) * DEPTH, :] = jnp.where(valid, 1.0, 0.0)
        pts32[s, (FEATS + 1) * DEPTH :, :] = jnp.zeros((6 * DEPTH, LANES), F32)
        scene_pts = pts32.at[s]
        for n in range(DEPTH):
            aug[s, :, n * LANES : (n + 1) * LANES] = scene_pts[pl.ds(n, 16, stride=DEPTH), :].astype(
                BF16
            )
    stacked = jnp.concatenate([aug[s] for s in range(SCENES)], axis=0)
    gram_all = dot_nt(stacked, jnp.concatenate([stacked, stacked], axis=0))
    moments = jnp.zeros((4, LANES), F32)
    for s in range(SCENES):
        for b in range(3):
            piece = gram_all[16 * s + 4 * b : 16 * s + 4 * b + 4, :]
            at = 40 * b + 10 * s
            piece = pltpu.roll(piece, (at - 16 * s) % LANES, axis=1)
            moments = moments + jnp.where((lane >= at) & (lane < at + 10), piece, 0.0)

    hot = ref.hot
    above = iota((LANES, LANES), 0) < iota((LANES, LANES), 1)
    slot_row = iota((LANES, LANES), 0).astype(F32) * 4.0
    for s in range(SCENES):
        tile = ref.tiles[s : s + 1, :]
        tile = jnp.bitwise_and(tile, n_cols - 1) * n_rows + jnp.right_shift(
            tile, n_cols.bit_length() - 1
        )
        tile = digits_sub(tile, me).astype(F32)
        wide = jnp.broadcast_to(tile, (LANES, LANES))
        same = (jnp.transpose(wide) == wide) & above
        rank = jnp.sum(jnp.where(same, 1.0, 0.0), axis=0, keepdims=True)
        code = tile * 4.0 + rank
        for k in range(SLOTS):
            hot[s * SLOTS + k] = one_hot(slot_row + float(k) == code)

    lane_row = iota((LANES, LANES), 0)
    spots = jnp.zeros((LANES, LANES), F32)
    for q in range(4):
        for pair in range(PAIRS):
            s = 2 * pair + q // 2
            cell = ref.cells[s : s + 1, :]
            spot = (jnp.bitwise_and(cell, 31) if q % 2 else jnp.right_shift(cell, 5)) + 1
            for k in range(SLOTS):
                at = jnp.where(lane_row == q * 8 + 3 * pair + k, spot.astype(F32), 0.0)
                spots = spots + dot_nt(hot[s * SLOTS + k], at.astype(BF16))
    ref.spots[...] = spots
    for i in range(n_rows):
        ref.cell_send[i] = ref.spots[pl.ds(i, n_cols, stride=n_rows), :]
    ref.cell_land[0] = ref.cell_send[0]
    ref.m_send[0] = moments
    ref.m_land[0] = moments
    ref.hello[0] = moments

    ref.square[...] = jnp.zeros((LANES, LANES), F32)
    ref.square[0:8, 0:FEATS] = ref.pfn[...].astype(F32)
    ref.w_tmp[...] = jnp.transpose(ref.square[...])[0:16, :]
    ref.w_tmp[9:12, 0:8] = ref.gain[...].astype(F32)
    ref.w_tmp[12:15, 0:8] = ref.bias[...].astype(F32)
    ref.w_send[...] = pltpu.roll(ref.w_tmp[...], row * 8, axis=1)
    ref.w_land[0] = ref.w_send[...]
    pl.semaphore_wait(barrier, len(lines))
    m_wait = wire.spread(
        n_rows,
        wire.peer,
        lambda i: ref.m_send.at[0],
        lambda i: ref.m_land.at[i],
        ref.m_land.at[pl.ds(1, n_rows - 1)],
    )
    hello_wait = wire.spread(
        4,
        lambda i: wire.peer(i * 8),
        lambda i: ref.hello.at[0],
        lambda i: ref.hello.at[i],
        ref.hello.at[pl.ds(1, 3)],
    )
    w_wait = wire.spread(
        n_rows,
        wire.peer,
        lambda i: ref.w_send,
        lambda i: ref.w_land.at[i],
        ref.w_land.at[pl.ds(1, n_rows - 1)],
    )
    m_wait.wait_recv()
    hello_wait.wait_recv()
    moments = jnp.sum(ref.m_land[...], axis=0)
    ref.m_send[1] = moments
    ref.m2_land[0] = moments
    m2_wait = wire.spread(
        n_cols,
        wire.along_cols,
        lambda i: ref.m_send.at[1],
        lambda i: ref.m2_land.at[i],
        ref.m2_land.at[pl.ds(1, n_cols - 1)],
    )

    cell_wait = wire.spread(
        n_rows,
        wire.peer,
        lambda i: ref.cell_send.at[i],
        lambda i: ref.cell_land.at[i],
        ref.cell_land.at[pl.ds(1, n_rows - 1)],
    )

    def halo_send(values, index, pair, full):
        cols, halo = ref.cols.at[index, pair], ref.halo.at[index, pair]
        inner = values.at[pair]
        for side in range(2 if full else 1):
            cols[side] = inner[pl.ds(side * (HALF_COLS - 1), HALF_ROWS, stride=HALF_COLS), :]

        def send(src, start, count, at, down, right):
            return wire.one(
                src.at[pl.ds(start, count)], halo.at[pl.ds(at, count)], wire.near(down, right)
            )

        waits = [
            send(inner, 0, 8, 120, -1, -1),
            send(cols.at[0], 0, 32, 64, 0, -1),
            send(inner, 0, 16, 16, -1, 0),
        ]
        if full:
            waits += [
                send(inner, 504, 8, 96, 1, 1),
                send(inner, 8, 8, 112, -1, 1),
                send(inner, 496, 8, 104, 1, -1),
                send(cols.at[1], 0, 32, 32, 0, 1),
                send(inner, 496, 16, 0, 1, 0),
            ]
        return waits

    def there(cond):
        return jnp.where(cond, 1.0, 0.0)

    up, down = there(row > 0), there(row < n_rows - 1)
    left, right = there(col > 0), there(col < n_cols - 1)
    spot = iota((LANES, LANES), 0)
    halo_mask = jnp.where(spot < 16, up, jnp.where(spot < 32, down, jnp.where(spot < 64, left, right)))
    halo_mask = jnp.where(spot < 96, halo_mask, jnp.where(spot < 112, up, down))
    halo_mask = jnp.where(
        spot < 96,
        halo_mask,
        halo_mask * jnp.where((spot < 104) | ((spot >= 112) & (spot < 120)), left, right),
    )

    def fill_ext(index, pair, inner, edge):
        grid = ref.ext.at[index, pair]
        for i in range(HALF_ROWS):
            at = (i + 1) * EXT_COLS + EDGE
            grid[at : at + HALF_COLS, :] = inner[i * HALF_COLS : (i + 1) * HALF_COLS, :]
        grid[EDGE : EDGE + HALF_COLS, :] = edge[0:16, :]
        last = (EXT_ROWS - 1) * EXT_COLS
        grid[last + EDGE : last + EDGE + HALF_COLS, :] = edge[16:32, :]
        grid[pl.ds(EXT_COLS + EDGE - 1, HALF_ROWS, stride=EXT_COLS), :] = edge[32:64, :]
        grid[pl.ds(EXT_COLS + EDGE + HALF_COLS, HALF_ROWS, stride=EXT_COLS), :] = edge[64:96, :]
        grid[EDGE - 1 : EDGE, :] = edge[103:104, :]
        grid[EDGE + HALF_COLS : EDGE + HALF_COLS + 1, :] = edge[104:105, :]
        grid[last + EDGE - 1 : last + EDGE, :] = edge[119:120, :]
        grid[last + EDGE + HALF_COLS : last + EDGE + HALF_COLS + 1, :] = edge[120:121, :]

    def shifted(index, pair, shift, rows):
        grid = ref.ext.at[index, pair]
        start = EDGE - 1 + shift
        return [
            grid[i * EXT_COLS + start : i * EXT_COLS + start + HALF_COLS, :].astype(BF16)
            for i in rows
        ]

    def column_sum(v):
        return jnp.sum(v, axis=0, keepdims=True)

    def global_sums(index, first, second):
        send, land = ref.st_send.at[index], ref.st_land.at[index]
        send[0:1, :] = first
        send[1:2, :] = second
        land[0] = send[...]
        return wire.spread(
            total,
            wire.peer,
            lambda i: send,
            lambda i: land.at[i],
            land.at[pl.ds(1, total - 1)],
        )

    def summed(index):
        return jnp.sum(ref.st_land[index], axis=0)

    pixel_total = float(PIXELS * total)

    def norm_of(sums):
        center = sums[0:1, :] / pixel_total
        spread = sums[1:2, :] / pixel_total - center * center
        return center, lax.rsqrt(spread + EPSILON)

    ref.square[:, 0:OWN_ROWS] = jnp.concatenate(
        [ref.conv[0].astype(F32), ref.conv[1].astype(F32)], axis=0
    )
    ref.c_send[...] = jnp.transpose(ref.square[...])[0:PAD_ROWS, :].astype(BF16)
    ref.c_land[0] = ref.c_send[...]
    w_wait.wait_recv()
    w_full = jnp.sum(ref.w_land[...], axis=0)
    feature_row = iota((16, LANES), 0)
    w_row = jnp.where(feature_row < FEATS, w_full, 0.0)
    matrix = jnp.transpose(square_of(w_row))[0:CH, 0:16].astype(BF16)
    STEP = 8
    for s in range(SCENES):
        for j in range(DEPTH // STEP):
            value = dot_nn(matrix, aug[s, :, j * STEP * LANES : (j + 1) * STEP * LANES])
            for t in range(STEP):
                ref.linear[s, STEP * j + t] = value[:, t * LANES : (t + 1) * LANES]
    cell_wait.wait_recv()
    cell_land = ref.cell_land.reshape(n_rows * n_cols, LANES)
    for i in range(n_cols):
        ref.cell2_send[i] = cell_land[pl.ds(i, n_rows, stride=n_cols), :]
    ref.cell2_land[0] = ref.cell2_send[0]
    cell2_wait = wire.spread(
        n_cols,
        wire.along_cols,
        lambda i: ref.cell2_send.at[i],
        lambda i: ref.cell2_land.at[i],
        ref.cell2_land.at[pl.ds(1, n_cols - 1)],
    )
    m2_wait.wait_recv()


    def twice(v):
        return v + roll64(v)

    gain0, bias0 = w_full[9:10, :], w_full[12:13, :]
    gain1, bias1 = twice(w_full[10:11, :]), twice(w_full[13:14, :])
    gain2, bias2 = twice(w_full[11:12, :]), twice(w_full[14:15, :])
    moments = jnp.sum(ref.m2_land[...], axis=0)
    gram = ref.gram
    gram[...] = jnp.zeros((SCENES * 16, LANES), F32)
    for s in range(SCENES):
        for b in range(3):
            piece = pltpu.roll(moments, (LANES - 40 * b - 10 * s) % LANES, axis=1)
            at = 16 * s + 4 * b
            gram[at : at + 4, :] = jnp.where(lane < 10, piece, 0.0)
    crosses = dot_nn(gram[:, 0:16], w_row, HIGH)
    norm0, columns = [], []
    for s in range(SCENES):
        products, cross = gram[16 * s : 16 * s + 16, :], crosses[16 * s : 16 * s + 16, :]
        count = products[9:10, 9:10]
        center = cross[9:10, :] / count
        spread = column_sum(w_row * cross) / count - center * center
        factor = lax.rsqrt(spread + EPSILON)
        scale = factor * gain0
        norm0.append((center, factor, scale, count, cross, products))
        columns += [scale, 0.5 * scale, 0.5 * (bias0 - center * scale)]
    columns = jnp.transpose(square_of(jnp.concatenate(columns, axis=0)))[0:CH, :]
    for s in range(SCENES):
        for kind in range(2):
            at = 3 * s + 1 + kind
            ref.halves[s, kind] = jnp.broadcast_to(columns[:, at : at + 1], (CH, LANES))

    x_waits = []
    for pair in range(PAIRS):
        for s in (2 * pair, 2 * pair + 1):
            bound = ref.counts[s : s + 1, :]
            half_scale, half_shift = ref.halves[s, 0], ref.halves[s, 1]
            peak = jnp.full((CH, LANES), -1e30, F32)
            for n in range(DEPTH):
                half = ref.linear[s, n] * half_scale + half_shift
                active = jnp.where(n < bound, half * jnp.tanh(half) + half, -1e30)
                ref.act[s, n] = active
                peak = jnp.maximum(peak, active)
            whole = jnp.zeros((CH, LANES), F32)
            for n in range(DEPTH):
                whole = whole + jnp.exp(ref.act[s, n] - peak)
            ref.pil[s] = peak + jnp.log(whole)
        x_send = ref.x_send.at[pair].reshape(128 * 8, LANES)
        a, b = ref.pil[2 * pair].astype(BF16), ref.pil[2 * pair + 1].astype(BF16)
        none = jnp.zeros((CH, LANES), BF16)
        both = jnp.concatenate(
            [jnp.concatenate([a, none], axis=1), jnp.concatenate([none, b], axis=1)], axis=0
        )
        for k in range(SLOTS):
            pick = jnp.concatenate(
                [hot[2 * pair * SLOTS + k], hot[(2 * pair + 1) * SLOTS + k]], axis=1
            )
            x_send[pl.ds(k, 128, stride=8), :] = dot_nt(pick, both)
        ref.x_land[pair, 0, 0:SLOTS, :] = ref.x_send[pair, 0, 0:SLOTS, :]
        x_waits.append(
            wire.spread(
                total,
                wire.peer,
                lambda i, pair=pair: ref.x_send.at[pair, i, pl.ds(0, SLOTS)],
                lambda i, pair=pair: ref.x_land.at[pair, i, pl.ds(0, SLOTS)],
                ref.x_land.at[pair, pl.ds(1, total - 1), pl.ds(0, SLOTS)],
            )
        )

    c_wait = wire.spread(
        n_rows,
        wire.peer,
        lambda i: ref.c_send,
        lambda i: ref.c_land.at[i],
        ref.c_land.at[pl.ds(1, n_rows - 1)],
    )

    def slopes(step, carry):
        s, block = step // 4, lax.rem(step, 4)
        rows = pl.ds(pl.multiple_of(block * 16, 16), 16)
        top = ref.pil[s, rows, :]
        half_scale, half_shift = ref.halves[s, 0, rows, :], ref.halves[s, 1, rows, :]

        def inner(j, sums):
            sums = list(sums)
            for t in range(UNROLL):
                n = UNROLL * j + t
                line, active = ref.linear[s, n, rows, :], ref.act[s, n, rows, :]
                half = line * half_scale + half_shift
                turn = jnp.tanh(half)
                share = jnp.exp(active - top) * ((0.5 + 0.5 * turn) * (1.0 + half * (1.0 - turn)))
                ref.share[s, n, rows, :] = share
                sums[0] = sums[0] + share
                sums[1] = sums[1] + share * line
                for c in range(FEATS):
                    sums[2 + c] = sums[2 + c] + share * pts32[s, pl.ds(c * DEPTH + n, 1), :]
            return tuple(sums)

        zero = jnp.zeros((16, LANES), F32)
        sums = lax.fori_loop(0, DEPTH // UNROLL, inner, (zero,) * (2 + FEATS))
        ref.q_sum[s, 0, rows, :] = sums[0]
        ref.q_sum[s, 1, rows, :] = sums[1]
        for c in range(FEATS):
            ref.t_sum[s, c, rows, :] = sums[2 + c] * (2.0 * half_scale)
        return carry

    cell2_wait.wait_recv()
    along_all = ref.cell2_land[...].reshape(LANES, LANES)
    across_all = jnp.transpose(along_all)
    place, rim, parity, fetch = ref.place, ref.rim, ref.parity, ref.fetch

    def pixel_of(tall, wide):
        i, j = tall.astype(I32) - 1, wide.astype(I32) - 1
        pixel = jnp.right_shift(i, 1) * HALF_COLS + jnp.right_shift(j, 1)
        plane = 2 * jnp.bitwise_and(i, 1) + jnp.bitwise_and(j, 1)
        return jnp.where(i < 0, -1, pixel), jnp.where(i < 0, -1, plane)

    rim_pixel = iota((48, LANES), 0)
    rim_pixel = jnp.where(rim_pixel < 16, 496 + rim_pixel, rim_pixel * 16 - 241)
    for pair in range(PAIRS):
        for half in range(2):
            for k in range(SLOTS):
                at = 16 * half + 3 * pair + k
                block = (half * SLOTS + k) * LANES
                blocks = slice(block, block + LANES)
                across, _ = pixel_of(across_all[at : at + 1, :], across_all[at + 8 : at + 9, :])
                _, along = pixel_of(along_all[:, at : at + 1], along_all[:, at + 8 : at + 9])
                along = jnp.broadcast_to(along, (LANES, LANES))
                for m in range(4):
                    tile = slice(m * LANES, (m + 1) * LANES)
                    place[pair, tile, blocks] = one_hot(
                        iota((LANES, LANES), 0) + m * LANES == across
                    )
                    parity[pair, blocks, tile] = one_hot(along == m)
                rim[pair, :, blocks] = one_hot(rim_pixel == across)

    lax.fori_loop(0, PARTS[0], slopes, 0)

    planes_of, d_waits = [], []
    for pair in range(PAIRS):
        x_waits[pair].wait_recv()
        x_land = ref.x_land.at[pair].reshape(128 * 8, LANES)
        landed = [x_land[pl.ds(k, 128, stride=8), :] for k in range(SLOTS)]
        values = [jnp.where(first_half, v, 0.0) for v in landed]
        values += [jnp.where(first_half, 0.0, v) for v in landed]
        values = jnp.concatenate(values, axis=0).astype(BF16)
        values = jnp.concatenate([values] * 4, axis=1) * parity[pair]
        planes_of.append(values)
        edge = low(dot_nn(rim[pair], values))
        rim_send, rim_land = ref.rim_send.at[pair], ref.rim_land.at[pair]
        rim_send[0, 0:16, :] = edge[0:16, 2 * LANES : 3 * LANES]
        rim_send[1, 0:16, :] = edge[0:16, 3 * LANES :]
        rim_send[0, 16:48, :] = edge[16:48, LANES : 2 * LANES]
        rim_send[1, 16:48, :] = edge[16:48, 3 * LANES :]
        d_waits.append(
            [
                wire.one(rim_send.at[1, pl.ds(40, 8)], rim_land.at[0, pl.ds(48, 8)], wire.near(1, 1)),
                wire.one(
                    rim_send.at[:, pl.ds(16, 32)], rim_land.at[:, pl.ds(16, 32)], wire.near(0, 1)
                ),
                wire.one(rim_send.at[:, pl.ds(0, 16)], rim_land.at[:, pl.ds(0, 16)], wire.near(1, 0)),
            ]
        )

    c_wait.wait_recv()
    taps = ref.taps
    for i in range(n_rows):
        owner = wire.source(i)[0]
        taps[pl.ds(pl.multiple_of(owner * OWN_ROWS, 8), OWN_ROWS), :] = ref.c_land[i].astype(F32)[
            0:OWN_ROWS, :
        ]
    ref.back1[...] = jnp.zeros((4 * LANES, 4 * LANES), BF16)
    for t in range(TAPS):
        both = taps[t * CH : (t + 1) * CH, :]
        swapped = roll64(both)
        at = t * LANES
        k1 = jnp.concatenate(
            [jnp.where(first_half, both, 0.0), jnp.where(first_half, 0.0, swapped)], axis=0
        )
        k2 = jnp.concatenate(
            [jnp.where(first_half, swapped, 0.0), jnp.where(first_half, 0.0, both)], axis=0
        )
        ref.wide1[at : at + LANES, :] = k1.astype(BF16)
        if t % 3 == 0:
            ref.side1[t // 3 * LANES : (t // 3 + 1) * LANES, :] = k1.astype(BF16)
        ref.wide2[at : at + LANES, :] = k2.astype(BF16)
        ref.back2[at : at + LANES, :] = jnp.transpose(k2).astype(BF16)
        a, b = t // 3, t % 3
        window = 2 * (a == 0) + (b == 0)
        plane = 2 * (a != 1) + (b != 1)
        turned = jnp.transpose(k1)
        for half in range(2):
            own = turned[half * CH : (half + 1) * CH, :]
            own = (own if half == plane % 2 else roll64(own)).astype(BF16)
            at = window * LANES + half * CH
            tile = (2 * half + plane // 2) * LANES
            ref.back1[at : at + CH, tile : tile + LANES] += own

    y1 = ref.y1
    first_col = jnp.bitwise_and(iota((PIXELS, LANES), 0), HALF_COLS - 1) == 0
    no_row = jnp.zeros((HALF_COLS, LANES), BF16)
    for pair in range(PAIRS):
        grid = low(dot_nn(place[pair], planes_of[pair]))
        still = [grid[:, q * LANES : (q + 1) * LANES] for q in range(4)]
        moved = {q: jnp.where(first_col, 0.0, pltpu.roll(still[q], 1, axis=0)) for q in (1, 3)}
        for t in range(TAPS):
            a, b = t // 3, t % 3
            plane = 2 * (a != 1) + (b != 1)
            window = (moved[plane] if b == 0 else still[plane]).astype(BF16)
            if a == 0:
                window = jnp.concatenate([no_row, window[: PIXELS - HALF_COLS, :]], axis=0)
            ref.im1[pair, :, t * LANES : (t + 1) * LANES] = window
        y1[pair] = dot_nn(ref.im1[pair], ref.wide1[...])

    e_waits, e_edges = [], []
    for pair in range(PAIRS):
        for wait in d_waits[pair]:
            wait.wait_recv()
        rim_land = ref.rim_land.at[pair]
        rows_in = [rim_land[p, 0:16, :] * up for p in range(2)]
        cols_in = [rim_land[p, 16:48, :] * left for p in range(2)]
        corner = rim_land[0, 55:56, :] * (up * left)
        top = [
            jnp.where(iota((16, LANES), 0) == 0, corner, pltpu.roll(rows_in[1], 1, axis=0)),
            rows_in[0],
            rows_in[1],
        ]
        side = [
            jnp.where(iota((32, LANES), 0) == 0, 0.0, pltpu.roll(cols_in[1], 1, axis=0)),
            cols_in[0],
            cols_in[1],
        ]
        ref.top1[pair] = jnp.concatenate(top, axis=1).astype(BF16)
        ref.left1[pair] = jnp.concatenate(side, axis=1).astype(BF16)
        y1[pair, 0:16, :] += dot_nn(ref.top1[pair], ref.wide1[0 : 3 * LANES, :])
        beside = pl.ds(0, HALF_ROWS, stride=HALF_COLS)
        y1.at[pair][beside, :] += dot_nn(ref.left1[pair], ref.side1[...])
        value = y1[pair]
        e_waits.append(global_sums(pair, column_sum(value), column_sum(value * value)))
        e_edges.append(halo_send(y1, 1, pair, True))

    cot = ref.cot
    for pair in range(PAIRS):
        spread_to = cot.at[pair]
        for m in range(HALF_COLS // 2):
            a = ref.cotangent[2 * pair, :, m * LANES : (m + 1) * LANES].astype(F32)
            b = ref.cotangent[2 * pair + 1, :, m * LANES : (m + 1) * LANES].astype(F32)
            spread_to[pl.ds(2 * m, HALF_ROWS, stride=HALF_COLS), :] = jnp.where(
                first_half, a, roll64(b)
            )
            spread_to[pl.ds(2 * m + 1, HALF_ROWS, stride=HALF_COLS), :] = jnp.where(
                first_half, roll64(a), b
            )
    cot_waits = [wait for pair in range(PAIRS) for wait in halo_send(cot, 0, pair, True)]

    for c in range(FEATS):
        ref.pick_c[c * LANES : (c + 1) * LANES, :] = one_hot(iota((LANES, LANES), 1) == c)
    for pair in range(PAIRS):
        for half in range(2):
            for k in range(SLOTS):
                at = 16 * half + 3 * pair + k
                block = (half * SLOTS + k) * LANES
                along, _ = pixel_of(along_all[:, at : at + 1], along_all[:, at + 8 : at + 9])
                along = jnp.broadcast_to(along, (LANES, LANES))
                for m in range(4):
                    fetch[pair, block : block + LANES, m * LANES : (m + 1) * LANES] = one_hot(
                        iota((LANES, LANES), 1) + m * LANES == along
                    )
    lax.fori_loop(PARTS[0], PARTS[1], slopes, 0)

    norm1, f_waits, f_edges = [], [], []
    y2 = ref.y2
    for pair in range(PAIRS):
        e_waits[pair].wait_recv()
        for wait in e_edges[pair]:
            wait.wait_recv()
        center, factor = norm_of(summed(pair))
        norm1.append((center, factor))
        scaled = (y1[pair] - center) * factor
        pre = scaled * gain1 + bias1
        sigma = sigmoid(pre)
        edge = (ref.halo[1, pair] - center) * factor * gain1 + bias1
        fill_ext(0, pair, low(pre * sigma), low(edge * sigmoid(edge)) * halo_mask)
        for b in range(3):
            window = shifted(0, pair, b, range(EXT_ROWS))
            for a in range(3):
                t = 3 * a + b
                ref.im2[pair, :, t * LANES : (t + 1) * LANES] = jnp.concatenate(
                    window[a : a + HALF_ROWS], axis=0
                )
        value = dot_nn(ref.im2[pair], ref.wide2[...])
        y2[pair] = value
        f_waits.append(global_sums(2 + pair, column_sum(value), column_sum(value * value)))
        f_edges.append(halo_send(y2, 2, pair, True))
        ref.x1[pair] = scaled
        ref.s1[pair] = sigma * (1.0 + pre * (1.0 - sigma))

    lax.fori_loop(PARTS[1], PARTS[2], slopes, 0)

    norm2, g_waits = [], []
    for pair in range(PAIRS):
        f_waits[pair].wait_recv()
        center, factor = norm_of(summed(2 + pair))
        norm2.append((center, factor))
        scaled = (y2[pair] - center) * factor
        pre = scaled * gain2 + bias2
        sigma = sigmoid(pre)
        grad = cot[pair] * (sigma * (1.0 + pre * (1.0 - sigma)))
        g_waits.append(global_sums(4 + pair, column_sum(grad), column_sum(grad * scaled)))
        ref.x2[pair] = scaled
        ref.g2[pair] = grad
        ref.feat[pair] = pre * sigma

    for pair in range(PAIRS):
        grid = ref.feat.at[pair]
        for m in range(HALF_COLS // 2):
            a = grid[pl.ds(2 * m, HALF_ROWS, stride=HALF_COLS), :]
            b = grid[pl.ds(2 * m + 1, HALF_ROWS, stride=HALF_COLS), :]
            at = slice(m * LANES, (m + 1) * LANES)
            ref.features[2 * pair, :, at] = jnp.where(first_half, a, roll64(b)).astype(BF16)
            ref.features[2 * pair + 1, :, at] = jnp.where(first_half, roll64(a), b).astype(BF16)
    edges2 = []
    for pair in range(PAIRS):
        for wait in f_edges[pair] + cot_waits[8 * pair : 8 * pair + 8]:
            wait.wait_recv()
        center, factor = norm2[pair]
        scaled = (ref.halo[2, pair] - center) * factor
        pre = scaled * gain2 + bias2
        sigma = sigmoid(pre)
        edges2.append((scaled, ref.halo[0, pair] * (sigma * (1.0 + pre * (1.0 - sigma)))))
    lax.fori_loop(PARTS[2], PARTS[3], slopes, 0)

    total2, h_waits, h_edges = [], [], []
    for pair in range(PAIRS):
        g_waits[pair].wait_recv()
        sums = summed(4 + pair)
        total2.append(sums)
        scale = norm2[pair][1] * gain2
        mean_grad, mean_scaled = sums[0:1, :] / pixel_total, sums[1:2, :] / pixel_total
        inner = low(scale * (ref.g2[pair] - mean_grad - ref.x2[pair] * mean_scaled))
        edge_scaled, edge_grad = edges2[pair]
        edge = low(scale * (edge_grad - mean_grad - edge_scaled * mean_scaled)) * halo_mask
        ref.d2[pair] = inner.astype(BF16)
        fill_ext(1, pair, inner, edge)
        for b in range(3):
            window = shifted(1, pair, 2 - b, range(EXT_ROWS))
            for a in range(3):
                t = 3 * a + b
                ref.im3[pair, :, t * LANES : (t + 1) * LANES] = jnp.concatenate(
                    window[2 - a : 2 - a + HALF_ROWS], axis=0
                )
        grad = dot_nn(ref.im3[pair], ref.back2[...]) * ref.s1[pair]
        ref.g1[pair] = grad
        h_waits.append(global_sums(6 + pair, column_sum(grad), column_sum(grad * ref.x1[pair])))
        h_edges.append(halo_send(ref.g1, 3, pair, False))

    def kernel_grad(grads, windows):
        product = sum(dot_tn(grads[pair], windows[pair]) for pair in range(PAIRS))
        taps = [product[:, t * LANES : (t + 1) * LANES] for t in range(windows[0].shape[1] // LANES)]
        return [tap[0:CH, :] + roll64(tap[CH:LANES, :]) for tap in taps]

    def to_owners(index, grads):
        dk = ref.dk.at[index]
        for t in range(0, TAPS, 2):
            both = [grads[t], grads[min(t + 1, TAPS - 1)]]
            both = jnp.transpose(jnp.concatenate(both, axis=0))[0:CH, :]
            dk[t * CH : (t + 1) * CH, :] = both
            if t + 1 < TAPS:
                dk[(t + 1) * CH : (t + 2) * CH, :] = roll64(both)
        none = jnp.zeros((BLOCK - PIECE, LANES), F32)
        for i in range(n_rows):
            at = wire.peer(i)[0] * OWN_ROWS
            first = dk[pl.ds(pl.multiple_of(at, 8), PIECE), :]
            second = dk[pl.ds(pl.multiple_of(at + OWN_ROWS - PIECE, 8), PIECE), :]
            block = jnp.where(first_half, first, roll64(second))
            ref.g_send[index, i] = jnp.concatenate([block, none], axis=0).astype(BF16)
        ref.g_land[index, 0] = ref.g_send[index, 0]
        return wire.spread(
            n_rows,
            wire.peer,
            lambda i: ref.g_send.at[index, i],
            lambda i: ref.g_land.at[index, i],
            ref.g_land.at[index, pl.ds(1, n_rows - 1)],
        )

    lax.fori_loop(PARTS[3], 4 * SCENES, slopes, 0)
    grads2 = kernel_grad([ref.d2[0], ref.d2[1]], [ref.im2[0], ref.im2[1]])
    g_waits = [to_owners(1, grads2)]

    total1, y_waits = [], []
    for pair in range(PAIRS):
        h_waits[pair].wait_recv()
        for wait in h_edges[pair]:
            wait.wait_recv()
        sums = summed(6 + pair)
        total1.append(sums)
        center, factor = norm1[pair]
        scale = factor * gain1
        mean_grad, mean_scaled = sums[0:1, :] / pixel_total, sums[1:2, :] / pixel_total
        inner = low(scale * (ref.g1[pair] - mean_grad - ref.x1[pair] * mean_scaled))
        edge_scaled = (ref.halo[1, pair] - center) * factor
        edge = low(scale * (ref.halo[3, pair] - mean_grad - edge_scaled * mean_scaled))
        edge = jnp.where(halo_mask > 0.0, edge, 0.0)
        ref.d1[pair] = inner
        fill_ext(2, pair, inner, edge)
        here = shifted(2, pair, 1, range(1, EXT_ROWS))
        beside = shifted(2, pair, 2, range(1, EXT_ROWS))
        windows = [here[:HALF_ROWS], beside[:HALF_ROWS], here[1:], beside[1:]]
        for w in range(4):
            ref.im4[pair, :, w * LANES : (w + 1) * LANES] = jnp.concatenate(windows[w], axis=0)
        ref.back[pair] = dot_nn(ref.im4[pair], ref.back1[...]).astype(BF16)
        y_send = ref.y_send.at[pair].reshape(128 * 8, LANES)
        chosen = []
        for half in range(2):
            slots = slice(half * SLOTS * LANES, (half + 1) * SLOTS * LANES)
            value = dot_nn(fetch[pair, slots, :], ref.back[pair, :, 2 * half * LANES : 2 * (half + 1) * LANES])
            masks = [parity[pair, slots, q * LANES : (q + 1) * LANES].astype(F32) for q in range(4)]
            picked = value[:, 0:LANES] * jnp.where(first_half, masks[0], masks[1])
            picked = picked + value[:, LANES:] * jnp.where(first_half, masks[2], masks[3])
            picked = picked + roll64(picked)
            chosen += [picked[k * LANES : (k + 1) * LANES, :] for k in range(SLOTS)]
        for k in range(SLOTS):
            y_send[pl.ds(k, 128, stride=8), :] = jnp.where(first_half, chosen[k], chosen[SLOTS + k])
        ref.y_land[pair, 0, 0:SLOTS, :] = ref.y_send[pair, 0, 0:SLOTS, :]
        y_waits.append(
            wire.spread(
                total,
                lambda i: wire.source(i),
                lambda i, pair=pair: ref.y_send.at[pair, i, pl.ds(0, SLOTS)],
                lambda i, pair=pair: ref.y_land.at[pair, i, pl.ds(0, SLOTS)],
                ref.y_land.at[pair, pl.ds(1, total - 1), pl.ds(0, SLOTS)],
            )
        )

    def owned_sum(index):
        return jnp.sum(ref.g_land[index].astype(F32), axis=0).astype(BF16)

    g_waits[0].wait_recv()
    ref.gx_land[0] = owned_sum(1)
    gx_wait = wire.spread(
        4,
        lambda i: wire.peer(i * 8),
        lambda i: ref.gx_land.at[0],
        lambda i: ref.gx_land.at[i],
        ref.gx_land.at[pl.ds(1, 3)],
    )
    own1 = [ref.d1[pair].astype(BF16) for pair in range(PAIRS)]
    beside1 = [
        ref.d1.at[pair][pl.ds(0, HALF_ROWS, stride=HALF_COLS), :].astype(BF16)
        for pair in range(PAIRS)
    ]
    grads = kernel_grad(own1, [ref.im1[0], ref.im1[1]])
    upper = kernel_grad([own[0:HALF_COLS, :] for own in own1], [ref.top1[0], ref.top1[1]])
    lefts = kernel_grad(beside1, [ref.left1[0], ref.left1[1]])
    for t in range(3):
        grads[t] = grads[t] + upper[t]
        grads[3 * t] = grads[3 * t] + lefts[t]
    g_waits.append(to_owners(0, grads))

    k_waits = []
    ones = jnp.ones((16, 2 * LANES), BF16)
    for pair in range(PAIRS):
        y_waits[pair].wait_recv()
        y_land = ref.y_land.at[pair].reshape(128 * 8, LANES)
        landed = [jnp.transpose(y_land[pl.ds(k, 128, stride=8), :]) for k in range(SLOTS)]
        landed = jnp.concatenate(landed, axis=1).astype(BF16)
        parts = [[], []]
        for half in range(2):
            s = 2 * pair + half
            pick = jnp.concatenate([hot[s * SLOTS + k] for k in range(SLOTS)], axis=0)
            grad = dot_nn(landed[half * CH : (half + 1) * CH, :], pick)
            ref.grads[s] = grad
            for kind in range(2):
                parts[kind].append(grad * ref.q_sum[s, kind])
        products = jnp.concatenate(parts[0] + parts[1], axis=0)
        coarse = low(products)
        products = jnp.concatenate([coarse, products - coarse], axis=1).astype(BF16)
        sums = dot_nt(ones, products)
        sums = (sums[0:1, 0:LANES], sums[0:1, LANES:])
        if pair == 0:
            k_waits.append(global_sums(8, *sums))
            for c in range(FEATS):
                ref.t_sum[0, c] = ref.grads[0] * ref.t_sum[0, c] + ref.grads[1] * ref.t_sum[1, c]
    split = [[], []]
    for c in range(FEATS):
        product = ref.t_sum[0, c]
        for s in range(2, SCENES):
            product = product + ref.grads[s] * ref.t_sum[s, c]
        coarse = low(product)
        split[0].append(coarse)
        split[1].append(product - coarse)
    weight_grad = jnp.zeros((CH, LANES), F32)
    for part in split:
        weight_grad = weight_grad + dot_nn(
            jnp.concatenate(part, axis=1).astype(BF16), ref.pick_c[...]
        )
    ref.p_col[...] = weight_grad
    packed = jnp.zeros((8, LANES), F32)
    for k in range(8):
        packed = packed + pltpu.roll(ref.p_col[pl.ds(k, 8, stride=8), :], 16 * k, axis=1)
    for r in range(n_rows):
        ref.k_send[r, 0:1, :] = sums[0]
        ref.k_send[r, 1:2, :] = sums[1]
        ref.k_send[r, 2:3, :] = packed[r : r + 1, :]
    ref.k_land[0, 0:3, :] = ref.k_send[row, 0:3, :]
    k_waits.append(
        wire.spread(
            total,
            wire.peer,
            lambda i: ref.k_send.at[wire.peer(i)[0], pl.ds(0, 3)],
            lambda i: ref.k_land.at[i, pl.ds(0, 3)],
            ref.k_land.at[pl.ds(1, total - 1), pl.ds(0, 3)],
        )
    )
    gx_wait.wait_recv()
    ref.gz_land[0] = jnp.sum(ref.gx_land[...].astype(F32), axis=0).astype(BF16)
    gz_wait = wire.spread(
        4,
        lambda i: wire.peer(i * 32),
        lambda i: ref.gz_land.at[0],
        lambda i: ref.gz_land.at[i],
        ref.gz_land.at[pl.ds(1, 3)],
    )

    g_waits[1].wait_recv()
    ref.gc_land[0] = owned_sum(0)
    gc_wait = wire.spread(
        n_cols,
        wire.along_cols,
        lambda i: ref.gc_land.at[0],
        lambda i: ref.gc_land.at[i],
        ref.gc_land.at[pl.ds(1, n_cols - 1)],
    )

    def update(s):
        scaled_w = w_row * norm0[s][2]
        coarse = low(scaled_w)
        matrix = jnp.where(first_half, coarse, roll64(scaled_w - coarse)).astype(BF16)
        grad = ref.grads[s]
        for j in range(DEPTH // 4):
            block = [(ref.share[s, 4 * j + t] * grad).astype(BF16) for t in range(4)]
            block = jnp.concatenate(block, axis=1)
            ref.upd[s, :, j * 4 * LANES : (j + 1) * 4 * LANES] = dot_nn(
                matrix, jnp.concatenate([block, block], axis=0)
            )

    for s in range(SCENES):
        update(s)

    bias_sum, gain_sum = jnp.zeros((1, LANES), F32), jnp.zeros((1, LANES), F32)
    correction = jnp.zeros((16, LANES), F32)
    for pair in range(PAIRS):
        k_waits[pair].wait_recv()
        sums = jnp.sum(ref.k_land[:, 0:3, :], axis=0) if pair else summed(8)
        for half in range(2):
            s = 2 * pair + half
            center, factor, scale, count, cross, products = norm0[s]
            own = jnp.where(first_half, roll64(sums) if half else sums, 0.0)
            grad_sum = own[0:1, :]
            scaled_sum = factor * (own[1:2, :] - center * grad_sum)
            bias_sum, gain_sum = bias_sum + grad_sum, gain_sum + scaled_sum
            grad_mean, scaled_mean = grad_sum / count, scaled_sum / count
            point_sums = products[:, 9:10]
            correction = correction + scale * (
                grad_mean * point_sums + scaled_mean * factor * (cross - center * point_sums)
            )
            unit = w_row * factor - jnp.where(feature_row == FEATS, center * factor, 0.0)
            unit = unit * scaled_mean + jnp.where(feature_row == FEATS, grad_mean, 0.0)
            mix = dot_nt(w_row * scale, unit, HIGH)
            coarse = low(mix)
            mix = jnp.concatenate([coarse, mix - coarse], axis=1).astype(BF16)
            out = ref.point_grads.at[s]
            points = aug[s]
            value = ref.upd[s] - dot_nn(mix, jnp.concatenate([points, points], axis=0))
            for n in range(DEPTH):
                at = slice(n * LANES, (n + 1) * LANES)
                out[pl.ds(n, 8, stride=DEPTH), :] = value[0:8, at]
                out[8 * DEPTH + n : 8 * DEPTH + n + 1, :] = value[8:9, at]

    def own_lanes(values):
        return pltpu.roll(values, lax.rem(LANES - 8 * row, LANES), axis=1)

    def both_scenes(values, index):
        added = values[0][index : index + 1, :] + values[1][index : index + 1, :]
        return added + roll64(added)

    small = ref.small
    small[...] = jnp.zeros((8, LANES), F32)
    small[0:1, :] = bias_sum
    small[1:2, :] = both_scenes(total1, 0)
    small[2:3, :] = both_scenes(total2, 0)
    small[3:4, :] = gain_sum
    small[4:5, :] = both_scenes(total1, 1)
    small[5:6, :] = both_scenes(total2, 1)
    owned = own_lanes(small[...])
    ref.bias_grad[...] = owned[0:3, 0:8]
    ref.gain_grad[...] = owned[3:6, 0:8]
    correction = jnp.transpose(square_of(own_lanes(correction)))
    block = [pltpu.roll(sums[2:3, :], (LANES - 16 * k) % LANES, axis=1) for k in range(8)]
    block = jnp.concatenate(block, axis=0)
    ref.pfn_grad[...] = (block - correction[0:8, :])[:, 0:FEATS]
    for index, (wait, land) in enumerate([(gc_wait, ref.gc_land), (gz_wait, ref.gz_land)]):
        wait.wait_recv()
        block = jnp.transpose(square_of(jnp.sum(land[...].astype(F32), axis=0)))
        ref.conv_grad[index, :, 0:PIECE] = block[0:CH, 0:PIECE]
        ref.conv_grad[index, :, OWN_ROWS - PIECE :] = block[CH:LANES, 0:PIECE]
    wire.settle()


def result_kernel(*refs):
    sems = refs[-1]
    copies = [
        pltpu.make_async_copy(refs[i], refs[RESULTS + i], sems.at[i]) for i in range(RESULTS)
    ]
    for copy in copies:
        copy.start()
    for copy in copies:
        copy.wait()


def body(points, counts, tiles, cells, pfn_weight, conv_weight, norm_gain, norm_bias, cotangent):
    scenes, feats, depth, pillars = points.shape
    n_rows, n_cols = lax.axis_size("rows"), lax.axis_size("cols")
    anywhere = pl.BlockSpec(memory_space=pl.ANY)
    inside = pl.BlockSpec(memory_space=pltpu.VMEM)
    shapes = [
        jax.ShapeDtypeStruct(cotangent.shape, BF16),
        jax.ShapeDtypeStruct((scenes, feats * depth, pillars), F32),
        jax.ShapeDtypeStruct(pfn_weight.shape[::-1], F32),
        jax.ShapeDtypeStruct((2, CH, OWN_ROWS), F32),
        jax.ShapeDtypeStruct(norm_gain.shape, F32),
        jax.ShapeDtypeStruct(norm_bias.shape, F32),
    ]
    results = pl.pallas_call(
        functools.partial(step_kernel, n_rows, n_cols),
        out_shape=[pltpu.VMEM(shape.shape, shape.dtype) for shape in shapes],
        in_specs=[anywhere] * INPUTS,
        out_specs=[inside] * RESULTS,
        scratch_shapes=[pltpu.VMEM(shape, dtype) for shape, dtype in SCRATCH.values()]
        + [
            pltpu.SemaphoreType.DMA((SEMS,)),
            pltpu.SemaphoreType.DMA((SEMS,)),
            pltpu.SemaphoreType.DMA((INPUTS,)),
        ],
        compiler_params=pltpu.CompilerParams(
            collective_id=0, has_side_effects=True, vmem_limit_bytes=54 * 2**20
        ),
    )(
        points.reshape(scenes, feats * depth, pillars),
        counts,
        tiles.reshape(scenes, pillars),
        cells,
        pfn_weight.T,
        conv_weight.transpose(0, 2, 1),
        norm_gain,
        norm_bias,
        cotangent,
    )
    results = pl.pallas_call(
        result_kernel,
        out_shape=shapes,
        in_specs=[inside] * RESULTS,
        out_specs=[anywhere] * RESULTS,
        scratch_shapes=[pltpu.SemaphoreType.DMA((RESULTS,))],
    )(*[pltpu.with_memory_space_constraint(result, pltpu.VMEM) for result in results])
    return (
        results[0],
        results[1].reshape(points.shape),
        results[2].T,
        results[3].transpose(0, 2, 1),
        results[4],
        results[5],
    )


def solution(mesh):
    in_specs = (
        P(None, None, None, ("rows", "cols")),
        P(None, ("rows", "cols")),
        P(None, ("rows", "cols"), None),
        P(None, ("rows", "cols")),
        P(None, "rows"),
        P(None, "rows", None),
        P(None, "rows"),
        P(None, "rows"),
        P(None, "rows", "cols"),
    )
    out_specs = (
        P(None, "rows", "cols"),
        P(None, None, None, ("rows", "cols")),
        P(None, "rows"),
        P(None, "rows", None),
        P(None, "rows"),
        P(None, "rows"),
    )
    return jax.shard_map(body, mesh=mesh, in_specs=in_specs, out_specs=out_specs, check_vma=False)
```
